32 devices in a mesh: group: 2 (over y), clip: 8 (over z, x), micro: 2 (over core).
Axes of the slice: x: 2, y: 2, z: 4, core: 2. Of those that a mesh axis runs over, the one named last changes fastest.
Arguments:
- inputs: bfloat16 [2, 4, 8, 1568, 384], P('group', 'micro', 'clip'), may hold values from -6 to 6
- offsets: int32 [2], P('group'), may hold values from 0 to 2, as said below
- cotangent: bfloat16 [2, 4, 8, 392, 768], P('group', 'micro', 'clip'), may hold values from -6 to 6
- gain_attn1: float32 [384], replicated, may hold values from 0.1 to 1.9
- w_qkv1: bfloat16 [384, 1152], replicated, may hold values from -0.625 to 0.625
- w_proj1: bfloat16 [384, 384], replicated, may hold values from -0.15625 to 0.15625
- gain_mlp1: float32 [384], replicated, may hold values from 0.1 to 1.9
- w_fc1: bfloat16 [384, 1536], replicated, may hold values from -0.3125 to 0.3125
- w_out1: bfloat16 [1536, 384], replicated, may hold values from -0.21875 to 0.21875
- gain_attn2: float32 [384], replicated, may hold values from 0.1 to 1.9
- w_qkv2: bfloat16 [384, 2304], replicated, may hold values from -0.625 to 0.625
- w_proj2: bfloat16 [768, 768], replicated, may hold values from -0.109375 to 0.109375
- w_skip: bfloat16 [384, 768], replicated, may hold values from -0.625 to 0.625
- gain_mlp2: float32 [768], replicated, may hold values from 0.1 to 1.9
- w_fc2: bfloat16 [768, 3072], replicated, may hold values from -0.21875 to 0.21875
- w_out2: bfloat16 [3072, 768], replicated, may hold values from -0.15625 to 0.15625
Outputs:
- output: bfloat16 [2, 4, 8, 392, 768], P('group', 'micro', 'clip')
- input_grad: bfloat16 [2, 4, 8, 1568, 384], P('group', 'micro', 'clip')
- grad_gain_attn1: float32 [384], replicated
- grad_gain_mlp1: float32 [384], replicated
- grad_gain_attn2: float32 [384], replicated
- grad_gain_mlp2: float32 [768], replicated
- grad_w_qkv1: float32 [442368], P(('clip', 'micro'))
- grad_w_proj1: float32 [147456], P(('clip', 'micro'))
- grad_w_fc1: float32 [589824], P(('clip', 'micro'))
- grad_w_out1: float32 [589824], P(('clip', 'micro'))
- grad_w_qkv2: float32 [884736], P(('clip', 'micro'))
- grad_w_proj2: float32 [589824], P(('clip', 'micro'))
- grad_w_skip: float32 [294912], P(('clip', 'micro'))
- grad_w_fc2: float32 [2359296], P(('clip', 'micro'))
- grad_w_out2: float32 [2359296], P(('clip', 'micro'))
The draws below stay inside these ranges and needn't reach their ends.
Inputs may be any that keep to these rules, and one draw needn't show every extreme that they name: Memory frames of index below offsets[g] are not attended by any clip of stride group g; no two stride groups have the same offset.
All inputs are finite; a program needn't handle non-finite values.
Results may differ from the reference program's by a relative error of at most 0.023.
Values may be sent and summed in bfloat16 or wider, within the bound.
A program may use at most 448 MiB of HBM per device.

```python
import jax
import jax.numpy as jnp
from jax import lax

H1 = 4
H2 = 8
D1 = 384
D2 = 768
F1 = 1536
F2 = 3072
FR = 8
HT = 14
WD = 14
QT = 1568
PT = 392
MT = 196
GROUPS = 2
VIDEOS = 4
CLIPS = 8
N_CLIP = 8


def draw_offsets(key, part):
    key = jax.random.fold_in(key, 5)
    pick_key, rest_key = jax.random.split(key)
    largest = FR // 2 - 2
    chosen = jax.random.randint(pick_key, (), 0, GROUPS, dtype=jnp.int32)
    others = jax.random.randint(rest_key, (GROUPS,), 0, largest, dtype=jnp.int32)
    places = jnp.arange(GROUPS, dtype=jnp.int32)
    return jnp.where(places == chosen, jnp.int32(largest), others).astype(jnp.int32)


def level_of(rng, shape, cuts, low, top_value):
    loudness = 1.0
    for axis_at, shards_of in cuts:
        draws = jax.random.uniform(jax.random.fold_in(jax.random.fold_in(rng, 6), axis_at), (shards_of,), jnp.float32, low / len(cuts), top_value / len(cuts))
        loudness = loudness * jnp.repeat(jnp.exp(draws), shape[axis_at] // shards_of).reshape((-1,) + (1,) * (len(shape) - 1 - axis_at))
    return loudness


def gaussian(stream_key, extent, deviation, reach, cuts=(), held_as=jnp.bfloat16):
    values = jax.random.normal(stream_key, extent, jnp.float32) * deviation
    if len(cuts) > 0:
        values = level_of(stream_key, extent, cuts, -0.22, 0.18) * values
    return jnp.clip(values, min=-reach, max=reach).astype(held_as)


def setup_inputs(seed: int = 0) -> dict:
    seeds = jax.random.split(jax.random.key(seed), 17)
    inputs = gaussian(seeds[0], (GROUPS, VIDEOS, CLIPS, QT, D1), 1.0, 6.0, ((0, 2), (1, 2), (2, 8)))
    offsets = draw_offsets(jax.random.fold_in(seeds[16], 71), 0)
    cotangent = gaussian(seeds[2], (GROUPS, VIDEOS, CLIPS, PT, D2), 1.0, 6.0, ((0, 2), (1, 2), (2, 8)))
    gain_attn1 = jnp.clip(1.0 + 0.18 * jax.random.normal(seeds[3], (D1,), jnp.float32), 0.1, 1.9)
    w_qkv1 = gaussian(seeds[4], (D1, 3 * D1), (D1 // 4) ** -0.5, 0.625)
    w_proj1 = gaussian(seeds[5], (D1, D1), (4 * D1) ** -0.5, 0.15625)
    gain_mlp1 = jnp.clip(1.0 + 0.18 * jax.random.normal(seeds[6], (D1,), jnp.float32), 0.1, 1.9)
    w_fc1 = gaussian(seeds[7], (D1, F1), D1 ** -0.5, 0.3125)
    w_out1 = gaussian(seeds[8], (F1, D1), (F1 // 2) ** -0.5, 0.21875)
    gain_attn2 = jnp.clip(1.0 + 0.18 * jax.random.normal(seeds[9], (D1,), jnp.float32), 0.1, 1.9)
    w_qkv2 = gaussian(seeds[10], (D1, 3 * D2), (D1 // 4) ** -0.5, 0.625)
    w_proj2 = gaussian(seeds[11], (D2, D2), (4 * D2) ** -0.5, 0.109375)
    w_skip = gaussian(seeds[12], (D1, D2), (D1 // 4) ** -0.5, 0.625)
    gain_mlp2 = jnp.clip(1.0 + 0.18 * jax.random.normal(seeds[13], (D2,), jnp.float32), 0.1, 1.9)
    w_fc2 = gaussian(seeds[14], (D2, F2), D2 ** -0.5, 0.21875)
    w_out2 = gaussian(seeds[15], (F2, D2), (F2 // 2) ** -0.5, 0.15625)
    return {"inputs": inputs, "offsets": offsets, "cotangent": cotangent, "gain_attn1": gain_attn1, "w_qkv1": w_qkv1, "w_proj1": w_proj1, "gain_mlp1": gain_mlp1, "w_fc1": w_fc1, "w_out1": w_out1, "gain_attn2": gain_attn2, "w_qkv2": w_qkv2, "w_proj2": w_proj2, "w_skip": w_skip, "gain_mlp2": gain_mlp2, "w_fc2": w_fc2, "w_out2": w_out2}


@jax.custom_vjp
def low(v):
    return lax.optimization_barrier(v.astype(jnp.bfloat16)).astype(jnp.float32)

@jax.custom_vjp
def low_back(v):
    return v

def low_keep(v):
    return (low(v), None)

def low_pass(kept, grad):
    return (grad,)

def back_keep(v):
    return (v, None)

def back_low(kept, grad):
    return (low(grad),)
low.defvjp(low_keep, low_pass)
low_back.defvjp(back_keep, back_low)
highest = lax.Precision.HIGHEST
epsilon = 1e-06

def layer_norm(values, gain):
    center = values - lax.optimization_barrier(jnp.mean(values, axis=-1, keepdims=True))
    spread = lax.optimization_barrier(jnp.mean(center * center, axis=-1, keepdims=True))
    return center * lax.rsqrt(spread + epsilon) * gain

def product(left, right):
    return jnp.dot(left, right, precision=highest)

def pool_space(values):
    width = values.shape[-1]
    frames = values.shape[-2] // (HT * WD)
    shaped = values.reshape(values.shape[:-2] + (frames, HT // 2, 2, WD // 2, 2, width))
    return lax.optimization_barrier(jnp.mean(shaped, axis=(-4, -2))).reshape(values.shape[:-2] + (-1, width))

def pool_time(values):
    width = values.shape[-1]
    shaped = values.reshape(values.shape[:-2] + (FR // 2, 2, -1, width))
    return lax.optimization_barrier(jnp.mean(shaped, axis=-3)).reshape(values.shape[:-2] + (-1, width))

def key_mask(clip, offset):
    frame = jnp.arange(MT, dtype=jnp.int32) // (HT // 2 * (WD // 2))
    later = frame >= offset
    own = jnp.ones((PT,), jnp.bool_)
    return jnp.concatenate([own, later & (clip >= 1), later & (clip >= 2)])

def attend(queries, keys, values, valid, heads):
    count = queries.shape[0]
    head_size = queries.shape[1] // heads
    scores = jnp.einsum('nhd,khd->hnk', queries.reshape(count, heads, head_size), keys.reshape(-1, heads, head_size), precision=highest)
    scores = low_back(scores * head_size ** (-0.5))
    scores = jnp.where(valid[None, None, :], scores, -1e+30)
    weights = low(jax.nn.softmax(scores, axis=-1))
    mixed = jnp.einsum('hnk,khd->nhd', weights, values.reshape(-1, heads, head_size), precision=highest)
    return mixed.reshape(count, heads * head_size)

def finish(residual, queries, keys, values, memory, valid, heads, params):
    w_proj, gain, w_fc, w_out = params
    near_keys, near_values, far_keys, far_values = memory
    all_keys = jnp.concatenate([keys, near_keys, far_keys], axis=0)
    all_values = jnp.concatenate([values, near_values, far_values], axis=0)
    mixed = attend(queries, all_keys, all_values, valid, heads)
    joined = low_back(low(mixed + queries))
    hidden = residual + low_back(product(joined, w_proj))
    normed = low(layer_norm(hidden, gain))
    inner = low_back(product(normed, w_fc))
    active = low(jax.nn.gelu(inner, approximate=False))
    return hidden + low_back(product(active, w_out))

def project_first(inputs, gain, w_qkv):
    normed = low(layer_norm(inputs, gain))
    queries, keys, values = jnp.split(product(normed, w_qkv), 3, axis=-1)
    queries = low_back(low(queries))
    keys = low_back(low(pool_space(keys)))
    values = low_back(low(pool_space(values)))
    return (queries, keys, values, low(pool_time(keys)), low(pool_time(values)))

def project_second(inputs, gain, w_qkv, w_skip):
    normed = low(layer_norm(inputs, gain))
    queries, keys, values = jnp.split(product(normed, w_qkv), 3, axis=-1)
    queries = low_back(low(pool_space(queries)))
    keys = low_back(low(pool_space(keys)))
    values = low_back(low(pool_space(values)))
    skipped = low_back(product(low(pool_space(normed)), w_skip))
    return (queries, keys, values, low(pool_time(keys)), low(pool_time(values)), skipped)

def shifted(memory, hops):
    shaped = memory.reshape((-1, N_CLIP) + memory.shape[1:])
    moved = jnp.concatenate([jnp.zeros_like(shaped[:, :hops]), shaped[:, :-hops]], axis=1)
    return moved.reshape(memory.shape)

def forward(inputs, params, offsets):
    gain_a1, w_qkv1, w_proj1, gain_m1, w_fc1, w_out1, gain_a2, w_qkv2, w_proj2, w_skip, gain_m2, w_fc2, w_out2 = params
    items = inputs.reshape(-1, QT, D1)
    number = items.shape[0]
    clips = jnp.arange(number, dtype=jnp.int32) % N_CLIP
    aligned = jnp.repeat(offsets, number // offsets.shape[0])
    first = lax.map(jax.checkpoint(lambda item: project_first(item, gain_a1, w_qkv1)), items)

    def first_rest(packed):
        item, queries, keys, values, near_k, near_v, far_k, far_v, clip, offset = packed
        return finish(item, queries, keys, values, (near_k, near_v, far_k, far_v), key_mask(clip, offset), H1, (w_proj1, gain_m1, w_fc1, w_out1))
    middle = lax.map(jax.checkpoint(first_rest), (items, first[0], first[1], first[2], shifted(first[3], 1), shifted(first[4], 1), shifted(first[3], 2), shifted(first[4], 2), clips, aligned))
    second = lax.map(jax.checkpoint(lambda item: project_second(item, gain_a2, w_qkv2, w_skip)), middle)

    def second_rest(packed):
        skipped, queries, keys, values, near_k, near_v, far_k, far_v, clip, offset = packed
        return finish(skipped, queries, keys, values, (near_k, near_v, far_k, far_v), key_mask(clip, offset), H2, (w_proj2, gain_m2, w_fc2, w_out2))
    final = lax.map(jax.checkpoint(second_rest), (second[5], second[0], second[1], second[2], shifted(second[3], 1), shifted(second[4], 1), shifted(second[3], 2), shifted(second[4], 2), clips, aligned))
    return final.reshape(inputs.shape[:-2] + (PT, D2))

def reference(inputs, offsets, cotangent, gain_attn1, w_qkv1, w_proj1, gain_mlp1, w_fc1, w_out1, gain_attn2, w_qkv2, w_proj2, w_skip, gain_mlp2, w_fc2, w_out2):
    params = tuple((p.astype(jnp.float32) for p in (gain_attn1, w_qkv1, w_proj1, gain_mlp1, w_fc1, w_out1, gain_attn2, w_qkv2, w_proj2, w_skip, gain_mlp2, w_fc2, w_out2)))

    def whole(values, *weights):
        return forward(values, weights, offsets)
    output, pullback = jax.vjp(whole, inputs.astype(jnp.float32), *params)
    grads = pullback(cotangent.astype(jnp.float32))
    return (output.astype(jnp.bfloat16), grads[0].astype(jnp.bfloat16), grads[1], grads[4], grads[7], grads[11], grads[2].reshape(-1), grads[3].reshape(-1), grads[5].reshape(-1), grads[6].reshape(-1), grads[8].reshape(-1), grads[9].reshape(-1), grads[10].reshape(-1), grads[12].reshape(-1), grads[13].reshape(-1))
```

```python
from functools import partial

import jax
import jax.numpy as jnp
from jax import lax
from jax.sharding import PartitionSpec as P

D1 = 384
D2 = 768
QT = 1568
PT = 392
MT = 196
HD = 96
FR = 8
HT = 14
WD = 14
H1 = 4
H2 = 8
epsilon = 1e-06
f32 = jnp.float32
bf16 = jnp.bfloat16


def shift(value, steps):
    count = lax.axis_size("clip")
    first, last = (max(0, -steps), min(count, count - steps))
    return lax.ppermute(value, "clip", [(s, s + steps) for s in range(first, last)])


def norm_stats(values):
    center = values - jnp.mean(values, axis=-1, keepdims=True)
    inv = lax.rsqrt(jnp.mean(center * center, axis=-1, keepdims=True) + epsilon)
    return (center * inv, inv)


def norm_back(grad, unit, inv, gain):
    du = grad * gain
    dg = jnp.sum(grad * unit, axis=tuple(range(grad.ndim - 1)))
    dx = inv * (
        du - jnp.mean(du, axis=-1, keepdims=True) - unit * jnp.mean(du * unit, axis=-1, keepdims=True)
    )
    return (dx, dg)


def dot(a, b):
    return jnp.einsum("...nc,cf->...nf", a, b, preferred_element_type=f32)


def dot_t(a, b):
    return jnp.einsum("...nf,cf->...nc", a, b, preferred_element_type=f32)


def wgrad(a, b):
    a = a.reshape(-1, a.shape[-1])
    b = b.reshape(-1, b.shape[-1])
    return jnp.einsum("nc,nf->cf", a, b, preferred_element_type=f32)


def split_heads(v, heads):
    return v.reshape(v.shape[:-1] + (heads, HD))


def attend(q, k, v, bias, heads):
    s = jnp.einsum(
        "bnhd,bkhd->bhnk", split_heads(q, heads), split_heads(k, heads), preferred_element_type=f32
    ) * HD ** (-0.5)
    s = s + bias
    top = jnp.max(s, axis=-1, keepdims=True)
    e = jnp.exp(s - top)
    total = jnp.sum(e, axis=-1, keepdims=True)
    o = jnp.einsum(
        "bhnk,bkhd->bnhd", (e / total).astype(bf16), split_heads(v, heads), preferred_element_type=f32
    )
    return (o.reshape(q.shape), top + jnp.log(total))


def attend_back(q, k, v, bias, lse, gz, heads):
    sq, sk, sv, sg = (split_heads(t, heads) for t in (q, k, v, gz))
    s = jnp.einsum("bnhd,bkhd->bhnk", sq, sk, preferred_element_type=f32) * HD ** (-0.5)
    p = jnp.exp(s + bias - lse)
    dp = jnp.einsum("bnhd,bkhd->bhnk", sg, sv, preferred_element_type=f32)
    delta = jnp.sum(dp * p, axis=-1, keepdims=True)
    ds = (p * (dp - delta)).astype(bf16)
    dq = jnp.einsum("bhnk,bkhd->bnhd", ds, sk, preferred_element_type=f32) * HD ** (-0.5)
    dk = jnp.einsum("bhnk,bnhd->bkhd", ds, sq, preferred_element_type=f32) * HD ** (-0.5)
    dv = jnp.einsum("bhnk,bnhd->bkhd", p.astype(bf16), sg, preferred_element_type=f32)
    return (dq.reshape(q.shape), dk.reshape(k.shape), dv.reshape(v.shape))


def gelu_both(x):
    phi = 0.5 * (1.0 + lax.erf(x * 0.7071067811865476))
    dens = jnp.exp(-0.5 * x * x) * 0.3989422804014327
    return ((x * phi).astype(bf16), phi + x * dens)


def tmean_matrix():
    rows = lax.broadcasted_iota(jnp.int32, (MT, PT), 0)
    cols = lax.broadcasted_iota(jnp.int32, (MT, PT), 1)
    cell = MT // (FR // 2)
    hit = (cols // (2 * cell) == rows // cell) & (cols % cell == rows % cell)
    return jnp.where(hit, 0.5, 0.0).astype(bf16)


def remember(pooled):
    mem = jnp.einsum("mp,bpc->bmc", tmean_matrix(), pooled, preferred_element_type=f32).astype(bf16)
    return jnp.concatenate([pooled, shift(mem, 1), shift(mem, 2)], axis=1)


def recall(grad_rows):
    near = shift(grad_rows[:, PT : PT + MT].astype(bf16), -1)
    far = shift(grad_rows[:, PT + MT :].astype(bf16), -2)
    total = (near.astype(f32) + far.astype(f32)).astype(bf16)
    back = jnp.einsum("mp,bmc->bpc", tmean_matrix(), total, preferred_element_type=f32)
    return grad_rows[:, :PT] + back


def halve(value, axis, bit, index):
    n = lax.axis_size(axis)
    mine = lax.dynamic_index_in_dim(value, index, 0, keepdims=False)
    theirs = lax.dynamic_index_in_dim(value, 1 - index, 0, keepdims=False).astype(bf16)
    got = lax.ppermute(theirs, axis, [(i, i ^ (1 << bit)) for i in range(n)])
    return mine.astype(f32) + got.astype(f32)


def reduce_share(grad):
    clips, micros = lax.axis_size("clip"), lax.axis_size("micro")
    shares = clips * micros
    rows, cols = grad.shape
    v = grad.reshape(clips, micros, rows // shares, cols)
    v = halve(jnp.moveaxis(v, 1, 0), "micro", 0, lax.axis_index("micro"))
    half = cols // 2
    v = jnp.stack([v[..., :half], v[..., half:]])
    g = lax.axis_index("group")
    v = halve(v, "group", 0, g)
    c = lax.axis_index("clip")
    bits = clips.bit_length() - 1
    for bit in range(bits):
        open_bits = bits - bit
        w = v.reshape((2 ** (open_bits - 1), 2) + v.shape[1:])
        v = halve(jnp.moveaxis(w, 1, 0), "clip", bit, (c >> bit) & 1)
    v = v.reshape(rows // shares, half).astype(bf16)
    other = lax.ppermute(v, "group", [(0, 1), (1, 0)])
    low = jnp.where(g == 0, v, other)
    high = jnp.where(g == 0, other, v)
    return jnp.concatenate([low, high], axis=-1).astype(f32).reshape(-1)


def body(inputs, offsets, cotangent, gain_attn1, w_qkv1, w_proj1, gain_mlp1, w_fc1, w_out1,
         gain_attn2, w_qkv2, w_proj2, w_skip, gain_mlp2, w_fc2, w_out2):
    B = inputs.shape[1]
    clip = lax.axis_index("clip")
    frame = jnp.arange(MT, dtype=jnp.int32) // (MT // (FR // 2))
    later = frame >= offsets[0]
    valid = jnp.concatenate([jnp.ones((PT,), jnp.bool_), later & (clip >= 1), later & (clip >= 2)])
    bias = jnp.where(valid, 0.0, -1e30).astype(f32)[None, None, None, :]
    x = inputs.reshape(B, FR, HT // 2, 2, WD // 2, 2, D1).transpose(0, 3, 5, 1, 2, 4, 6)
    x = x.reshape(B, 4, PT, D1).astype(f32)

    unit_a, inv_a = norm_stats(x)
    na = (unit_a * gain_attn1).astype(bf16)
    qa = dot(na, w_qkv1[:, :D1]).astype(bf16).reshape(B, QT, D1)
    kva = remember(jnp.mean(na.astype(f32), axis=1).astype(bf16))
    KVa = dot(kva, w_qkv1[:, D1:]).astype(bf16)
    Ka, Va = KVa[..., :D1], KVa[..., D1:]
    oa, lse_a = attend(qa, Ka, Va, bias, H1)
    za = (oa + qa.astype(f32)).astype(bf16)
    ha = x + dot(za, w_proj1).reshape(x.shape)
    unit_b, inv_b = norm_stats(ha)
    nb = (unit_b * gain_mlp1).astype(bf16)
    ub, gpb = gelu_both(dot(nb, w_fc1))
    middle = ha + dot(ub, w_out1)
    unit_c, inv_c = norm_stats(middle)
    nc = (unit_c * gain_attn2).astype(bf16)
    pc = jnp.mean(nc.astype(f32), axis=1).astype(bf16)
    kvc = remember(pc)
    qc = dot(pc, w_qkv2[:, :D2]).astype(bf16)
    skipped = dot(pc, w_skip)
    KVc = dot(kvc, w_qkv2[:, D2:]).astype(bf16)
    Kc, Vc = KVc[..., :D2], KVc[..., D2:]
    oc, lse_c = attend(qc, Kc, Vc, bias, H2)
    zc = (oc + qc.astype(f32)).astype(bf16)
    hc = skipped + dot(zc, w_proj2)
    unit_d, inv_d = norm_stats(hc)
    nd = (unit_d * gain_mlp2).astype(bf16)
    ud, gpd = gelu_both(dot(nd, w_fc2))
    output = hc + dot(ud, w_out2)

    Gm = cotangent.reshape(B, PT, D2)
    gw_out2 = wgrad(ud, Gm)
    gid = (gpd * dot_t(Gm, w_out2)).astype(bf16)
    gw_fc2 = wgrad(nd, gid)
    dx, gg_mlp2 = norm_back(dot_t(gid, w_fc2), unit_d, inv_d, gain_mlp2)
    Gh = (Gm.astype(f32) + dx).astype(bf16)
    gw_proj2 = wgrad(zc, Gh)
    gw_skip = wgrad(pc, Gh)
    gz = dot_t(Gh, w_proj2).astype(bf16)
    dq, dk, dv = attend_back(qc, Kc, Vc, bias, lse_c, gz, H2)
    gqc = (gz.astype(f32) + dq).astype(bf16)
    dKV = jnp.concatenate([dk, dv], axis=-1).astype(bf16)
    gw_qkv2 = jnp.concatenate([wgrad(pc, gqc), wgrad(kvc, dKV)], axis=-1)
    dpc = dot_t(gqc, w_qkv2[:, :D2]) + dot_t(Gh, w_skip) + recall(dot_t(dKV, w_qkv2[:, D2:]))
    dnc = jnp.broadcast_to((0.25 * dpc)[:, None], middle.shape)
    Gmid, gg_attn2 = norm_back(dnc, unit_c, inv_c, gain_attn2)

    Gm1 = Gmid.astype(bf16)
    gw_out1 = wgrad(ub, Gm1)
    gib = (gpb * dot_t(Gm1, w_out1)).astype(bf16)
    gw_fc1 = wgrad(nb, gib)
    dx, gg_mlp1 = norm_back(dot_t(gib, w_fc1), unit_b, inv_b, gain_mlp1)
    Gha = Gmid + dx
    Gh = Gha.astype(bf16).reshape(B, QT, D1)
    gw_proj1 = wgrad(za, Gh)
    gz = dot_t(Gh, w_proj1).astype(bf16)
    dq, dk, dv = attend_back(qa, Ka, Va, bias, lse_a, gz, H1)
    gqa = (gz.astype(f32) + dq).astype(bf16)
    dKV = jnp.concatenate([dk, dv], axis=-1).astype(bf16)
    gw_qkv1 = jnp.concatenate([wgrad(na, gqa), wgrad(kva, dKV)], axis=-1)
    dkv = recall(dot_t(dKV, w_qkv1[:, D1:]))
    dna = dot_t(gqa, w_qkv1[:, :D1]).reshape(x.shape) + (0.25 * dkv)[:, None]
    dx, gg_attn1 = norm_back(dna, unit_a, inv_a, gain_attn1)
    gx = (Gha + dx).astype(bf16)
    gx = gx.reshape(B, 2, 2, FR, HT // 2, WD // 2, D1).transpose(0, 3, 4, 1, 5, 2, 6)

    gains = lax.psum((gg_attn1, gg_mlp1, gg_attn2, gg_mlp2), ("group", "clip", "micro"))
    grads = (gw_qkv1, gw_proj1, gw_fc1, gw_out1, gw_qkv2, gw_proj2, gw_skip, gw_fc2, gw_out2)
    shares = tuple(reduce_share(g) for g in grads)
    return (output.astype(bf16).reshape(cotangent.shape), gx.reshape(inputs.shape)) + tuple(gains) + shares


def solution(mesh):
    tokens = P("group", "micro", "clip", None, None)
    share = P(("clip", "micro"))
    return jax.shard_map(
        body,
        mesh=mesh,
        in_specs=(tokens, P("group"), tokens) + (P(),) * 13,
        out_specs=(tokens, tokens) + (P(),) * 4 + (share,) * 9,
        check_vma=False,
    )
```

```python
from functools import partial

import jax
import jax.numpy as jnp
from jax import lax
from jax.experimental import pallas as pl
from jax.experimental.pallas import tpu as pltpu
from jax.sharding import PartitionSpec as P

D1 = 384
D2 = 768
F1 = 1536
F2 = 3072
QT = 1568
PT = 392
MT = 196
HD = 96
FR = 8
HT = 14
WD = 14
H1 = 4
H2 = 8
CELL = (HT // 2) * (WD // 2)
LANE = 128
PR = 400
MR = 208
KR = PR + 2 * MR
TILE = 224
STEPS = QT // TILE
W1 = H1 * LANE
W2 = H2 * LANE
epsilon = 1e-06
f32 = jnp.float32
bf16 = jnp.bfloat16
SCALE = HD ** (-0.5)
RATE = SCALE * 1.4426950408889634
VMEM = pltpu.VMEM


def mm(a, b):
    return lax.dot_general(a, b, (((1,), (0,)), ((), ())), preferred_element_type=f32)


def mm_nt(a, b):
    return lax.dot_general(a, b, (((1,), (1,)), ((), ())), preferred_element_type=f32)


def mm_tn(a, b):
    return lax.dot_general(a, b, (((0,), (0,)), ((), ())), preferred_element_type=f32)


def lanes(shape):
    return lax.broadcasted_iota(jnp.int32, shape, len(shape) - 1)


def rows_of(shape):
    return lax.broadcasted_iota(jnp.int32, shape, len(shape) - 2)


def norm_stats(values):
    center = values - jnp.mean(values, axis=-1, keepdims=True)
    inv = lax.rsqrt(jnp.mean(center * center, axis=-1, keepdims=True) + epsilon)
    return (center * inv, inv)


def norm_back(grad, unit, inv, gain):
    du = grad * gain
    dg = jnp.sum(grad * unit, axis=0, keepdims=True)
    dx = inv * (
        du - jnp.mean(du, axis=-1, keepdims=True) - unit * jnp.mean(du * unit, axis=-1, keepdims=True)
    )
    return (dx, dg)


def gelu_both(x):
    z = jnp.abs(x)
    t = 1.0 / (1.0 + 0.23164188 * z)
    e = jnp.exp2(x * x * -0.7213475204444817)
    poly = t * (0.127414796 + t * (-0.142248368 + t * (0.7107068705 + t * (-0.7265760135 + t * 0.5307027145))))
    tail = poly * e
    phi = jnp.where(x >= 0.0, 1.0 - tail, tail)
    return (x * phi, phi + (x * 0.3989422804014327) * e)


def split3(v):
    hi = v.astype(bf16).astype(f32)
    mid = (v - hi).astype(bf16).astype(f32)
    return (hi, mid, v - hi - mid)


def put3(base, v):
    hi, mid, low = split3(v)
    lane = lanes(base.shape)
    return jnp.where(
        lane < HD, base, jnp.where(lane == HD, hi, jnp.where(lane == HD + 1, mid, jnp.where(lane == HD + 2, low, base)))
    )


def tmean_matrix():
    rows = rows_of((MR, PR))
    cols = lanes((MR, PR))
    hit = rows < 0
    for pair in range(FR // 2):
        inside = (rows >= pair * CELL) & (rows < (pair + 1) * CELL)
        shift_by = cols - rows - pair * CELL
        hit = hit | (inside & ((shift_by == 0) | (shift_by == CELL)))
    return jnp.where(hit, 0.5, 0.0).astype(bf16)


def pool_rows(ref):
    total = ref[0:PT, :] + ref[PT : 2 * PT, :] + ref[2 * PT : 3 * PT, :] + ref[3 * PT : 4 * PT, :]
    return jnp.concatenate([0.25 * total, jnp.zeros((PR - PT, total.shape[1]), f32)], axis=0).astype(bf16)


def call(kernel, grid, ins, outs, scratch=(), flops=0, name=None):
    arrays = [a for a, _ in ins]
    moved = sum(a.size * a.dtype.itemsize for a in arrays) + sum(s.size * s.dtype.itemsize for s, _ in outs)
    return pl.pallas_call(
        kernel,
        grid=grid,
        in_specs=[s for _, s in ins],
        out_specs=[s for _, s in outs],
        out_shape=[o for o, _ in outs],
        scratch_shapes=list(scratch),
        compiler_params=pltpu.CompilerParams(
            vmem_limit_bytes=58 * 1024 * 1024, dimension_semantics=("arbitrary",) * len(grid)
        ),
        cost_estimate=pl.CostEstimate(flops=int(flops), bytes_accessed=int(moved), transcendentals=0),
        name=name,
    )(*arrays)


def whole(array):
    return (array, pl.BlockSpec(array.shape, lambda i: (0,) * array.ndim))


def rows_tiled(array, tile=TILE):
    return (array, pl.BlockSpec((tile, array.shape[1]), lambda i: (i, 0)))


def cols_tiled(array, tile, first=0):
    return (array, pl.BlockSpec((array.shape[0], tile), lambda i: (0, i + first)))


def shape_of(shape, dtype):
    return jax.ShapeDtypeStruct(shape, dtype)


def pad_kernel(wa, pa, wc, pc, wa_out, pa_out, wc_out, pc_out):
    for src, dst in ((wa, wa_out), (wc, wc_out)):
        blank = jnp.zeros((src.shape[0], LANE - HD), bf16)
        for j in range(src.shape[1] // HD):
            dst[:, LANE * j : LANE * (j + 1)] = jnp.concatenate([src[:, HD * j : HD * (j + 1)], blank], axis=1)
    for src, dst in ((pa, pa_out), (pc, pc_out)):
        blank = jnp.zeros((LANE - HD, src.shape[1]), bf16)
        for j in range(src.shape[0] // HD):
            dst[LANE * j : LANE * j + HD, :] = src[HD * j : HD * (j + 1), :]
            dst[LANE * j + HD : LANE * (j + 1), :] = blank


def pad_weights(w_qkv1, w_proj1, w_qkv2, w_proj2):
    outs = [
        shape_of((D1, 3 * W1), bf16),
        shape_of((W1, D1), bf16),
        shape_of((D1, 3 * W2), bf16),
        shape_of((W2, D2), bf16),
    ]
    return call(
        pad_kernel,
        (1,),
        [whole(w) for w in (w_qkv1, w_proj1, w_qkv2, w_proj2)],
        [whole(o) for o in outs],
        name="pad_heads",
    )


def source_of(rows_shape, start):
    r = rows_of(rows_shape)
    s = r // 56
    p = r - s * 56 + start
    f = p // CELL
    rest = p - f * CELL
    r2 = rest // 7
    c2 = rest - r2 * 7
    a = s // 2
    return f * (HT * WD) + r2 * (2 * WD) + a * WD + c2 * 2 + (s - 2 * a)


def first_kernel(x, gain, xp, na, kv, mem, xs):
    for i in range(7):
        lo = 196 * i // 16 * 16
        hi = min(QT, (196 * i + 392 + 15) // 16 * 16)
        shape = (TILE, hi - lo)
        pick = jnp.where(source_of(shape, 56 * i) == lanes(shape) + lo, 1.0, 0.0).astype(bf16)
        out = mm(pick, x[0, 0, 0, lo:hi, :])
        for s in range(4):
            xs[PT * s + 56 * i : PT * s + 56 * (i + 1), :] = out[56 * s : 56 * (s + 1)]
    for i in range(STEPS):
        at = slice(TILE * i, TILE * (i + 1))
        v = xs[at, :]
        unit, _ = norm_stats(v)
        n = (unit * gain[...]).astype(bf16)
        xp[at, :] = v.astype(bf16)
        na[at, :] = n
        xs[at, :] = n.astype(f32)
    pooled = pool_rows(xs)
    kv[...] = pooled
    mem[...] = mm(tmean_matrix(), pooled).astype(bf16)


def first(inputs, video, gain):
    outs = [
        shape_of((QT, D1), bf16),
        shape_of((QT, D1), bf16),
        shape_of((PR, D1), bf16),
        shape_of((MR, D1), bf16),
    ]
    x_spec = pl.BlockSpec((1, 1, 1, QT, D1), lambda i: (0, video, 0, 0, 0))
    return call(
        first_kernel,
        (1,),
        [(inputs, x_spec), whole(gain)],
        [whole(o) for o in outs],
        [VMEM((QT, D1), f32)],
        flops=2 * QT * 416 * D1,
        name="first_norm",
    )


def keys_ext(kall, wk, wv, kext, heads, k_out, v_out):
    k = mm(kall, wk)
    v = mm(kall, wv)
    lane = lanes((KR, LANE))
    ones = jnp.where((lane >= HD) & (lane < HD + 3), 1.0, 0.0)
    for h in range(heads):
        at = slice(LANE * h, LANE * (h + 1))
        k_out[:, at] = (k[:, at] + kext).astype(bf16)
        v_out[:, at] = (v[:, at] + ones).astype(bf16)


def head_forward(q, k, v):
    s = mm_nt(q, k)
    top = jnp.max(s, axis=-1, keepdims=True)
    e = jnp.exp2((s - top) * RATE).astype(bf16)
    mixed = mm(e, v)
    total = mixed[:, HD : HD + 1]
    lse = top + jnp.log(total) * (1.0 / SCALE)
    return (mixed * (1.0 / total), put3(q.astype(f32), -lse).astype(bf16))


def one_lane(shape):
    return jnp.where(lanes(shape) % LANE == HD + 3, 1.0, 0.0)


def block1_kernel(
    kv, near, far, kext, na, xp, wq, wk, wv, wp, gain_m, wfc, wout, gain_c,
    kall, k_out, v_out, qe, o_out, za, ha_out, nb_out, ub_out, gp_out, mid_out, pc, mem, xs,
):
    step = pl.program_id(0)

    @pl.when(step == 0)
    def _():
        kall[0:PR, :] = kv[...]
        kall[PR : PR + MR, :] = near[...]
        kall[PR + MR : KR, :] = far[...]
        keys_ext(kall[...], wk[...], wv[...], kext[...], H1, k_out, v_out)

    q = (mm(na[...], wq[...]) + one_lane((TILE, W1))).astype(bf16)
    for h in range(H1):
        at = slice(LANE * h, LANE * (h + 1))
        o, qx = head_forward(q[:, at], k_out[:, at], v_out[:, at])
        qe[:, at] = qx
        o_out[:, at] = o.astype(bf16)
        za[:, at] = (o + q[:, at].astype(f32)).astype(bf16)
    ha = xp[...].astype(f32) + mm(za[...], wp[...])
    ha_out[...] = ha
    unit, _ = norm_stats(ha)
    nb = (unit * gain_m[...]).astype(bf16)
    nb_out[...] = nb
    part = F1 // 3
    mid = ha
    for j in range(3):
        at = slice(part * j, part * (j + 1))
        act, slope = gelu_both(mm(nb, wfc[:, at]))
        act = act.astype(bf16)
        ub_out[:, at] = act
        gp_out[:, at] = slope.astype(bf16)
        mid = mid + mm(act, wout[at, :])
    mid_out[...] = mid
    unit, _ = norm_stats(mid)
    xs[pl.ds(pl.multiple_of(step * TILE, TILE), TILE), :] = (unit * gain_c[...]).astype(bf16).astype(f32)

    @pl.when(step == STEPS - 1)
    def _():
        pooled = pool_rows(xs)
        pc[...] = pooled
        mem[...] = mm(tmean_matrix(), pooled).astype(bf16)


def block1(kv, near, far, kext, na, xp, w, wp, gain_m, wfc, wout, gain_c):
    ins = [whole(kv), whole(near), whole(far), whole(kext), rows_tiled(na), rows_tiled(xp)]
    ins += [cols_fixed(w, W1, j) for j in range(3)]
    ins += [whole(wp), whole(gain_m), whole(wfc), whole(wout), whole(gain_c)]
    outs = [
        whole(shape_of((KR, D1), bf16)),
        whole(shape_of((KR, W1), bf16)),
        whole(shape_of((KR, W1), bf16)),
        rows_tiled(shape_of((QT, W1), bf16)),
        rows_tiled(shape_of((QT, W1), bf16)),
        rows_tiled(shape_of((QT, W1), bf16)),
        rows_tiled(shape_of((QT, D1), f32)),
        rows_tiled(shape_of((QT, D1), bf16)),
        rows_tiled(shape_of((QT, F1), bf16)),
        rows_tiled(shape_of((QT, F1), bf16)),
        rows_tiled(shape_of((QT, D1), f32)),
        whole(shape_of((PR, D1), bf16)),
        whole(shape_of((MR, D1), bf16)),
    ]
    flops = 2 * QT * (D1 * W1 * 2 + 2 * D1 * F1 + 4 * KR * W1)
    return call(block1_kernel, (STEPS,), ins, outs, [VMEM((QT, D1), f32)], flops=flops, name="block1_forward")


def cols_fixed(array, tile, at):
    return (array, pl.BlockSpec((array.shape[0], tile), lambda i: (0, at)))


PAIR = 2 * LANE


def block2_kernel(pc, near, far, kext, wq, wk, wv, wskip, wp, kall, k_out, v_out, qe, o_out, zc, hc):
    @pl.when(pl.program_id(0) == 0)
    def _():
        kall[0:PR, :] = pc[...]
        kall[PR : PR + MR, :] = near[...]
        kall[PR + MR : KR, :] = far[...]
        hc[...] = mm(pc[...], wskip[...])

    keys_ext(kall[...], wk[...], wv[...], kext[...], 2, k_out, v_out)
    q = (mm(pc[...], wq[...]) + one_lane((PR, PAIR))).astype(bf16)
    for h in range(2):
        at = slice(LANE * h, LANE * (h + 1))
        o, qx = head_forward(q[:, at], k_out[:, at], v_out[:, at])
        qe[:, at] = qx
        o_out[:, at] = o.astype(bf16)
        zc[:, at] = (o + q[:, at].astype(f32)).astype(bf16)
    hc[...] += mm(zc[...], wp[...])


def block2(pc, near, far, kext, w, wskip, wp):
    pairs = H2 // 2
    ins = [whole(pc), whole(near), whole(far), whole(kext)]
    ins += [cols_tiled(w, PAIR, j * pairs) for j in range(3)]
    ins += [whole(wskip), rows_tiled(wp, PAIR)]
    outs = [whole(shape_of((KR, D1), bf16))]
    outs += [cols_tiled(shape_of((n, W2), bf16), PAIR) for n in (KR, KR, PR, PR, PR)]
    outs += [whole(shape_of((PR, D2), f32))]
    flops = 2 * (PR * D1 * (W2 + D2) + 2 * KR * D1 * W2 + PR * W2 * D2 + 4 * PR * KR * W2)
    return call(block2_kernel, (pairs,), ins, outs, flops=flops, name="block2_attention")


PART = 768


def pick_share(micro, even, odd):
    first_ = micro == 0
    return (jnp.where(first_, even, odd).astype(bf16), jnp.where(first_, odd, even).astype(bf16))


def mlp2_kernel(micro, h0, h1, cot, gain, wfc, wout, out, gh, keep_fc, send_fc, keep_out, send_out, gg, hs, nd, ndt, gm, acc, dn):
    step = pl.program_id(0)

    @pl.when(step == 0)
    def _():
        blank = jnp.zeros((PR - PT, D2), f32)
        for b, h in enumerate((h0, h1)):
            at = slice(PR * b, PR * (b + 1))
            v = h[...]
            hs[at, :] = v
            unit, _ = norm_stats(v)
            nd[at, :] = (unit * gain[...]).astype(bf16)
            g = cot[0, b, 0].astype(f32)
            gm[at, :] = jnp.concatenate([g, blank], axis=0).astype(bf16)
        ndt[...] = nd[...].T

    act, slope = gelu_both(mm(nd[...], wfc[...]))
    act = act.astype(bf16)
    gi = (slope * mm_nt(gm[...], wout[...])).astype(bf16)
    m = micro[0]
    gw = mm_tn(act, gm[...])
    rows = keep_fc.shape[1]
    for i in range(keep_out.shape[0]):
        keep, send = pick_share(m, gw[8 * rows * i : 8 * rows * i + 4 * rows], gw[8 * rows * i + 4 * rows : 8 * rows * (i + 1)])
        for a in range(4):
            keep_out[i, :, D2 * a : D2 * (a + 1)] = keep[rows * a : rows * (a + 1)]
            send_out[i, :, D2 * a : D2 * (a + 1)] = send[rows * a : rows * (a + 1)]
    gw = mm(ndt[...], gi)
    for i in range(keep_fc.shape[0]):
        keep, send = pick_share(m, gw[2 * rows * i : 2 * rows * i + rows], gw[2 * rows * i + rows : 2 * rows * (i + 1)])
        keep_fc[i] = keep
        send_fc[i] = send
    o = mm(act, wout[...])
    d = mm_nt(gi, wfc[...])

    @pl.when(step == 0)
    def _():
        acc[...] = o
        dn[...] = d

    @pl.when(step > 0)
    def _():
        acc[...] += o
        dn[...] += d

    @pl.when(step == F2 // PART - 1)
    def _():
        v = hs[...]
        y = v + acc[...]
        unit, inv = norm_stats(v)
        dx, dg = norm_back(dn[...], unit, inv, gain[...])
        gg[...] = dg
        g = (gm[...].astype(f32) + dx).astype(bf16)
        for b in range(2):
            out[0, b, 0] = y[PR * b : PR * b + PT].astype(bf16)
            gh[b] = g[PR * b : PR * (b + 1)]


def scalar(value):
    return (value.astype(jnp.int32).reshape(1), pl.BlockSpec(memory_space=pltpu.SMEM))


def mlp2(micro, clips, h0, h1, cot, gain, wfc, wout):
    rows = D2 // (2 * clips)
    steps = F2 // PART
    ins = [scalar(micro), whole(h0), whole(h1), whole(cot), whole(gain), cols_tiled(wfc, PART), rows_tiled(wout, PART)]
    share = shape_of((clips, rows, F2), bf16)
    fc_spec = (share, pl.BlockSpec((clips, rows, PART), lambda i: (0, 0, i)))
    out_spec = (share, pl.BlockSpec((clips // steps, rows, F2), lambda i: (i, 0, 0)))
    outs = [
        whole(shape_of(cot.shape, bf16)),
        whole(shape_of((2, PR, D2), bf16)),
        fc_spec,
        fc_spec,
        out_spec,
        out_spec,
        whole(shape_of((1, D2), f32)),
    ]
    n = 2 * PR
    scratch = [
        VMEM((n, D2), f32),
        VMEM((n, D2), bf16),
        VMEM((D2, n), bf16),
        VMEM((n, D2), bf16),
        VMEM((n, D2), f32),
        VMEM((n, D2), f32),
    ]
    return call(mlp2_kernel, (steps,), ins, outs, scratch, flops=12 * n * D2 * F2, name="block2_mlp")


def head_backward(q, g, k, v, tiles):
    kt = k.T
    dk = jnp.zeros((KR, LANE), f32)
    dv = jnp.zeros((KR, LANE), f32)
    dqs = []
    for at in tiles:
        p = jnp.exp2(mm_nt(k, q[at]) * RATE)
        ds = (p * mm_nt(v, g[at])).astype(bf16)
        dv = dv + mm(p.astype(bf16), g[at])
        dk = dk + mm(ds, q[at])
        dqs.append((mm(kt, ds) * SCALE).T)
    return (dqs, dk * SCALE, dv)


def grad_ext(gz, o):
    delta = jnp.sum(jnp.where(lanes(gz.shape) < HD, gz.astype(f32) * o.astype(f32), 0.0), axis=-1, keepdims=True)
    return put3(gz.astype(f32), -delta).astype(bf16)


def att2_back_kernel(carry, *refs):
    n_in = 15 + (5 if carry else 0)
    gh, wp, qe, o, k, v, zc, pc, kall, wskip, wq, wk, wv, _, _ = refs[:15]
    before = refs[15:n_in]
    dnear, dfar, dpc, gq_w, gk_w, gv_w, gp_w, gs_w, dkv = refs[n_in:]
    step = pl.program_id(0)

    def out(ref, value, i):
        ref[...] = value + before[i][...] if carry else value

    @pl.when(step == 0)
    def _():
        dpc[...] = mm_nt(gh[0], wskip[...])
        out(gs_w, mm_tn(pc[...], gh[0]), 4)
        dkv[...] = jnp.zeros_like(dkv)

    gz = mm_nt(gh[0], wp[...]).astype(bf16)
    out(gp_w, mm_tn(zc[...], gh[0]), 3)
    gq, dk, dv = [], [], []
    for h in range(2):
        at = slice(LANE * h, LANE * (h + 1))
        g = grad_ext(gz[:, at], o[:, at])
        dqs, dkh, dvh = head_backward(qe[:, at], g, k[:, at], v[:, at], [slice(0, PR)])
        gq.append((gz[:, at].astype(f32) + dqs[0]).astype(bf16))
        dk.append(dkh.astype(bf16))
        dv.append(dvh.astype(bf16))
    gq = jnp.concatenate(gq, axis=1)
    dk = jnp.concatenate(dk, axis=1)
    dv = jnp.concatenate(dv, axis=1)
    dpc[...] += mm_nt(gq, wq[...])
    dkv[...] += mm_nt(dk, wk[...]) + mm_nt(dv, wv[...])
    out(gq_w, mm_tn(pc[...], gq), 0)
    out(gk_w, mm_tn(kall[...], dk), 1)
    out(gv_w, mm_tn(kall[...], dv), 2)

    @pl.when(step == H2 // 2 - 1)
    def _():
        dpc[...] += dkv[0:PR, :]
        dnear[...] = dkv[PR : PR + MR, :].astype(bf16)
        dfar[...] = dkv[PR + MR : KR, :].astype(bf16)


def att2_back(video, gh, wp, qe, o, k, v, zc, pc, kall, wskip, w, before):
    pairs = H2 // 2
    ins = [(gh, pl.BlockSpec((1, PR, D2), lambda i: (video, 0, 0))), rows_tiled(wp, PAIR)]
    ins += [cols_tiled(a, PAIR) for a in (qe, o, k, v, zc)]
    ins += [whole(pc), whole(kall), whole(wskip)]
    ins += [cols_tiled(w, PAIR, j * pairs) for j in range(3)]
    tiny = jnp.zeros((8, LANE), f32)
    ins += [whole(tiny), whole(tiny)]
    grads = [cols_tiled(shape_of((D1, W2), f32), PAIR) for _ in range(3)]
    grads += [rows_tiled(shape_of((W2, D2), f32), PAIR), whole(shape_of((D1, D2), f32))]
    if before is not None:
        ins += [(b, s) for b, (_, s) in zip(before, grads)]
    outs = [
        whole(shape_of((MR, D1), bf16)),
        whole(shape_of((MR, D1), bf16)),
        whole(shape_of((PR, D1), f32)),
    ] + grads
    flops = 2 * (10 * PR * KR * W2 + 4 * PR * D1 * W2 + 4 * KR * D1 * W2 + 4 * PR * W2 * D2)
    return call(
        partial(att2_back_kernel, before is not None),
        (pairs,),
        ins,
        outs,
        [VMEM((KR, D1), f32)],
        flops=flops,
        name="block2_attention_back",
    )


def mlp1_back_kernel(carry, *refs):
    n_in = 14 + (3 if carry else 0)
    dpc, rn, rf, gain_c, gain_m, mid, ha, nb, ub, gp, za, o, wout, wfc = refs[:14]
    n_in += 1
    wp = refs[14]
    before = refs[15:n_in]
    gha, gze, gg_c, gg_m, gw_out, gw_fc, gw_p, ds = refs[n_in:]
    step = pl.program_id(0)

    @pl.when(step == 0)
    def _():
        got = (rn[...].astype(f32) + rf[...].astype(f32)).astype(bf16)
        d = 0.25 * (dpc[...] + mm_tn(tmean_matrix(), got))
        for s in range(4):
            ds[PT * s : PT * (s + 1), :] = d[0:PT]
        gg_c[...] = jnp.zeros_like(gg_c)
        gg_m[...] = jnp.zeros_like(gg_m)
        for i, ref in enumerate((gw_out, gw_fc, gw_p)):
            ref[...] = before[i][...] if carry else jnp.zeros_like(ref)

    unit, inv = norm_stats(mid[...])
    dnc = ds[pl.ds(pl.multiple_of(step * TILE, TILE), TILE), :]
    gmid, dg = norm_back(dnc, unit, inv, gain_c[...])
    gg_c[...] += dg
    gm = gmid.astype(bf16)
    gmt = gm.T
    nbt = nb[...].T
    part = F1 // 3
    dn = jnp.zeros((TILE, D1), f32)
    for j in range(3):
        at = slice(part * j, part * (j + 1))
        gi = (gp[:, at].astype(f32) * mm_nt(gm, wout[at, :])).astype(bf16)
        gw_out[:, at] += mm(gmt, ub[:, at])
        gw_fc[:, at] += mm(nbt, gi)
        dn = dn + mm_nt(gi, wfc[:, at])
    unit, inv = norm_stats(ha[...])
    dx, dg = norm_back(dn, unit, inv, gain_m[...])
    gg_m[...] += dg
    g = gmid + dx
    gha[...] = g
    gh = g.astype(bf16)
    gw_p[...] += mm_tn(za[...], gh)
    gz = mm_nt(gh, wp[...]).astype(bf16)
    for h in range(H1):
        at = slice(LANE * h, LANE * (h + 1))
        gze[:, at] = grad_ext(gz[:, at], o[:, at])


def mlp1_back(dpc, rn, rf, gain_c, gain_m, mid, ha, nb, ub, gp, za, o, wout, wfc, wp, before):
    ins = [whole(a) for a in (dpc, rn, rf, gain_c, gain_m)]
    ins += [rows_tiled(a) for a in (mid, ha, nb, ub, gp, za, o)]
    ins += [whole(wout), whole(wfc), whole(wp)]
    grads = [whole(shape_of((D1, F1), f32)), whole(shape_of((D1, F1), f32)), whole(shape_of((W1, D1), f32))]
    if before is not None:
        ins += [(b, s) for b, (_, s) in zip(before, grads)]
    outs = [
        rows_tiled(shape_of((QT, D1), f32)),
        rows_tiled(shape_of((QT, W1), bf16)),
        whole(shape_of((1, D1), f32)),
        whole(shape_of((1, D1), f32)),
    ] + grads
    flops = 2 * QT * (4 * D1 * F1 + 2 * D1 * W1)
    return call(
        partial(mlp1_back_kernel, before is not None),
        (STEPS,),
        ins,
        outs,
        [VMEM((QT, D1), f32)],
        flops=flops,
        name="block1_mlp_back",
    )


QUERY_TILES = [slice(0, 512), slice(512, 1024), slice(1024, QT)]


def att1_back_kernel(carry, *refs):
    n_in = 9 + (3 if carry else 0)
    qe, gze, k, v, na, kall, wq, wk, wv = refs[:9]
    before = refs[9:n_in]
    dnear, dfar, down, dna, gq_w, gk_w, gv_w, dkv, nat = refs[n_in:]
    step = pl.program_id(0)

    def out(ref, value, i):
        ref[...] = value + before[i][...] if carry else value

    @pl.when(step == 0)
    def _():
        dkv[...] = jnp.zeros_like(dkv)
        dna[...] = jnp.zeros_like(dna)
        nat[...] = na[...].T

    gq, dk, dv = [[] for _ in QUERY_TILES], [], []
    for h in range(2):
        at = slice(LANE * h, LANE * (h + 1))
        g = gze[:, at]
        dqs, dkh, dvh = head_backward(qe[:, at], g, k[:, at], v[:, at], QUERY_TILES)
        for i, rows in enumerate(QUERY_TILES):
            gq[i].append((g[rows].astype(f32) + dqs[i]).astype(bf16))
        dk.append(dkh.astype(bf16))
        dv.append(dvh.astype(bf16))
    gq = jnp.concatenate([jnp.concatenate(t, axis=1) for t in gq], axis=0)
    lane = lanes((1, PAIR)) % LANE
    gq = jnp.where(lane < HD, gq, jnp.zeros_like(gq))
    dk = jnp.concatenate(dk, axis=1)
    dv = jnp.concatenate(dv, axis=1)
    dna[...] += mm_nt(gq, wq[...])
    dkv[...] += mm_nt(dk, wk[...]) + mm_nt(dv, wv[...])
    out(gq_w, mm(nat[...], gq), 0)
    out(gk_w, mm_tn(kall[...], dk), 1)
    out(gv_w, mm_tn(kall[...], dv), 2)

    @pl.when(step == H1 // 2 - 1)
    def _():
        down[...] = dkv[0:PR, :]
        dnear[...] = dkv[PR : PR + MR, :].astype(bf16)
        dfar[...] = dkv[PR + MR : KR, :].astype(bf16)


def att1_back(qe, gze, k, v, na, kall, w, before):
    pairs = H1 // 2
    ins = [cols_tiled(a, PAIR) for a in (qe, gze, k, v)]
    ins += [whole(na), whole(kall)]
    ins += [cols_tiled(w, PAIR, j * pairs) for j in range(3)]
    grads = [cols_tiled(shape_of((D1, W1), f32), PAIR) for _ in range(3)]
    if before is not None:
        ins += [(b, s) for b, (_, s) in zip(before, grads)]
    outs = [
        whole(shape_of((MR, D1), bf16)),
        whole(shape_of((MR, D1), bf16)),
        whole(shape_of((PR, D1), f32)),
        whole(shape_of((QT, D1), f32)),
    ] + grads
    flops = 2 * (10 * QT * KR * W1 + 2 * QT * D1 * W1 + 4 * KR * D1 * W1)
    return call(
        partial(att1_back_kernel, before is not None),
        (pairs,),
        ins,
        outs,
        [VMEM((KR, D1), f32), VMEM((D1, QT), bf16)],
        flops=flops,
        name="block1_attention_back",
    )


def last_kernel(dna, down, rn, rf, xp, gha, gain, gx, gg, gs, ds):
    got = (rn[...].astype(f32) + rf[...].astype(f32)).astype(bf16)
    d = 0.25 * (down[...] + mm_tn(tmean_matrix(), got))
    for s in range(4):
        ds[PT * s : PT * (s + 1), :] = d[0:PT]
    total = jnp.zeros((1, D1), f32)
    for i in range(STEPS):
        at = slice(TILE * i, TILE * (i + 1))
        unit, inv = norm_stats(xp[at, :].astype(f32))
        dx, dg = norm_back(dna[at, :] + ds[at, :], unit, inv, gain[...])
        total = total + dg
        gs[at, :] = gha[at, :] + dx
    gg[...] = total
    for i in range(STEPS):
        lo = min(CELL * i // 8 * 8, PT - 112)
        window = jnp.concatenate([gs[PT * s + lo : PT * s + lo + 112, :] for s in range(4)], axis=0).astype(bf16)
        shape = (TILE, 4 * 112)
        t = rows_of(shape) + TILE * i
        f = t // (HT * WD)
        rest = t - f * (HT * WD)
        r = rest // WD
        c = rest - r * WD
        r2 = r // 2
        c2 = c // 2
        s = 2 * (r - 2 * r2) + (c - 2 * c2)
        p = f * CELL + r2 * 7 + c2
        pick = jnp.where(s * 112 + p - lo == lanes(shape), 1.0, 0.0).astype(bf16)
        gx[TILE * i : TILE * (i + 1), :] = mm(pick, window).astype(bf16)


def last(dna, down, rn, rf, xp, gha, gain):
    outs = [shape_of((QT, D1), bf16), shape_of((1, D1), f32)]
    return call(
        last_kernel,
        (1,),
        [whole(a) for a in (dna, down, rn, rf, xp, gha, gain)],
        [whole(o) for o in outs],
        [VMEM((QT, D1), f32), VMEM((QT, D1), f32)],
        flops=2 * QT * 448 * D1,
        name="last_norm_back",
    )


def shift(value, steps):
    count = lax.axis_size("clip")
    first_, last_ = (max(0, -steps), min(count, count - steps))
    return lax.ppermute(value, "clip", [(s, s + steps) for s in range(first_, last_)])


def swap(value, axis, bit=0):
    n = lax.axis_size(axis)
    return lax.ppermute(value, axis, [(i, i ^ (1 << bit)) for i in range(n)])


def strip(grad):
    return jnp.concatenate([grad[:, LANE * h : LANE * h + HD] for h in range(grad.shape[1] // LANE)], axis=1)


def pack2_kernel(micro, gq, gk, gv, gp, gs, keep_a, send_a, keep_b, send_b, qkv):
    for j, g in enumerate((gq, gk, gv)):
        qkv[:, D2 * j : D2 * (j + 1)] = strip(g[...])
    clips, rows, _ = keep_a.shape
    first_ = micro[0] == 0

    def proj(share, a):
        lo = rows * (2 * share + a)
        h = lo // HD
        if (lo + rows - 1) // HD == h:
            return gp[lo + (LANE - HD) * h : lo + (LANE - HD) * h + rows, :]
        cut = HD * (h + 1) - lo
        top = gp[lo + (LANE - HD) * h : lo + (LANE - HD) * h + cut, :]
        return jnp.concatenate([top, gp[LANE * (h + 1) : LANE * (h + 1) + rows - cut, :]], axis=0)

    for i in range(clips):
        for keep, send, piece in (
            (keep_a, send_a, lambda n: qkv[rows * n : rows * (n + 1), :]),
            (keep_b, send_b, lambda n: jnp.concatenate([proj(n, 0), proj(n, 1), gs[rows * n : rows * (n + 1), :]], axis=1)),
        ):
            k, t = pick_share(micro[0], piece(2 * i), piece(2 * i + 1))
            keep[i] = k
            send[i] = t


def pack2(micro, clips, grads):
    share = shape_of((clips, D1 // (2 * clips), 3 * D2), bf16)
    return call(
        pack2_kernel,
        (1,),
        [scalar(micro)] + [whole(g) for g in grads],
        [whole(share)] * 4,
        [VMEM((D1, 3 * D2), f32)],
        name="pack_block2_grads",
    )


def pack1_kernel(micro, gq, gk, gv, gp, gfc, gout, keep_a, send_a, keep_b, send_b, qkv, out):
    for j, g in enumerate((gq, gk, gv)):
        qkv[:, D1 * j : D1 * (j + 1)] = strip(g[...])
    for h in range(H1):
        qkv[HD * h : HD * (h + 1), 3 * D1 :] = gp[LANE * h : LANE * h + HD, :]
    out[...] = gout[...].T
    clips, rows, _ = keep_a.shape
    half = 2 * D1

    def piece_a(n):
        at = slice(rows * n, rows * (n + 1))
        return jnp.concatenate([gfc[at, :], qkv[at, :half]], axis=1)

    def piece_b(n):
        at = slice(rows * n, rows * (n + 1))
        blocks = [out[rows * (4 * n + a) : rows * (4 * n + a + 1), :] for a in range(4)]
        return jnp.concatenate(blocks + [qkv[at, half:]], axis=1)

    for i in range(clips):
        for keep, send, piece in ((keep_a, send_a, piece_a), (keep_b, send_b, piece_b)):
            k, t = pick_share(micro[0], piece(2 * i), piece(2 * i + 1))
            keep[i] = k
            send[i] = t


def pack1(micro, clips, grads):
    share = shape_of((clips, D1 // (2 * clips), 6 * D1), bf16)
    return call(
        pack1_kernel,
        (1,),
        [scalar(micro)] + [whole(g) for g in grads],
        [whole(share)] * 4,
        [VMEM((D1, 4 * D1), f32), VMEM((F1, D1), f32)],
        name="pack_block1_grads",
    )


def add_up(a, b):
    return a.astype(f32) + b.astype(f32)


def over_micro(parts):
    keep_a, send_a, keep_b, send_b = parts
    return (keep_a, swap(send_a, "micro"), keep_b, swap(send_b, "micro"))


def over_group(parts):
    keep_a, got_a, keep_b, got_b = parts
    first_ = lax.axis_index("group") == 0
    a, b = add_up(keep_a, got_a), add_up(keep_b, got_b)
    keep = jnp.where(first_, a, b).astype(bf16)
    send = jnp.where(first_, b, a).astype(bf16)
    return (keep, swap(send, "group"))


def over_clip(parts, bit):
    total = add_up(*parts).astype(bf16)
    bits = lax.axis_size("clip").bit_length() - 1
    v = total.reshape((2 ** (bits - bit - 1), 2) + total.shape[1:])
    mine = (lax.axis_index("clip") >> bit) & 1
    keep = lax.dynamic_index_in_dim(v, mine, 1, keepdims=False)
    send = lax.dynamic_index_in_dim(v, 1 - mine, 1, keepdims=False)
    return (keep, swap(send, "clip", bit))


def settle(parts):
    total = add_up(*parts).astype(bf16)[0]
    other = swap(total, "group")
    first_ = lax.axis_index("group") == 0
    return (jnp.where(first_, total, other).astype(f32), jnp.where(first_, other, total).astype(f32))


def stack_blocks(v, count):
    return jnp.concatenate(jnp.split(v, count, axis=1), axis=0)


def tied(held, *others):
    flat, tree = jax.tree.flatten((held, others))
    held, others = jax.tree.unflatten(tree, lax.optimization_barrier(flat))
    return (held, *others)


def body(inputs, offsets, cotangent, gain_attn1, w_qkv1, w_proj1, gain_mlp1, w_fc1, w_out1,
         gain_attn2, w_qkv2, w_proj2, w_skip, gain_mlp2, w_fc2, w_out2):
    videos = range(inputs.shape[1])
    clip = lax.axis_index("clip")
    g_a1, g_m1, g_a2, g_m2 = (g.reshape(1, -1) for g in (gain_attn1, gain_mlp1, gain_attn2, gain_mlp2))
    row = jnp.arange(KR, dtype=jnp.int32)[:, None]
    place = jnp.where(row < PR + MR, row - PR, row - PR - MR)
    later = (place // CELL >= offsets[0]) & (place < MT)
    hops = jnp.where(row < PR + MR, 1, 2)
    valid = jnp.where(row < PR, row < PT, later & (clip >= hops))
    lane = jnp.arange(LANE, dtype=jnp.int32)[None, :]
    kext = jnp.where(lane == HD + 3, jnp.where(valid, 0.0, -1e30), jnp.where((lane >= HD) & (lane < HD + 3), 1.0, 0.0))
    kext = kext.astype(f32)

    w1p, p1p, w2p, p2p = pad_weights(w_qkv1, w_proj1, w_qkv2, w_proj2)
    xp, na, kva, mema = zip(*[first(inputs, b, g_a1) for b in videos])
    a = [
        block1(kva[b], shift(mema[b], 1), shift(mema[b], 2), kext, na[b], xp[b], w1p, p1p, g_m1, w_fc1, w_out1, g_a2)
        for b in videos
    ]
    ka, Ka, Va, qea, oa, za, ha, nb, ub, gp, mid, pc, memc = zip(*a)
    c = [block2(pc[b], shift(memc[b], 1), shift(memc[b], 2), kext, w2p, w_skip, p2p) for b in videos]
    kc, Kc, Vc, qec, oc, zc, hc = zip(*c)
    micro, clips = lax.axis_index("micro"), lax.axis_size("clip")
    bits = clips.bit_length() - 1
    output, gh, keep_fc, send_fc, keep_out, send_out, gg_mlp2 = mlp2(micro, clips, hc[0], hc[1], cotangent, g_m2, w_fc2, w_out2)
    big = over_micro((keep_fc, send_fc, keep_out, send_out))

    before, dn2, df2, dpc = None, [], [], []
    for b in videos:
        if b == 1:
            big, gh = tied(big, gh)
            big = over_group(big)
        near, far, d, *before = att2_back(
            b, gh, p2p, qec[b], oc[b], Kc[b], Vc[b], zc[b], pc[b], kc[b], w_skip, w2p, before
        )
        dn2.append(shift(near, -1))
        df2.append(shift(far, -2))
        dpc.append(d)
    middle = over_micro(pack2(micro, clips, before))
    before, gha, gze, gg_c, gg_m = None, [], [], 0.0, 0.0
    for b in videos:
        d = dpc[b]
        if b == 1:
            big, middle, d = tied(big, middle, d)
            big = over_clip(big, 0)
            middle = over_group(middle)
        g, z, gc, gm, *before = mlp1_back(
            d, dn2[b], df2[b], g_a2, g_m1, mid[b], ha[b], nb[b], ub[b], gp[b], za[b], oa[b], w_out1, w_fc1, p1p, before
        )
        gha.append(g)
        gze.append(z)
        gg_c = gg_c + gc
        gg_m = gg_m + gm
    gw_out1t, gw_fc1, gp1 = before
    before, dn1, df1, down, dna = None, [], [], [], []
    for b in videos:
        z = gze[b]
        if b == 0:
            big, middle, z = tied(big, middle, z)
            big = over_clip(big, 1)
            middle = over_clip(middle, 0)
        else:
            big, middle, z = tied(big, middle, z)
            for bit in range(2, bits):
                big = over_clip(big, bit)
            middle = over_clip(middle, 1)
        near, far, d, dn, *before = att1_back(qea[b], z, Ka[b], Va[b], na[b], ka[b], w1p, before)
        dn1.append(shift(near, -1))
        df1.append(shift(far, -2))
        down.append(d)
        dna.append(dn)
    small = over_micro(pack1(micro, clips, list(before) + [gp1, gw_fc1, gw_out1t]))
    ends = [last(dna[b], down[b], dn1[b], df1[b], xp[b], gha[b], g_a1) for b in videos]
    gx = jnp.stack([e[0] for e in ends])
    gg_a = ends[0][1] + ends[1][1]
    gains = jnp.concatenate([gg_a, gg_m, gg_c, gg_mlp2], axis=1)
    gains = gains + swap(gains, "micro")
    gains = gains + swap(gains, "group")
    for bit in range(bits):
        gains = gains + swap(gains, "clip", bit)
    for bit in range(2, bits):
        middle = over_clip(middle, bit)
    small = over_group(small)
    for bit in range(bits):
        small = over_clip(small, bit)
    gw_fc2, gw_out2 = settle(big)
    gw_qkv2, rest2 = settle(middle)
    left, right = settle(small)
    r = rest2.shape[0]
    shares = (
        jnp.concatenate([left[:, F1:], right[:, F1 : F1 + D1]], axis=1),
        right[:, F1 + D1 :],
        left[:, :F1],
        stack_blocks(right[:, :F1], 4),
        gw_qkv2,
        stack_blocks(rest2[:, : 2 * D2], 2),
        rest2[:, 2 * D2 :],
        gw_fc2,
        stack_blocks(gw_out2, 4),
    )
    gains = jnp.split(gains.reshape(-1), [D1, 2 * D1, 3 * D1])
    return (output, gx.reshape(inputs.shape)) + tuple(gains) + tuple(v.reshape(-1) for v in shares)


def solution(mesh):
    tokens = P("group", "micro", "clip", None, None)
    share = P(("clip", "micro"))
    return jax.shard_map(
        body,
        mesh=mesh,
        in_specs=(tokens, P("group"), tokens) + (P(),) * 13,
        out_specs=(tokens, tokens) + (P(),) * 4 + (share,) * 9,
        check_vma=False,
    )
```

```python
from functools import partial

import jax
import jax.numpy as jnp
from jax import lax
from jax.experimental import pallas as pl
from jax.experimental.pallas import tpu as pltpu
from jax.sharding import PartitionSpec as P

D1 = 384
D2 = 768
F1 = 1536
F2 = 3072
QT = 1568
PT = 392
MT = 196
HD = 96
FR = 8
HT = 14
WD = 14
H1 = 4
H2 = 8
CELL = (HT // 2) * (WD // 2)
LANE = 128
PR = 400
MR = 208
KR = PR + 2 * MR
TILE = 784
STEPS = QT // TILE
PIECE = 224
PIECES = QT // PIECE
W1 = H1 * LANE
W2 = H2 * LANE
epsilon = 1e-06
f32 = jnp.float32
bf16 = jnp.bfloat16
SCALE = HD ** (-0.5)
RATE = SCALE * 1.4426950408889634
VMEM = pltpu.VMEM


def mm(a, b):
    return lax.dot_general(a, b, (((1,), (0,)), ((), ())), preferred_element_type=f32)


def mm_nt(a, b):
    return lax.dot_general(a, b, (((1,), (1,)), ((), ())), preferred_element_type=f32)


def mm_tn(a, b):
    return lax.dot_general(a, b, (((0,), (0,)), ((), ())), preferred_element_type=f32)


def lanes(shape):
    return lax.broadcasted_iota(jnp.int32, shape, len(shape) - 1)


def rows_of(shape):
    return lax.broadcasted_iota(jnp.int32, shape, len(shape) - 2)


def norm_stats(values):
    center = values - jnp.mean(values, axis=-1, keepdims=True)
    inv = lax.rsqrt(jnp.mean(center * center, axis=-1, keepdims=True) + epsilon)
    return (center * inv, inv)


def norm_back(grad, unit, inv, gain):
    du = grad * gain
    dg = jnp.sum(grad * unit, axis=0, keepdims=True)
    dx = inv * (
        du - jnp.mean(du, axis=-1, keepdims=True) - unit * jnp.mean(du * unit, axis=-1, keepdims=True)
    )
    return (dx, dg)


def gelu_both(x):
    z = jnp.abs(x)
    t = 1.0 / (1.0 + 0.23164188 * z)
    e = jnp.exp2(x * x * -0.7213475204444817)
    poly = t * (0.127414796 + t * (-0.142248368 + t * (0.7107068705 + t * (-0.7265760135 + t * 0.5307027145))))
    tail = poly * e
    phi = jnp.where(x >= 0.0, 1.0 - tail, tail)
    return (x * phi, phi + (x * 0.3989422804014327) * e)


def split3(v):
    hi = v.astype(bf16).astype(f32)
    mid = (v - hi).astype(bf16).astype(f32)
    return (hi, mid, v - hi - mid)


def put3(base, v):
    hi, mid, low = split3(v)
    lane = lanes(base.shape)
    return jnp.where(
        lane < HD, base, jnp.where(lane == HD, hi, jnp.where(lane == HD + 1, mid, jnp.where(lane == HD + 2, low, base)))
    )


def tmean_matrix():
    rows = rows_of((MR, PR))
    cols = lanes((MR, PR))
    hit = rows < 0
    for pair in range(FR // 2):
        inside = (rows >= pair * CELL) & (rows < (pair + 1) * CELL)
        shift_by = cols - rows - pair * CELL
        hit = hit | (inside & ((shift_by == 0) | (shift_by == CELL)))
    return jnp.where(hit, 0.5, 0.0).astype(bf16)


def pool_rows(ref):
    total = ref[0:PT, :] + ref[PT : 2 * PT, :] + ref[2 * PT : 3 * PT, :] + ref[3 * PT : 4 * PT, :]
    return jnp.concatenate([0.25 * total, jnp.zeros((PR - PT, total.shape[1]), f32)], axis=0).astype(bf16)


def call(kernel, grid, ins, outs, scratch=(), flops=0, name=None):
    arrays = [a for a, _ in ins]
    moved = sum(a.size * a.dtype.itemsize for a in arrays) + sum(s.size * s.dtype.itemsize for s, _ in outs)
    return pl.pallas_call(
        kernel,
        grid=grid,
        in_specs=[s for _, s in ins],
        out_specs=[s for _, s in outs],
        out_shape=[o for o, _ in outs],
        scratch_shapes=list(scratch),
        compiler_params=pltpu.CompilerParams(
            vmem_limit_bytes=58 * 1024 * 1024, dimension_semantics=("arbitrary",) * len(grid)
        ),
        cost_estimate=pl.CostEstimate(flops=int(flops), bytes_accessed=int(moved), transcendentals=0),
        name=name,
    )(*arrays)


def whole(array):
    return (array, pl.BlockSpec(array.shape, lambda i: (0,) * array.ndim))


def rows_tiled(array, tile=TILE):
    return (array, pl.BlockSpec((tile, array.shape[1]), lambda i: (i, 0)))


def cols_tiled(array, tile, first=0):
    return (array, pl.BlockSpec((array.shape[0], tile), lambda i: (0, i + first)))


def shape_of(shape, dtype):
    return jax.ShapeDtypeStruct(shape, dtype)


def pad_kernel(wa, pa, wc, pc, wa_out, pa_out, wc_out, pc_out):
    for src, dst in ((wa, wa_out), (wc, wc_out)):
        blank = jnp.zeros((src.shape[0], LANE - HD), bf16)
        for j in range(src.shape[1] // HD):
            dst[:, LANE * j : LANE * (j + 1)] = jnp.concatenate([src[:, HD * j : HD * (j + 1)], blank], axis=1)
    for src, dst in ((pa, pa_out), (pc, pc_out)):
        blank = jnp.zeros((LANE - HD, src.shape[1]), bf16)
        for j in range(src.shape[0] // HD):
            dst[LANE * j : LANE * j + HD, :] = src[HD * j : HD * (j + 1), :]
            dst[LANE * j + HD : LANE * (j + 1), :] = blank


def pad_weights(w_qkv1, w_proj1, w_qkv2, w_proj2):
    outs = [
        shape_of((D1, 3 * W1), bf16),
        shape_of((W1, D1), bf16),
        shape_of((D1, 3 * W2), bf16),
        shape_of((W2, D2), bf16),
    ]
    return call(
        pad_kernel,
        (1,),
        [whole(w) for w in (w_qkv1, w_proj1, w_qkv2, w_proj2)],
        [whole(o) for o in outs],
        name="pad_heads",
    )


def source_of(rows_shape, start):
    r = rows_of(rows_shape)
    s = r // 56
    p = r - s * 56 + start
    f = p // CELL
    rest = p - f * CELL
    r2 = rest // 7
    c2 = rest - r2 * 7
    a = s // 2
    return f * (HT * WD) + r2 * (2 * WD) + a * WD + c2 * 2 + (s - 2 * a)


def first_kernel(x, gain, xn, kv, mem, xs):
    for i in range(7):
        lo = 196 * i // 16 * 16
        hi = min(QT, (196 * i + 392 + 15) // 16 * 16)
        shape = (PIECE, hi - lo)
        pick = jnp.where(source_of(shape, 56 * i) == lanes(shape) + lo, 1.0, 0.0).astype(bf16)
        out = mm(pick, x[0, 0, 0, lo:hi, :])
        for s in range(4):
            xs[PT * s + 56 * i : PT * s + 56 * (i + 1), :] = out[56 * s : 56 * (s + 1)]
    for i in range(PIECES):
        at = slice(PIECE * i, PIECE * (i + 1))
        v = xs[at, :]
        unit, _ = norm_stats(v)
        n = (unit * gain[...]).astype(bf16)
        xn[at, :D1] = v.astype(bf16)
        xn[at, D1:] = n
        xs[at, :] = n.astype(f32)
    pooled = pool_rows(xs)
    kv[...] = pooled
    mem[...] = mm(tmean_matrix(), pooled).astype(bf16)


def first(inputs, video, gain):
    outs = [
        shape_of((QT, 2 * D1), bf16),
        shape_of((PR, D1), bf16),
        shape_of((MR, D1), bf16),
    ]
    x_spec = pl.BlockSpec((1, 1, 1, QT, D1), lambda i: (0, video, 0, 0, 0))
    return call(
        first_kernel,
        (1,),
        [(inputs, x_spec), whole(gain)],
        [whole(o) for o in outs],
        [VMEM((QT, D1), f32)],
        flops=2 * QT * 416 * D1,
        name="first_norm",
    )


def keys_ext(kall, wk, wv, kext, heads, k_out, v_out):
    k = mm(kall, wk)
    v = mm(kall, wv)
    lane = lanes((KR, LANE))
    ones = jnp.where((lane >= HD) & (lane < HD + 3), 1.0, 0.0)
    for h in range(heads):
        at = slice(LANE * h, LANE * (h + 1))
        k_out[:, at] = (k[:, at] + kext).astype(bf16)
        v_out[:, at] = (v[:, at] + ones).astype(bf16)


def head_forward(q, s, v):
    top = jnp.max(s, axis=-1, keepdims=True)
    e = jnp.exp2((s - top) * RATE).astype(bf16)
    mixed = mm(e, v)
    total = mixed[:, HD : HD + 1]
    lse = top + jnp.log(total) * (1.0 / SCALE)
    return (mixed * (1.0 / total), put3(q.astype(f32), -lse).astype(bf16))


def one_lane(shape):
    return jnp.where(lanes(shape) % LANE == HD + 3, 1.0, 0.0)


def block1_kernel(
    kv, near, far, kext, xn, wq, wk, wv, wp, gain_m, wfc, wout, gain_c,
    kall, k_out, v_out, ozq, hm, ubgp, pc, mem, xs,
):
    step = pl.program_id(0)

    @pl.when(step == 0)
    def _():
        kall[0:PR, :] = kv[...]
        kall[PR : PR + MR, :] = near[...]
        kall[PR + MR : KR, :] = far[...]
        keys_ext(kall[...], wk[...], wv[...], kext[...], H1, k_out, v_out)

    q = (mm(xn[:, D1:], wq[...]) + one_lane((TILE, W1))).astype(bf16)
    heads = [slice(LANE * h, LANE * (h + 1)) for h in range(H1)]
    scores = [mm_nt(q[:, at], k_out[:, at]) for at in heads]
    for h, at in enumerate(heads):
        o, qx = head_forward(q[:, at], scores[h], v_out[:, at])
        ozq[:, 2 * W1 + LANE * h : 2 * W1 + LANE * (h + 1)] = qx
        ozq[:, at] = o.astype(bf16)
        ozq[:, W1 + LANE * h : W1 + LANE * (h + 1)] = (o + q[:, at].astype(f32)).astype(bf16)
    ha = xn[:, :D1].astype(f32) + mm(ozq[:, W1 : 2 * W1], wp[...])
    hm[:, :D1] = ha
    unit, _ = norm_stats(ha)
    nb = (unit * gain_m[...]).astype(bf16)
    part = F1 // 3
    mid = ha
    ahead = mm(nb, wfc[:, :part])
    for j in range(3):
        at = slice(part * j, part * (j + 1))
        inner = ahead
        if j < 2:
            ahead = mm(nb, wfc[:, part * (j + 1) : part * (j + 2)])
        act, slope = gelu_both(inner)
        act = act.astype(bf16)
        ubgp[:, at] = act
        ubgp[:, F1 + part * j : F1 + part * (j + 1)] = slope.astype(bf16)
        mid = mid + mm(act, wout[at, :])
    hm[:, D1:] = mid
    unit, _ = norm_stats(mid)
    xs[pl.ds(pl.multiple_of(step * TILE, TILE), TILE), :] = (unit * gain_c[...]).astype(bf16).astype(f32)

    @pl.when(step == STEPS - 1)
    def _():
        pooled = pool_rows(xs)
        pc[...] = pooled
        mem[...] = mm(tmean_matrix(), pooled).astype(bf16)


def block1(kv, near, far, kext, xn, w, wp, gain_m, wfc, wout, gain_c):
    ins = [whole(kv), whole(near), whole(far), whole(kext), rows_tiled(xn)]
    ins += [cols_fixed(w, W1, j) for j in range(3)]
    ins += [whole(wp), whole(gain_m), whole(wfc), whole(wout), whole(gain_c)]
    outs = [
        whole(shape_of((KR, D1), bf16)),
        whole(shape_of((KR, W1), bf16)),
        whole(shape_of((KR, W1), bf16)),
        rows_tiled(shape_of((QT, 3 * W1), bf16)),
        rows_tiled(shape_of((QT, 2 * D1), f32)),
        rows_tiled(shape_of((QT, 2 * F1), bf16)),
        whole(shape_of((PR, D1), bf16)),
        whole(shape_of((MR, D1), bf16)),
    ]
    flops = 2 * QT * (D1 * W1 * 2 + 2 * D1 * F1 + 4 * KR * W1)
    return call(block1_kernel, (STEPS,), ins, outs, [VMEM((QT, D1), f32)], flops=flops, name="block1_forward")


def cols_fixed(array, tile, at):
    return (array, pl.BlockSpec((array.shape[0], tile), lambda i: (0, at)))


PAIR = 2 * LANE


def block2_kernel(pc, near, far, kext, wq, wk, wv, wskip, wp, kall, k_out, v_out, qe, o_out, zc, hc):
    @pl.when(pl.program_id(0) == 0)
    def _():
        kall[0:PR, :] = pc[...]
        kall[PR : PR + MR, :] = near[...]
        kall[PR + MR : KR, :] = far[...]
        hc[...] = mm(pc[...], wskip[...])

    keys_ext(kall[...], wk[...], wv[...], kext[...], 2, k_out, v_out)
    q = (mm(pc[...], wq[...]) + one_lane((PR, PAIR))).astype(bf16)
    heads = [slice(LANE * h, LANE * (h + 1)) for h in range(2)]
    scores = [mm_nt(q[:, at], k_out[:, at]) for at in heads]
    for h, at in enumerate(heads):
        o, qx = head_forward(q[:, at], scores[h], v_out[:, at])
        qe[:, at] = qx
        o_out[:, at] = o.astype(bf16)
        zc[:, at] = (o + q[:, at].astype(f32)).astype(bf16)
    hc[...] += mm(zc[...], wp[...])


def block2(pc, near, far, kext, w, wskip, wp):
    pairs = H2 // 2
    ins = [whole(pc), whole(near), whole(far), whole(kext)]
    ins += [cols_tiled(w, PAIR, j * pairs) for j in range(3)]
    ins += [whole(wskip), rows_tiled(wp, PAIR)]
    outs = [whole(shape_of((KR, D1), bf16))]
    outs += [cols_tiled(shape_of((n, W2), bf16), PAIR) for n in (KR, KR, PR, PR, PR)]
    outs += [whole(shape_of((PR, D2), f32))]
    flops = 2 * (PR * D1 * (W2 + D2) + 2 * KR * D1 * W2 + PR * W2 * D2 + 4 * PR * KR * W2)
    return call(block2_kernel, (pairs,), ins, outs, flops=flops, name="block2_attention")


PART = 768


def pick_share(micro, even, odd):
    first_ = micro == 0
    return (jnp.where(first_, even, odd).astype(bf16), jnp.where(first_, odd, even).astype(bf16))


def mlp2_kernel(micro, h0, h1, cot, gain, wfc, wout, out, gh, keep_fc, send_fc, keep_out, send_out, gg, hs, nd, ndt, gm, acc, dn):
    step = pl.program_id(0)

    @pl.when(step == 0)
    def _():
        blank = jnp.zeros((PR - PT, D2), f32)
        for b, h in enumerate((h0, h1)):
            at = slice(PR * b, PR * (b + 1))
            v = h[...]
            hs[at, :] = v
            unit, _ = norm_stats(v)
            nd[at, :] = (unit * gain[...]).astype(bf16)
            g = cot[0, b, 0].astype(f32)
            gm[at, :] = jnp.concatenate([g, blank], axis=0).astype(bf16)
        ndt[...] = nd[...].T

    act, slope = gelu_both(mm(nd[...], wfc[...]))
    act = act.astype(bf16)
    gi = (slope * mm_nt(gm[...], wout[...])).astype(bf16)
    m = micro[0]
    gw = mm_tn(act, gm[...])
    rows = keep_fc.shape[1]
    for i in range(keep_out.shape[0]):
        keep, send = pick_share(m, gw[8 * rows * i : 8 * rows * i + 4 * rows], gw[8 * rows * i + 4 * rows : 8 * rows * (i + 1)])
        for a in range(4):
            keep_out[i, :, D2 * a : D2 * (a + 1)] = keep[rows * a : rows * (a + 1)]
            send_out[i, :, D2 * a : D2 * (a + 1)] = send[rows * a : rows * (a + 1)]
    gw = mm(ndt[...], gi)
    for i in range(keep_fc.shape[0]):
        keep, send = pick_share(m, gw[2 * rows * i : 2 * rows * i + rows], gw[2 * rows * i + rows : 2 * rows * (i + 1)])
        keep_fc[i] = keep
        send_fc[i] = send
    o = mm(act, wout[...])
    d = mm_nt(gi, wfc[...])

    @pl.when(step == 0)
    def _():
        acc[...] = o
        dn[...] = d

    @pl.when(step > 0)
    def _():
        acc[...] += o
        dn[...] += d

    @pl.when(step == F2 // PART - 1)
    def _():
        v = hs[...]
        y = v + acc[...]
        unit, inv = norm_stats(v)
        dx, dg = norm_back(dn[...], unit, inv, gain[...])
        gg[...] = dg
        g = (gm[...].astype(f32) + dx).astype(bf16)
        for b in range(2):
            out[0, b, 0] = y[PR * b : PR * b + PT].astype(bf16)
            gh[b] = g[PR * b : PR * (b + 1)]


def scalar(value):
    return (value.astype(jnp.int32).reshape(1), pl.BlockSpec(memory_space=pltpu.SMEM))


def mlp2(micro, clips, h0, h1, cot, gain, wfc, wout):
    rows = D2 // (2 * clips)
    steps = F2 // PART
    ins = [scalar(micro), whole(h0), whole(h1), whole(cot), whole(gain), cols_tiled(wfc, PART), rows_tiled(wout, PART)]
    share = shape_of((clips, rows, F2), bf16)
    fc_spec = (share, pl.BlockSpec((clips, rows, PART), lambda i: (0, 0, i)))
    out_spec = (share, pl.BlockSpec((clips // steps, rows, F2), lambda i: (i, 0, 0)))
    outs = [
        whole(shape_of(cot.shape, bf16)),
        whole(shape_of((2, PR, D2), bf16)),
        fc_spec,
        fc_spec,
        out_spec,
        out_spec,
        whole(shape_of((1, D2), f32)),
    ]
    n = 2 * PR
    scratch = [
        VMEM((n, D2), f32),
        VMEM((n, D2), bf16),
        VMEM((D2, n), bf16),
        VMEM((n, D2), bf16),
        VMEM((n, D2), f32),
        VMEM((n, D2), f32),
    ]
    return call(mlp2_kernel, (steps,), ins, outs, scratch, flops=12 * n * D2 * F2, name="block2_mlp")


def head_backward(q, g, k, v, tiles):
    kt = k.T
    dk = jnp.zeros((KR, LANE), f32)
    dv = jnp.zeros((KR, LANE), f32)
    dqs = []
    for at in tiles:
        p = jnp.exp2(mm_nt(k, q[at]) * RATE)
        ds = (p * mm_nt(v, g[at])).astype(bf16)
        dv = dv + mm(p.astype(bf16), g[at])
        dk = dk + mm(ds, q[at])
        dqs.append((mm(kt, ds) * SCALE).T)
    return (dqs, dk * SCALE, dv)


def grad_ext(gz, o):
    delta = jnp.sum(jnp.where(lanes(gz.shape) < HD, gz.astype(f32) * o.astype(f32), 0.0), axis=-1, keepdims=True)
    return put3(gz.astype(f32), -delta).astype(bf16)


def att2_back_kernel(carry, *refs):
    n_in = 15 + (5 if carry else 0)
    gh, wp, qe, o, k, v, zc, pc, kall, wskip, wq, wk, wv, _, _ = refs[:15]
    before = refs[15:n_in]
    dnear, dfar, dpc, gq_w, gk_w, gv_w, gp_w, gs_w, dkv = refs[n_in:]
    step = pl.program_id(0)

    def out(ref, value, i):
        ref[...] = value + before[i][...] if carry else value

    @pl.when(step == 0)
    def _():
        dpc[...] = mm_nt(gh[0], wskip[...])
        out(gs_w, mm_tn(pc[...], gh[0]), 4)
        dkv[...] = jnp.zeros_like(dkv)

    gz = mm_nt(gh[0], wp[...]).astype(bf16)
    out(gp_w, mm_tn(zc[...], gh[0]), 3)
    gq, dk, dv = [], [], []
    for h in range(2):
        at = slice(LANE * h, LANE * (h + 1))
        g = grad_ext(gz[:, at], o[:, at])
        dqs, dkh, dvh = head_backward(qe[:, at], g, k[:, at], v[:, at], [slice(0, PR)])
        gq.append((gz[:, at].astype(f32) + dqs[0]).astype(bf16))
        dk.append(dkh.astype(bf16))
        dv.append(dvh.astype(bf16))
    gq = jnp.concatenate(gq, axis=1)
    dk = jnp.concatenate(dk, axis=1)
    dv = jnp.concatenate(dv, axis=1)
    dpc[...] += mm_nt(gq, wq[...])
    dkv[...] += mm_nt(dk, wk[...]) + mm_nt(dv, wv[...])
    out(gq_w, mm_tn(pc[...], gq), 0)
    out(gk_w, mm_tn(kall[...], dk), 1)
    out(gv_w, mm_tn(kall[...], dv), 2)

    @pl.when(step == H2 // 2 - 1)
    def _():
        dpc[...] += dkv[0:PR, :]
        dnear[...] = dkv[PR : PR + MR, :].astype(bf16)
        dfar[...] = dkv[PR + MR : KR, :].astype(bf16)


def att2_back(video, gh, wp, qe, o, k, v, zc, pc, kall, wskip, w, before):
    pairs = H2 // 2
    ins = [(gh, pl.BlockSpec((1, PR, D2), lambda i: (video, 0, 0))), rows_tiled(wp, PAIR)]
    ins += [cols_tiled(a, PAIR) for a in (qe, o, k, v, zc)]
    ins += [whole(pc), whole(kall), whole(wskip)]
    ins += [cols_tiled(w, PAIR, j * pairs) for j in range(3)]
    tiny = jnp.zeros((8, LANE), f32)
    ins += [whole(tiny), whole(tiny)]
    grads = [cols_tiled(shape_of((D1, W2), f32), PAIR) for _ in range(3)]
    grads += [rows_tiled(shape_of((W2, D2), f32), PAIR), whole(shape_of((D1, D2), f32))]
    if before is not None:
        ins += [(b, s) for b, (_, s) in zip(before, grads)]
    outs = [
        whole(shape_of((MR, D1), bf16)),
        whole(shape_of((MR, D1), bf16)),
        whole(shape_of((PR, D1), f32)),
    ] + grads
    flops = 2 * (10 * PR * KR * W2 + 4 * PR * D1 * W2 + 4 * KR * D1 * W2 + 4 * PR * W2 * D2)
    return call(
        partial(att2_back_kernel, before is not None),
        (pairs,),
        ins,
        outs,
        [VMEM((KR, D1), f32)],
        flops=flops,
        name="block2_attention_back",
    )


def mlp1_back_kernel(carry, *refs):
    n_in = 11 + (3 if carry else 0)
    dpc, rn, rf, gain_c, gain_m, hm, ubgp, oz, wout, wfc, wp = refs[:11]
    before = refs[11:n_in]
    gha, gze, gg_c, gg_m, gw_out, gw_fc, gw_p, ds = refs[n_in:]
    step = pl.program_id(0)

    @pl.when(step == 0)
    def _():
        got = (rn[...].astype(f32) + rf[...].astype(f32)).astype(bf16)
        d = 0.25 * (dpc[...] + mm_tn(tmean_matrix(), got))
        for s in range(4):
            ds[PT * s : PT * (s + 1), :] = d[0:PT]
        gg_c[...] = jnp.zeros_like(gg_c)
        gg_m[...] = jnp.zeros_like(gg_m)
        for i, ref in enumerate((gw_out, gw_fc, gw_p)):
            ref[...] = before[i][...] if carry else jnp.zeros_like(ref)

    unit, inv = norm_stats(hm[:, D1:])
    dnc = ds[pl.ds(pl.multiple_of(step * TILE, TILE), TILE), :]
    gmid, dg = norm_back(dnc, unit, inv, gain_c[...])
    gg_c[...] += dg
    gm = gmid.astype(bf16)
    gmt = gm.T
    unit_b, inv_b = norm_stats(hm[:, :D1])
    nbt = (unit_b * gain_m[...]).astype(bf16).T
    part = F1 // 3
    dn = jnp.zeros((TILE, D1), f32)
    for j in range(3):
        at = slice(part * j, part * (j + 1))
        slope = ubgp[:, F1 + part * j : F1 + part * (j + 1)].astype(f32)
        gi = (slope * mm_nt(gm, wout[at, :])).astype(bf16)
        gw_out[:, at] += mm(gmt, ubgp[:, at])
        gw_fc[:, at] += mm(nbt, gi)
        dn = dn + mm_nt(gi, wfc[:, at])
    dx, dg = norm_back(dn, unit_b, inv_b, gain_m[...])
    gg_m[...] += dg
    g = gmid + dx
    gha[...] = g
    gh = g.astype(bf16)
    gw_p[...] += mm_tn(oz[:, W1:], gh)
    gz = mm_nt(gh, wp[...]).astype(bf16)
    for h in range(H1):
        at = slice(LANE * h, LANE * (h + 1))
        gze[:, at] = grad_ext(gz[:, at], oz[:, at])


def mlp1_back(dpc, rn, rf, gain_c, gain_m, hm, ubgp, ozq, wout, wfc, wp, before):
    ins = [whole(a) for a in (dpc, rn, rf, gain_c, gain_m)]
    ins += [rows_tiled(hm), rows_tiled(ubgp), (ozq, pl.BlockSpec((TILE, 2 * W1), lambda i: (i, 0)))]
    ins += [whole(wout), whole(wfc), whole(wp)]
    grads = [whole(shape_of((D1, F1), f32)), whole(shape_of((D1, F1), f32)), whole(shape_of((W1, D1), f32))]
    if before is not None:
        ins += [(b, s) for b, (_, s) in zip(before, grads)]
    outs = [
        rows_tiled(shape_of((QT, D1), f32)),
        rows_tiled(shape_of((QT, W1), bf16)),
        whole(shape_of((1, D1), f32)),
        whole(shape_of((1, D1), f32)),
    ] + grads
    flops = 2 * QT * (4 * D1 * F1 + 2 * D1 * W1)
    return call(
        partial(mlp1_back_kernel, before is not None),
        (STEPS,),
        ins,
        outs,
        [VMEM((QT, D1), f32)],
        flops=flops,
        name="block1_mlp_back",
    )


QUERY_TILES = [slice(0, 512), slice(512, 1024), slice(1024, QT)]


def att1_back_kernel(carry, *refs):
    n_in = 9 + (3 if carry else 0)
    qe, gze, k, v, xn, kall, wq, wk, wv = refs[:9]
    before = refs[9:n_in]
    dnear, dfar, down, dna, gq_w, gk_w, gv_w, dkv, nat = refs[n_in:]
    step = pl.program_id(0)

    def out(ref, value, i):
        ref[...] = value + before[i][...] if carry else value

    @pl.when(step == 0)
    def _():
        dkv[...] = jnp.zeros_like(dkv)
        dna[...] = jnp.zeros_like(dna)
        nat[...] = xn[...].T

    gq, dk, dv = [[] for _ in QUERY_TILES], [], []
    for h in range(2):
        at = slice(LANE * h, LANE * (h + 1))
        g = gze[:, at]
        dqs, dkh, dvh = head_backward(qe[:, at], g, k[:, at], v[:, at], QUERY_TILES)
        for i, rows in enumerate(QUERY_TILES):
            gq[i].append((g[rows].astype(f32) + dqs[i]).astype(bf16))
        dk.append(dkh.astype(bf16))
        dv.append(dvh.astype(bf16))
    gq = jnp.concatenate([jnp.concatenate(t, axis=1) for t in gq], axis=0)
    lane = lanes((1, PAIR)) % LANE
    gq = jnp.where(lane < HD, gq, jnp.zeros_like(gq))
    dk = jnp.concatenate(dk, axis=1)
    dv = jnp.concatenate(dv, axis=1)
    dna[...] += mm_nt(gq, wq[...])
    dkv[...] += mm_nt(dk, wk[...]) + mm_nt(dv, wv[...])
    out(gq_w, mm(nat[...], gq), 0)
    out(gk_w, mm_tn(kall[...], dk), 1)
    out(gv_w, mm_tn(kall[...], dv), 2)

    @pl.when(step == H1 // 2 - 1)
    def _():
        down[...] = dkv[0:PR, :]
        dnear[...] = dkv[PR : PR + MR, :].astype(bf16)
        dfar[...] = dkv[PR + MR : KR, :].astype(bf16)


def att1_back(ozq, gze, k, v, xn, kall, w, before):
    pairs = H1 // 2
    ins = [cols_tiled(ozq, PAIR, 2 * pairs)] + [cols_tiled(a, PAIR) for a in (gze, k, v)]
    ins += [cols_fixed(xn, D1, 1), whole(kall)]
    ins += [cols_tiled(w, PAIR, j * pairs) for j in range(3)]
    grads = [cols_tiled(shape_of((D1, W1), f32), PAIR) for _ in range(3)]
    if before is not None:
        ins += [(b, s) for b, (_, s) in zip(before, grads)]
    outs = [
        whole(shape_of((MR, D1), bf16)),
        whole(shape_of((MR, D1), bf16)),
        whole(shape_of((PR, D1), f32)),
        whole(shape_of((QT, D1), f32)),
    ] + grads
    flops = 2 * (10 * QT * KR * W1 + 2 * QT * D1 * W1 + 4 * KR * D1 * W1)
    return call(
        partial(att1_back_kernel, before is not None),
        (pairs,),
        ins,
        outs,
        [VMEM((KR, D1), f32), VMEM((D1, QT), bf16)],
        flops=flops,
        name="block1_attention_back",
    )


def shift(value, steps):
    count = lax.axis_size("clip")
    first_, last_ = (max(0, -steps), min(count, count - steps))
    return lax.ppermute(value, "clip", [(s, s + steps) for s in range(first_, last_)])


def swap(value, axis, bit=0):
    n = lax.axis_size(axis)
    return lax.ppermute(value, axis, [(i, i ^ (1 << bit)) for i in range(n)])


def strip(grad):
    return jnp.concatenate([grad[:, LANE * h : LANE * h + HD] for h in range(grad.shape[1] // LANE)], axis=1)


def fold(v):
    rows, cols = v.shape
    if rows != 24:
        return v
    rest = jnp.concatenate([v[16:, : cols // 2], v[16:, cols // 2 :]], axis=0)
    return jnp.concatenate([v[:16], rest], axis=1)


def unfold(v, rows):
    if rows != 24:
        return v
    cols = v.shape[1] * 2 // 3
    rest = jnp.concatenate([v[:8, cols:], v[8:, cols:]], axis=1)
    return jnp.concatenate([v[:, :cols], rest], axis=0)


def folded(rows, cols):
    return (16, cols * 3 // 2) if rows == 24 else (rows, cols)


def pack2_kernel(micro, gq, gk, gv, gp, gs, keep_a, send_a, keep_b, send_b, qkv):
    for j, g in enumerate((gq, gk, gv)):
        qkv[:, D2 * j : D2 * (j + 1)] = strip(g[...])
    clips, rows = keep_a.shape[0], D1 // (2 * keep_a.shape[0])
    first_ = micro[0] == 0

    def proj(share, a):
        lo = rows * (2 * share + a)
        h = lo // HD
        if (lo + rows - 1) // HD == h:
            return gp[lo + (LANE - HD) * h : lo + (LANE - HD) * h + rows, :]
        cut = HD * (h + 1) - lo
        top = gp[lo + (LANE - HD) * h : lo + (LANE - HD) * h + cut, :]
        return jnp.concatenate([top, gp[LANE * (h + 1) : LANE * (h + 1) + rows - cut, :]], axis=0)

    for i in range(clips):
        for keep, send, piece in (
            (keep_a, send_a, lambda n: qkv[rows * n : rows * (n + 1), :]),
            (keep_b, send_b, lambda n: jnp.concatenate([proj(n, 0), proj(n, 1), gs[rows * n : rows * (n + 1), :]], axis=1)),
        ):
            k, t = pick_share(micro[0], fold(piece(2 * i)), fold(piece(2 * i + 1)))
            keep[i] = k
            send[i] = t


def pack2(micro, clips, grads):
    share = shape_of((clips,) + folded(D1 // (2 * clips), 3 * D2), bf16)
    return call(
        pack2_kernel,
        (1,),
        [scalar(micro)] + [whole(g) for g in grads],
        [whole(share)] * 4,
        [VMEM((D1, 3 * D2), f32)],
        name="pack_block2_grads",
    )


def pack1_kernel(micro, gq, gk, gv, gp, gfc, gout, keep_a, send_a, keep_b, send_b, qkv, out):
    for j, g in enumerate((gq, gk, gv)):
        qkv[:, D1 * j : D1 * (j + 1)] = strip(g[...])
    for h in range(H1):
        qkv[HD * h : HD * (h + 1), 3 * D1 :] = gp[LANE * h : LANE * h + HD, :]
    out[...] = gout[...].T
    clips, rows = keep_a.shape[0], D1 // (2 * keep_a.shape[0])
    half = 2 * D1

    def piece_a(n):
        at = slice(rows * n, rows * (n + 1))
        return jnp.concatenate([gfc[at, :], qkv[at, :half]], axis=1)

    def piece_b(n):
        at = slice(rows * n, rows * (n + 1))
        blocks = [out[rows * (4 * n + a) : rows * (4 * n + a + 1), :] for a in range(4)]
        return jnp.concatenate(blocks + [qkv[at, half:]], axis=1)

    for i in range(clips):
        for keep, send, piece in ((keep_a, send_a, piece_a), (keep_b, send_b, piece_b)):
            k, t = pick_share(micro[0], fold(piece(2 * i)), fold(piece(2 * i + 1)))
            keep[i] = k
            send[i] = t


def pack1(micro, clips, grads):
    share = shape_of((clips,) + folded(D1 // (2 * clips), 6 * D1), bf16)
    return call(
        pack1_kernel,
        (1,),
        [scalar(micro)] + [whole(g) for g in grads],
        [whole(share)] * 4,
        [VMEM((D1, 4 * D1), f32), VMEM((F1, D1), f32)],
        name="pack_block1_grads",
    )


def add_up(a, b):
    return a.astype(f32) + b.astype(f32)


def over_clip(parts, bit, bits_left):
    total = add_up(*parts).astype(bf16)
    low = sum(1 for b in bits_left if b < bit)
    left = len(bits_left)
    v = total.reshape((2 ** (left - 1 - low), 2, 2**low) + total.shape[1:])
    mine = (lax.axis_index("clip") >> bit) & 1

    def part(which):
        w = lax.dynamic_index_in_dim(v, which, 1, keepdims=False)
        return w.reshape((2 ** (left - 1),) + total.shape[1:])

    return (part(mine), swap(part(1 - mine), "clip", bit))


def stack_blocks(v, count):
    return jnp.concatenate(jnp.split(v, count, axis=1), axis=0)


def tied(held, *others):
    flat, tree = jax.tree.flatten((held, others))
    held, others = jax.tree.unflatten(tree, lax.optimization_barrier(flat))
    return (held, *others)


STREAMS = 4


def bit_order(bits, stream):
    order = list(range(bits))
    if stream % 2 == 1 and bits > 1:
        order[0], order[1] = 1, 0
    return order


def finish_kernel(clips, *refs):
    videos = 2
    sends, keeps = refs[:STREAMS], refs[STREAMS : 2 * STREAMS]
    pos = 2 * STREAMS
    big_keep, big_got = refs[pos : pos + 2], refs[pos + 2 : pos + 4]
    gg_m, gg_c, gg_d, gain = refs[pos + 4 : pos + 8]
    pos += 8
    ins = [refs[pos + 6 * b : pos + 6 * (b + 1)] for b in range(videos)]
    pos += 6 * videos
    gx, gains = refs[pos : pos + 2]
    done = refs[pos + 2 : pos + 2 + STREAMS]
    big_done = refs[pos + 2 + STREAMS : pos + 4 + STREAMS]
    pos += 4 + STREAMS
    ds, gs, got0, big_sum, big_other, g_all, g_four = refs[pos : pos + 7]
    pos += 7
    bits = clips.bit_length() - 1
    stage = [refs[pos + 3 * i : pos + 3 * (i + 1)] for i in range(bits)]
    pos += 3 * bits
    last_sum, last_got, sem_s, sem_r, gsem_s, gsem_r, fsem_s, fsem_r = refs[pos:]

    g, c, m = (lax.axis_index(a) for a in ("group", "clip", "micro"))
    barrier = pltpu.get_barrier_semaphore()
    others = [{"clip": lax.rem(c + d, clips)} for d in range(1, clips)]
    others += [{"micro": 1 - m}, {"group": 1 - g}, {"group": 1 - g, "micro": 1 - m}]
    for other in others:
        pl.semaphore_signal(barrier, inc=1, device_id=other, device_id_type=pl.DeviceIdType.MESH)
    pl.semaphore_wait(barrier, len(others))

    def remote(src, dst, number, other):
        return pltpu.make_async_remote_copy(
            src_ref=src,
            dst_ref=dst,
            send_sem=sem_s.at[number],
            recv_sem=sem_r.at[number],
            device_id=other,
            device_id_type=pl.DeviceIdType.MESH,
        )

    copies = {}
    for i in range(STREAMS):
        copies[i] = remote(sends[i], got0.at[i], i, {"micro": 1 - m})
        copies[i].start()
    for i in range(2):
        big_sum[i] = add_up(big_keep[i][0], big_got[i][0]).astype(bf16)
        n = STREAMS * (bits + 2) + i
        copies[n] = remote(big_sum.at[i], big_other.at[i], n, {"group": 1 - g})
        copies[n].start()

    def step_clip(number):
        for i in range(STREAMS):
            n = i + STREAMS * number
            copies[n].wait()
            order = bit_order(bits, i)
            if number == 0:
                keep, got = keeps[i], got0.at[i]
            else:
                keep, got = stage[number - 1][0].at[i], stage[number - 1][2].at[i]
            if number == bits:
                last_sum[i] = add_up(keep[0], got[0]).astype(bf16)
                copies[n + STREAMS] = remote(last_sum.at[i], last_got.at[i], n + STREAMS, {"group": 1 - g})
            else:
                bit = order[number]
                low = sum(1 for b in order[number + 1 :] if b < bit)
                mine = lax.rem(lax.div(c, 2**bit), 2)
                kp, sd, gt = stage[number]
                for t in range(2 ** (bits - number - 1)):
                    base = ((t >> low) << (low + 1)) + (t & (2**low - 1))
                    away = base + (1 - mine) * 2**low
                    home = base + mine * 2**low
                    sd[i, t] = add_up(keep[away], got[away]).astype(bf16)
                    kp[i, t] = add_up(keep[home], got[home]).astype(bf16)
                partner = c + (1 - 2 * mine) * 2**bit
                copies[n + STREAMS] = remote(sd.at[i], gt.at[i], n + STREAMS, {"clip": partner})
            copies[n + STREAMS].start()

    def norm_part(b):
        dna, down, rn, rf, xn, gha = ins[b]
        got = add_up(rn[...], rf[...]).astype(bf16)
        d = 0.25 * (down[...] + mm_tn(tmean_matrix(), got))
        for s in range(4):
            ds[PT * s : PT * (s + 1), :] = d[0:PT]
        total = jnp.zeros((1, D1), f32)
        for i in range(PIECES):
            at = slice(PIECE * i, PIECE * (i + 1))
            unit, inv = norm_stats(xn[at, :].astype(f32))
            dx, dg = norm_back(dna[at, :] + ds[at, :], unit, inv, gain[...])
            total = total + dg
            gs[at, :] = gha[at, :] + dx
        return total

    def order_part(b):
        for i in range(PIECES):
            lo = min(CELL * i // 8 * 8, PT - 112)
            window = jnp.concatenate([gs[PT * s + lo : PT * s + lo + 112, :] for s in range(4)], axis=0).astype(bf16)
            shape = (PIECE, 4 * 112)
            t = rows_of(shape) + PIECE * i
            f = t // (HT * WD)
            rest = t - f * (HT * WD)
            r = rest // WD
            col = rest - r * WD
            r2 = r // 2
            c2 = col // 2
            s = 2 * (r - 2 * r2) + (col - 2 * c2)
            p = f * CELL + r2 * 7 + c2
            pick = jnp.where(s * 112 + p - lo == lanes(shape), 1.0, 0.0).astype(bf16)
            gx[b, PIECE * i : PIECE * (i + 1), :] = mm(pick, window).astype(bf16)

    gg = norm_part(0)
    step_clip(0)
    order_part(0)
    gg = gg + norm_part(1)
    mine_all = g_all.at[c]
    mine_all[...] = jnp.concatenate(
        [gg, gg_m[...], gg_c[...], gg_d[:, :D1], gg_d[:, D1:], jnp.zeros((3, D1), f32)], axis=0
    )
    gcopies = []
    for d in range(1, clips):
        gcopies.append(
            pltpu.make_async_remote_copy(
                src_ref=g_all.at[c],
                dst_ref=g_all.at[c],
                send_sem=gsem_s.at[d - 1],
                recv_sem=gsem_r.at[d - 1],
                device_id={"clip": lax.rem(c + d, clips)},
                device_id_type=pl.DeviceIdType.MESH,
            )
        )
        gcopies[-1].start()
    if bits > 0:
        step_clip(1)
    order_part(1)
    for copy in gcopies:
        copy.wait()
    total = g_all[0]
    for i in range(1, clips):
        total = total + g_all[i]
    place = 2 * g + m
    g_four[place] = total
    fcopies = []
    for i, other in enumerate(others[-3:]):
        fcopies.append(
            pltpu.make_async_remote_copy(
                src_ref=g_four.at[place],
                dst_ref=g_four.at[place],
                send_sem=fsem_s.at[i],
                recv_sem=fsem_r.at[i],
                device_id=other,
                device_id_type=pl.DeviceIdType.MESH,
            )
        )
        fcopies[-1].start()
    for number in range(2, bits + 1):
        step_clip(number)
    for copy in fcopies:
        copy.wait()
    gains[...] = (g_four[0] + g_four[1]) + (g_four[2] + g_four[3])
    first_ = g == 0
    for i in range(2):
        copies[STREAMS * (bits + 2) + i].wait()
        big_done[i][...] = add_up(big_sum[i], big_other[i])
    for i in range(STREAMS):
        copies[i + STREAMS * (bits + 1)].wait()
        done[i][...] = add_up(last_sum[i], last_got[i])


def finish(clips, sends, keeps, big, gg_m, gg_c, gg_d, gain, videos):
    bits = clips.bit_length() - 1
    part = sends[0].shape[1:]
    big_part = big[0][0].shape[1:]
    hbm = pl.BlockSpec(memory_space=pl.ANY)
    ins = [(a, hbm) for a in sends] + [whole(a) for a in keeps]
    ins += [whole(b[0]) for b in big] + [whole(b[1]) for b in big]
    ins += [whole(a) for a in (gg_m, gg_c, gg_d, gain)]
    for dna, down, rn, rf, xn, gha in videos:
        ins += [whole(a) for a in (dna, down, rn, rf)] + [cols_fixed(xn, D1, 0), whole(gha)]
    outs = [whole(shape_of((2, QT, D1), bf16)), whole(shape_of((8, D1), f32))]
    outs += [whole(shape_of(part, f32))] * STREAMS + [whole(shape_of(big_part, f32))] * 2
    scratch = [
        VMEM((QT, D1), f32),
        VMEM((QT, D1), f32),
        VMEM((STREAMS, clips) + part, bf16),
        VMEM((2,) + big_part, bf16),
        VMEM((2,) + big_part, bf16),
        VMEM((clips, 8, D1), f32),
        VMEM((4, 8, D1), f32),
    ]
    for i in range(bits):
        scratch += [VMEM((STREAMS, 2 ** (bits - 1 - i)) + part, bf16)] * 3
    count = STREAMS * (bits + 2) + 2
    dma = pltpu.SemaphoreType.DMA
    scratch += [VMEM((STREAMS,) + part, bf16)] * 2
    scratch += [dma((count,))] * 2 + [dma((clips - 1,))] * 2 + [dma((3,))] * 2
    arrays = [a for a, _ in ins]
    return pl.pallas_call(
        partial(finish_kernel, clips),
        grid=(1,),
        in_specs=[sp for _, sp in ins],
        out_specs=[sp for _, sp in outs],
        out_shape=[o for o, _ in outs],
        scratch_shapes=scratch,
        compiler_params=pltpu.CompilerParams(
            vmem_limit_bytes=58 * 1024 * 1024, collective_id=1, has_side_effects=True
        ),
        name="finish",
    )(*arrays)


def body(inputs, offsets, cotangent, gain_attn1, w_qkv1, w_proj1, gain_mlp1, w_fc1, w_out1,
         gain_attn2, w_qkv2, w_proj2, w_skip, gain_mlp2, w_fc2, w_out2):
    videos = range(inputs.shape[1])
    clip = lax.axis_index("clip")
    g_a1, g_m1, g_a2, g_m2 = (g.reshape(1, -1) for g in (gain_attn1, gain_mlp1, gain_attn2, gain_mlp2))
    row = jnp.arange(KR, dtype=jnp.int32)[:, None]
    place = jnp.where(row < PR + MR, row - PR, row - PR - MR)
    later = (place // CELL >= offsets[0]) & (place < MT)
    hops = jnp.where(row < PR + MR, 1, 2)
    valid = jnp.where(row < PR, row < PT, later & (clip >= hops))
    lane = jnp.arange(LANE, dtype=jnp.int32)[None, :]
    kext = jnp.where(lane == HD + 3, jnp.where(valid, 0.0, -1e30), jnp.where((lane >= HD) & (lane < HD + 3), 1.0, 0.0))
    kext = kext.astype(f32)

    w1p, p1p, w2p, p2p = pad_weights(w_qkv1, w_proj1, w_qkv2, w_proj2)
    xn, kva, mema = zip(*[first(inputs, b, g_a1) for b in videos])
    a = [
        block1(kva[b], shift(mema[b], 1), shift(mema[b], 2), kext, xn[b], w1p, p1p, g_m1, w_fc1, w_out1, g_a2)
        for b in videos
    ]
    ka, Ka, Va, ozq, hm, ubgp, pc, memc = zip(*a)
    c = [block2(pc[b], shift(memc[b], 1), shift(memc[b], 2), kext, w2p, w_skip, p2p) for b in videos]
    kc, Kc, Vc, qec, oc, zc, hc = zip(*c)
    micro, clips = lax.axis_index("micro"), lax.axis_size("clip")
    bits = clips.bit_length() - 1
    output, gh, keep_fc, send_fc, keep_out, send_out, gg_mlp2 = mlp2(micro, clips, hc[0], hc[1], cotangent, g_m2, w_fc2, w_out2)
    big = [(keep_fc, swap(send_fc, "micro")), (keep_out, swap(send_out, "micro"))]
    orders = [bit_order(bits, i) for i in range(2)]

    def big_step(parts, number):
        return [over_clip(p, o[number], o[number:]) for p, o in zip(parts, orders)]

    before, dn2, df2, dpc = None, [], [], []
    for b in videos:
        if b == 1:
            big, gh = tied(big, gh)
            big = big_step(big, 0)
        near, far, d, *before = att2_back(
            b, gh, p2p, qec[b], oc[b], Kc[b], Vc[b], zc[b], pc[b], kc[b], w_skip, w2p, before
        )
        dn2.append(shift(near, -1))
        df2.append(shift(far, -2))
        dpc.append(d)
    grads2 = pack2(micro, clips, before)
    before, gha, gze, gg_c, gg_m = None, [], [], 0.0, 0.0
    for b in videos:
        d = dpc[b]
        if b == 1:
            big, d = tied(big, d)
            big = big_step(big, 1)
        g, z, gc, gm, *before = mlp1_back(
            d, dn2[b], df2[b], g_a2, g_m1, hm[b], ubgp[b], ozq[b], w_out1, w_fc1, p1p, before
        )
        gha.append(g)
        gze.append(z)
        gg_c = gg_c + gc
        gg_m = gg_m + gm
    gw_out1t, gw_fc1, gp1 = before
    before, dn1, df1, down, dna = None, [], [], [], []
    for b in videos:
        z = gze[b]
        if b == 0:
            big, z = tied(big, z)
            for number in range(2, bits):
                big = big_step(big, number)
        near, far, d, dn, *before = att1_back(ozq[b], z, Ka[b], Va[b], xn[b], ka[b], w1p, before)
        dn1.append(shift(near, -1))
        df1.append(shift(far, -2))
        down.append(d)
        dna.append(dn)
    grads1 = pack1(micro, clips, list(before) + [gp1, gw_fc1, gw_out1t])
    keeps = [grads2[0], grads2[2], grads1[0], grads1[2]]
    sends = [grads2[1], grads2[3], grads1[1], grads1[3]]
    ends = [(dna[b], down[b], dn1[b], df1[b], xn[b], gha[b]) for b in videos]
    gx, gains, *sums = finish(clips, sends, keeps, big, gg_m, gg_c, gg_mlp2, g_a1, ends)
    rows = D1 // (2 * clips)
    gw_qkv2, rest2, left, right = (unfold(v, rows) for v in sums[:STREAMS])
    gw_fc2, gw_out2 = sums[STREAMS:]
    shares = (
        jnp.concatenate([left[:, F1:], right[:, F1 : F1 + D1]], axis=1),
        right[:, F1 + D1 :],
        left[:, :F1],
        stack_blocks(right[:, :F1], 4),
        gw_qkv2,
        stack_blocks(rest2[:, : 2 * D2], 2),
        rest2[:, 2 * D2 :],
        gw_fc2,
        stack_blocks(gw_out2, 4),
    )
    gains = (gains[0], gains[1], gains[2], gains[3:5].reshape(-1))
    return (output, gx.reshape(inputs.shape)) + gains + tuple(v.reshape(-1) for v in shares)


def solution(mesh):
    tokens = P("group", "micro", "clip", None, None)
    share = P(("clip", "micro"))
    return jax.shard_map(
        body,
        mesh=mesh,
        in_specs=(tokens, P("group"), tokens) + (P(),) * 13,
        out_specs=(tokens, tokens) + (P(),) * 4 + (share,) * 9,
        check_vma=False,
    )
```

```python
from functools import partial

import jax
import jax.numpy as jnp
from jax import lax
from jax.experimental import pallas as pl
from jax.experimental.pallas import tpu as pltpu
from jax.sharding import PartitionSpec as P

D1 = 384
D2 = 768
F1 = 1536
F2 = 3072
QT = 1568
PT = 392
MT = 196
HD = 96
FR = 8
HT = 14
WD = 14
H1 = 4
H2 = 8
CELL = (HT // 2) * (WD // 2)
LANE = 128
PR = 400
MR = 208
KR = PR + 2 * MR
TILE = 784
STEPS = QT // TILE
PIECE = 224
PIECES = QT // PIECE
W1 = H1 * LANE
W2 = H2 * LANE
epsilon = 1e-06
f32 = jnp.float32
bf16 = jnp.bfloat16
SCALE = HD ** (-0.5)
RATE = SCALE * 1.4426950408889634
VMEM_LIMIT = 60 * 1024 * 1024
VMEM = pltpu.VMEM


def mm(a, b):
    return lax.dot_general(a, b, (((1,), (0,)), ((), ())), preferred_element_type=f32)


def mm_nt(a, b):
    return lax.dot_general(a, b, (((1,), (1,)), ((), ())), preferred_element_type=f32)


def mm_tn(a, b):
    return lax.dot_general(a, b, (((0,), (0,)), ((), ())), preferred_element_type=f32)


def lanes(shape):
    return lax.broadcasted_iota(jnp.int32, shape, len(shape) - 1)


def rows_of(shape):
    return lax.broadcasted_iota(jnp.int32, shape, len(shape) - 2)


def norm_stats(values):
    center = values - jnp.mean(values, axis=-1, keepdims=True)
    inv = lax.rsqrt(jnp.mean(center * center, axis=-1, keepdims=True) + epsilon)
    return (center * inv, inv)


def norm_back(grad, unit, inv, gain):
    du = grad * gain
    dg = jnp.sum(grad * unit, axis=0, keepdims=True)
    dx = inv * (
        du - jnp.mean(du, axis=-1, keepdims=True) - unit * jnp.mean(du * unit, axis=-1, keepdims=True)
    )
    return (dx, dg)


def gelu_both(x):
    z = jnp.abs(x)
    t = 1.0 / (1.0 + 0.23164188 * z)
    e = jnp.exp2(x * x * -0.7213475204444817)
    poly = t * (0.127414796 + t * (-0.142248368 + t * (0.7107068705 + t * (-0.7265760135 + t * 0.5307027145))))
    tail = poly * e
    phi = jnp.where(x >= 0.0, 1.0 - tail, tail)
    return (x * phi, phi + (x * 0.3989422804014327) * e)


def split3(v):
    hi = v.astype(bf16).astype(f32)
    mid = (v - hi).astype(bf16).astype(f32)
    return (hi, mid, v - hi - mid)


def put3(base, v):
    hi, mid, low = split3(v)
    lane = lanes(base.shape)
    return jnp.where(
        lane < HD, base, jnp.where(lane == HD, hi, jnp.where(lane == HD + 1, mid, jnp.where(lane == HD + 2, low, base)))
    )


def tmean_matrix():
    rows = rows_of((MR, PR))
    cols = lanes((MR, PR))
    hit = rows < 0
    for pair in range(FR // 2):
        inside = (rows >= pair * CELL) & (rows < (pair + 1) * CELL)
        shift_by = cols - rows - pair * CELL
        hit = hit | (inside & ((shift_by == 0) | (shift_by == CELL)))
    return jnp.where(hit, 0.5, 0.0).astype(bf16)


def pool_rows(ref):
    total = ref[0:PT, :] + ref[PT : 2 * PT, :] + ref[2 * PT : 3 * PT, :] + ref[3 * PT : 4 * PT, :]
    return jnp.concatenate([0.25 * total, jnp.zeros((PR - PT, total.shape[1]), f32)], axis=0).astype(bf16)


MESH = pl.DeviceIdType.MESH
HBM = pl.BlockSpec(memory_space=pl.ANY)


def add_up(a, b):
    return a.astype(f32) + b.astype(f32)


class Shift:
    def __init__(self, source, steps, begin, end, inner=False):
        self.source = source
        self.ins = [] if isinstance(source, int) else [(source, HBM)]
        shape = (MR, D1)
        self.outs = [] if inner else [whole(shape_of(shape, bf16))]
        self.scratch = [VMEM(shape, bf16)]
        self.peers = [("shift", steps), ("shift", -steps)]
        self.steps, self.inner = steps, inner
        self.sems = 1
        self.events = {begin: [self.start], end: [self.finish]}

    def copy(self, refs, sems, args):
        src = args[self.source] if isinstance(self.source, int) else refs[0]
        return pltpu.make_async_remote_copy(
            src_ref=src, dst_ref=refs[-1], send_sem=sems[0].at[0], recv_sem=sems[1].at[0],
            device_id={"clip": lax.axis_index("clip") + self.steps}, device_id_type=MESH,
        )

    def start(self, refs, sems, args):
        pl.when(exists(self.steps))(lambda: self.copy(refs, sems, args).start())

    def finish(self, refs, sems, args):
        land = refs[-1]
        pl.when(exists(self.steps))(lambda: self.copy(refs, sems, args).wait_send())
        pl.when(exists(-self.steps))(lambda: self.copy(refs, sems, args).wait_recv())

        @pl.when(jnp.logical_not(exists(-self.steps)))
        def _():
            land[...] = jnp.zeros_like(land)

        if not self.inner:
            refs[-2][...] = land[...]


class Chain:
    def __init__(self, parts, order, plan, last):
        keep, other = parts
        self.order, self.plan = order, plan
        first_ = plan[0][0]
        tail = keep.shape[1:]
        self.ins = [(keep, HBM), (other, HBM)]
        self.scratch = [VMEM(keep.shape, bf16), VMEM(other.shape, bf16)]
        count = keep.shape[0]
        for number, _ in plan:
            if number >= 0:
                count //= 2
                self.scratch += [VMEM((count,) + tail, bf16)] * 2
                if number != plan[-1][0]:
                    self.scratch.append(VMEM((count,) + tail, bf16))
        self.only_swap = plan[-1][0] < 0
        final = (shape_of((count,) + tail, bf16), HBM)
        self.outs = [final] if self.only_swap else [whole(final[0]), final]
        self.peers = [("micro", 0) if n < 0 else ("bit", order[n]) for n, _ in plan]
        self.sems = len(plan) + 2
        self.events = {(0, 0): [self.load]}
        for i, (_, step) in enumerate(plan):
            self.events.setdefault((step, 0), []).append(partial(self.advance, i))
        self.events.setdefault((last, 1), []).append(self.finish)
        self.first = first_

    def slots(self, refs):
        keep, other = refs[:2]
        outs = refs[2 : 2 + len(self.outs)]
        held = refs[2 + len(self.outs) :]
        pos, slots = 2, []
        for i, (number, _) in enumerate(self.plan):
            final = i == len(self.plan) - 1
            if number < 0:
                slots.append((held[0], other, outs[-1] if final else held[1]))
                continue
            kept, away = held[pos], held[pos + 1]
            pos += 2
            if final:
                slots.append((kept, away, outs[-1]))
            else:
                slots.append((kept, away, held[pos]))
                pos += 1
        return slots

    def load(self, refs, sems, args):
        n = len(self.plan)
        held = refs[2 + len(self.outs) :]
        if not self.only_swap:
            pltpu.make_async_copy(refs[0], held[0], sems[0].at[n]).start()
        if self.first >= 0:
            pltpu.make_async_copy(refs[1], held[1], sems[0].at[n + 1]).start()

    def loaded(self, refs, sems, other):
        n = len(self.plan)
        held = refs[2 + len(self.outs) :]
        pltpu.make_async_copy(refs[0], held[0], sems[0].at[n]).wait()
        if other:
            pltpu.make_async_copy(refs[1], held[1], sems[0].at[n + 1]).wait()

    def copy(self, i, refs, sems):
        number = self.plan[i][0]
        _, away, land = self.slots(refs)[i]
        to = {"micro": 1 - lax.axis_index("micro")} if number < 0 else {"clip": flipped(self.order[number])}
        return pltpu.make_async_remote_copy(
            src_ref=away, dst_ref=land, send_sem=sems[0].at[i], recv_sem=sems[1].at[i],
            device_id=to, device_id_type=MESH,
        )

    def advance(self, i, refs, sems, args):
        number = self.plan[i][0]
        slots = self.slots(refs)
        if i > 0:
            self.copy(i - 1, refs, sems).wait()
        if number >= 0:
            if i == 0:
                self.loaded(refs, sems, True)
                held = refs[2 + len(self.outs) :]
                keep, got = held[0], held[1]
            else:
                if self.plan[i - 1][0] < 0:
                    self.loaded(refs, sems, False)
                keep, got = slots[i - 1][0], slots[i - 1][2]
            kept, away, _ = slots[i]
            bit = self.order[number]
            low = sum(1 for b in self.order[number + 1 :] if b < bit)
            split_shares(keep, got, kept, away, bit, low, kept.shape[0])
        self.copy(i, refs, sems).start()

    def finish(self, refs, sems, args):
        self.copy(len(self.plan) - 1, refs, sems).wait()
        if not self.only_swap:
            refs[2][...] = self.slots(refs)[-1][0][...]


def side(bit):
    return lax.rem(lax.div(lax.axis_index("clip"), 2**bit), 2)


def flipped(bit):
    return lax.axis_index("clip") + (1 - 2 * side(bit)) * 2**bit


def exists(steps):
    other = lax.axis_index("clip") + steps
    return jnp.logical_and(other >= 0, other < lax.axis_size("clip"))


def split_shares(keep, got, kept, send, bit, low, half):
    mine = side(bit)
    for t in range(half):
        base = ((t >> low) << (low + 1)) + (t & (2**low - 1))
        away = base + (1 - mine) * 2**low
        home = base + mine * 2**low
        send[t] = keep[away] + got[away]
        kept[t] = keep[home] + got[home]


def greet(peers):
    barrier = pltpu.get_barrier_semaphore()
    count = jnp.int32(0)
    for kind, arg in sorted(set(peers)):
        if kind == "shift":
            there = exists(arg)
            to = {"clip": lax.axis_index("clip") + arg}

            @pl.when(there)
            def _():
                pl.semaphore_signal(barrier, inc=1, device_id=to, device_id_type=MESH)

            count = count + there.astype(jnp.int32)
        else:
            to = {"micro": 1 - lax.axis_index("micro")} if kind == "micro" else {"clip": flipped(arg)}
            pl.semaphore_signal(barrier, inc=1, device_id=to, device_id_type=MESH)
            count = count + 1
    pl.semaphore_wait(barrier, count)


def call(kernel, grid, ins, outs, scratch=(), flops=0, name=None, jobs=(), tag=None):
    ins, outs, scratch = list(ins), list(outs), list(scratch)
    n_in, n_out, n_scratch = len(ins), len(outs), len(scratch)
    places = []
    for job in jobs:
        places.append((len(ins), len(outs), len(scratch)))
        ins += job.ins
        outs += job.outs
        scratch += job.scratch + [pltpu.SemaphoreType.DMA((job.sems,))] * 2

    def body_(*refs):
        i, o = len(ins), len(ins) + len(outs)
        args = refs[:n_in] + refs[i : i + n_out] + refs[o : o + n_scratch]
        if not jobs:
            kernel(*args)
            return
        step = pl.program_id(0)
        sets, lands = [], []
        for job, (pi, po, ps) in zip(jobs, places):
            mine = refs[pi : pi + len(job.ins)] + refs[i + po : i + po + len(job.outs)]
            mine += refs[o + ps : o + ps + len(job.scratch)]
            sems = refs[o + ps + len(job.scratch) : o + ps + len(job.scratch) + 2]
            sets.append((job, mine, sems))
            if getattr(job, "inner", False):
                lands.append(mine[-1])
        moments = sorted({when for job in jobs for when in job.events})

        def run(moment):
            for job, mine, sems in sets:
                for event in job.events.get(moment, ()):
                    event(mine, sems, args)

        @pl.when(step == 0)
        def _():
            greet([p for job in jobs for p in job.peers])

        for moment in moments:
            if moment[1] == 0:
                pl.when(step == moment[0])(partial(run, moment))
        kernel(*args, *lands)
        for moment in moments:
            if moment[1] == 1:
                pl.when(step == moment[0])(partial(run, moment))

    arrays = [a for a, _ in ins]
    moved = sum(a.size * a.dtype.itemsize for a in arrays) + sum(t.size * t.dtype.itemsize for t, _ in outs)
    got = pl.pallas_call(
        body_,
        grid=grid,
        in_specs=[t for _, t in ins],
        out_specs=[t for _, t in outs],
        out_shape=[t for t, _ in outs],
        scratch_shapes=scratch,
        compiler_params=pltpu.CompilerParams(
            vmem_limit_bytes=VMEM_LIMIT,
            dimension_semantics=("arbitrary",) * len(grid),
            **(dict(collective_id=tag, has_side_effects=True) if jobs else {}),
        ),
        cost_estimate=pl.CostEstimate(flops=int(flops), bytes_accessed=int(moved), transcendentals=0),
        name=name,
    )(*arrays)
    results = [got[po : po + len(job.outs)] for job, (_, po, _) in zip(jobs, places)]
    return (got[:n_out], results) if jobs else got


def whole(array):
    return (array, pl.BlockSpec(array.shape, lambda i: (0,) * array.ndim))


def per_video(array, n):
    return (array, pl.BlockSpec((None,) + array.shape[1:], lambda i: (i // n, 0, 0)))


def video_rows(array, n, tile, cols=None, at=0):
    return (array, pl.BlockSpec((None, tile, cols or array.shape[2]), lambda i: (i // n, i % n, at)))


def video_cols(array, n, tile, at=0):
    return (array, pl.BlockSpec((None, array.shape[1], tile), lambda i: (i // n, 0, i % n + at)))


def turn_cols(array, n, tile, at=0):
    return (array, pl.BlockSpec((array.shape[0], tile), lambda i: (0, i % n + at)))


def turn_rows(array, n, tile):
    return (array, pl.BlockSpec((tile, array.shape[1]), lambda i: (i % n, 0)))


def rows_tiled(array, tile=TILE):
    return (array, pl.BlockSpec((tile, array.shape[1]), lambda i: (i, 0)))


def cols_tiled(array, tile, first=0):
    return (array, pl.BlockSpec((array.shape[0], tile), lambda i: (0, i + first)))


def shape_of(shape, dtype):
    return jax.ShapeDtypeStruct(shape, dtype)


def pad_kernel(wa, pa, wc, pc, wa_out, pa_out, wc_out, pc_out):
    for src, dst in ((wa, wa_out), (wc, wc_out)):
        blank = jnp.zeros((src.shape[0], LANE - HD), bf16)
        for j in range(src.shape[1] // HD):
            dst[:, LANE * j : LANE * (j + 1)] = jnp.concatenate([src[:, HD * j : HD * (j + 1)], blank], axis=1)
    for src, dst in ((pa, pa_out), (pc, pc_out)):
        blank = jnp.zeros((LANE - HD, src.shape[1]), bf16)
        for j in range(src.shape[0] // HD):
            dst[LANE * j : LANE * j + HD, :] = src[HD * j : HD * (j + 1), :]
            dst[LANE * j + HD : LANE * (j + 1), :] = blank


def source_of(rows_shape, start):
    r = rows_of(rows_shape)
    s = r // 56
    p = r - s * 56 + start
    f = p // CELL
    rest = p - f * CELL
    r2 = rest // 7
    c2 = rest - r2 * 7
    a = s // 2
    return f * (HT * WD) + r2 * (2 * WD) + a * WD + c2 * 2 + (s - 2 * a)


def first_kernel(x, gain, xn, kv, mem, xs):
    for i in range(7):
        lo = 196 * i // 16 * 16
        hi = min(QT, (196 * i + 392 + 15) // 16 * 16)
        shape = (PIECE, hi - lo)
        pick = jnp.where(source_of(shape, 56 * i) == lanes(shape) + lo, 1.0, 0.0).astype(bf16)
        out = mm(pick, x[0, 0, 0, lo:hi, :])
        for s in range(4):
            xs[PT * s + 56 * i : PT * s + 56 * (i + 1), :] = out[56 * s : 56 * (s + 1)]
    for i in range(PIECES):
        at = slice(PIECE * i, PIECE * (i + 1))
        v = xs[at, :]
        unit, _ = norm_stats(v)
        n = (unit * gain[...]).astype(bf16)
        xn[at, :D1] = v.astype(bf16)
        xn[at, D1:] = n
        xs[at, :] = n.astype(f32)
    pooled = pool_rows(xs)
    kv[...] = pooled
    mem[...] = mm(tmean_matrix(), pooled).astype(bf16)


def front_kernel(x, gains, wa, pa, wc, pc, xn, kv, mem, wa_out, pa_out, wc_out, pc_out, xs, mem0):
    step = pl.program_id(0)
    first_kernel(x, gains.at[0:1, :], xn, kv, mem, xs)

    @pl.when(step == 0)
    def _():
        mem0[...] = mem[...]

    @pl.when(step == 1)
    def _():
        pad_kernel(wa, pa, wc, pc, wa_out, pa_out, wc_out, pc_out)


def front(inputs, gains, w_qkv1, w_proj1, w_qkv2, w_proj2):
    ins = [(inputs, pl.BlockSpec((1, 1, 1, QT, D1), lambda i: (0, i, 0, 0, 0))), whole(gains)]
    ins += [whole(w) for w in (w_qkv1, w_proj1, w_qkv2, w_proj2)]
    outs = [per_video(shape_of((2,) + t, bf16), 1) for t in ((QT, 2 * D1), (PR, D1), (MR, D1))]
    outs += [whole(shape_of(t, bf16)) for t in ((D1, 3 * W1), (W1, D1), (D1, 3 * W2), (W2, D2))]
    jobs = [Shift(14, 1, (0, 1), (1, 1)), Shift(14, 2, (0, 1), (1, 1))]
    return call(
        front_kernel, (2,), ins, outs, [VMEM((QT, D1), f32), VMEM((MR, D1), bf16)],
        flops=4 * QT * 416 * D1, name="first_norm", jobs=jobs, tag=1,
    )


def keys_ext(kall, wk, wv, kext, heads, k_out, v_out):
    k = mm(kall, wk)
    v = mm(kall, wv)
    lane = lanes((KR, LANE))
    ones = jnp.where((lane >= HD) & (lane < HD + 3), 1.0, 0.0)
    for h in range(heads):
        at = slice(LANE * h, LANE * (h + 1))
        k_out[:, at] = (k[:, at] + kext).astype(bf16)
        v_out[:, at] = (v[:, at] + ones).astype(bf16)


def head_forward(q, s, v):
    top = jnp.max(s, axis=-1, keepdims=True)
    e = jnp.exp2((s - top) * RATE).astype(bf16)
    mixed = mm(e, v)
    total = mixed[:, HD : HD + 1]
    lse = top + jnp.log(total) * (1.0 / SCALE)
    return (mixed * (1.0 / total), put3(q.astype(f32), -lse).astype(bf16))


def one_lane(shape):
    return jnp.where(lanes(shape) % LANE == HD + 3, 1.0, 0.0)


def remember(kall, step, near0, far0, near1, far1):
    @pl.when(step == 0)
    def _():
        kall[PR : PR + MR, :] = near0[...]
        kall[PR + MR : KR, :] = far0[...]

    @pl.when(step > 0)
    def _():
        kall[PR : PR + MR, :] = near1[...]
        kall[PR + MR : KR, :] = far1[...]


def block1_kernel(
    kv, near0, far0, kext, xn, wq, wk, wv, wp, gains, wfc, wout,
    kall, k_out, v_out, ozq, hm, ubgp, pc, mem, xs, mem0, near1, far1,
):
    step = pl.program_id(0)
    video, turn = step // STEPS, step % STEPS

    @pl.when(turn == 0)
    def _():
        kall[0:PR, :] = kv[...]
        remember(kall, step, near0, far0, near1, far1)
        keys_ext(kall[...], wk[...], wv[...], kext[...], H1, k_out, v_out)

    q = (mm(xn[:, D1:], wq[...]) + one_lane((TILE, W1))).astype(bf16)
    heads = [slice(LANE * h, LANE * (h + 1)) for h in range(H1)]
    scores = [mm_nt(q[:, at], k_out[:, at]) for at in heads]
    for h, at in enumerate(heads):
        o, qx = head_forward(q[:, at], scores[h], v_out[:, at])
        ozq[:, 2 * W1 + LANE * h : 2 * W1 + LANE * (h + 1)] = qx
        ozq[:, at] = o.astype(bf16)
        ozq[:, W1 + LANE * h : W1 + LANE * (h + 1)] = (o + q[:, at].astype(f32)).astype(bf16)
    ha = xn[:, :D1].astype(f32) + mm(ozq[:, W1 : 2 * W1], wp[...])
    hm[:, :D1] = ha
    unit, _ = norm_stats(ha)
    nb = (unit * gains[1:2, :]).astype(bf16)
    part = F1 // 3
    mid = ha
    ahead = mm(nb, wfc[:, :part])
    for j in range(3):
        at = slice(part * j, part * (j + 1))
        inner = ahead
        if j < 2:
            ahead = mm(nb, wfc[:, part * (j + 1) : part * (j + 2)])
        act, slope = gelu_both(inner)
        act = act.astype(bf16)
        ubgp[:, at] = act
        ubgp[:, F1 + part * j : F1 + part * (j + 1)] = slope.astype(bf16)
        mid = mid + mm(act, wout[at, :])
    hm[:, D1:] = mid
    unit, _ = norm_stats(mid)
    xs[pl.ds(pl.multiple_of(turn * TILE, TILE), TILE), :] = (unit * gains[2:3, :]).astype(bf16).astype(f32)

    @pl.when(turn == STEPS - 1)
    def _():
        pooled = pool_rows(xs)
        pc[...] = pooled
        m = mm(tmean_matrix(), pooled).astype(bf16)
        mem[...] = m

        @pl.when(video == 0)
        def _():
            mem0[...] = m


def block1(kv, got0, mem1, kext, xn, w, wp, gains, wfc, wout):
    n = STEPS
    ins = [per_video(kv, n), whole(got0[0]), whole(got0[1]), whole(kext), video_rows(xn, n, TILE)]
    ins += [cols_fixed(w, W1, j) for j in range(3)]
    ins += [whole(wp), whole(gains), whole(wfc), whole(wout)]
    outs = [per_video(shape_of((2, KR, c), bf16), n) for c in (D1, W1, W1)]
    outs += [video_rows(shape_of((2, QT, c), t), n, TILE) for c, t in ((3 * W1, bf16), (2 * D1, f32), (2 * F1, bf16))]
    outs += [per_video(shape_of((2, r, D1), bf16), n) for r in (PR, MR)]
    flops = 4 * QT * (D1 * W1 * 2 + 2 * D1 * F1 + 4 * KR * W1)
    jobs = [Shift(mem1, k, (0, 0), (n, 0), True) for k in (1, 2)]
    jobs += [Shift(21, k, (n - 1, 1), (2 * n - 1, 1)) for k in (1, 2)]
    scratch = [VMEM((QT, D1), f32), VMEM((MR, D1), bf16)]
    return call(block1_kernel, (2 * n,), ins, outs, scratch, flops=flops, name="block1_forward", jobs=jobs, tag=2)


def cols_fixed(array, tile, at):
    return (array, pl.BlockSpec((array.shape[0], tile), lambda i: (0, at)))


PAIR = 2 * LANE


def block2_kernel(pc, near0, far0, kext, wq, wk, wv, wskip, wp, kall, k_out, v_out, qe, o_out, zc, hc, near1, far1):
    step = pl.program_id(0)

    @pl.when(step % (H2 // 2) == 0)
    def _():
        kall[0:PR, :] = pc[...]
        remember(kall, step, near0, far0, near1, far1)
        hc[...] = mm(pc[...], wskip[...])

    keys_ext(kall[...], wk[...], wv[...], kext[...], 2, k_out, v_out)
    q = (mm(pc[...], wq[...]) + one_lane((PR, PAIR))).astype(bf16)
    heads = [slice(LANE * h, LANE * (h + 1)) for h in range(2)]
    scores = [mm_nt(q[:, at], k_out[:, at]) for at in heads]
    for h, at in enumerate(heads):
        o, qx = head_forward(q[:, at], scores[h], v_out[:, at])
        qe[:, at] = qx
        o_out[:, at] = o.astype(bf16)
        zc[:, at] = (o + q[:, at].astype(f32)).astype(bf16)
    hc[...] += mm(zc[...], wp[...])


def block2(pc, got0, mem1, kext, w, wskip, wp):
    n = H2 // 2
    ins = [per_video(pc, n), whole(got0[0]), whole(got0[1]), whole(kext)]
    ins += [turn_cols(w, n, PAIR, j * n) for j in range(3)]
    ins += [whole(wskip), turn_rows(wp, n, PAIR)]
    outs = [per_video(shape_of((2, KR, D1), bf16), n)]
    outs += [video_cols(shape_of((2, r, W2), bf16), n, PAIR) for r in (KR, KR, PR, PR, PR)]
    outs += [per_video(shape_of((2, PR, D2), f32), n)]
    flops = 4 * (PR * D1 * (W2 + D2) + 2 * KR * D1 * W2 + PR * W2 * D2 + 4 * PR * KR * W2)
    jobs = [Shift(mem1, k, (0, 0), (n, 0), True) for k in (1, 2)]
    return call(block2_kernel, (2 * n,), ins, outs, flops=flops, name="block2_attention", jobs=jobs, tag=3)


PART = 768


def pick_share(micro, even, odd):
    first_ = micro == 0
    return (jnp.where(first_, even, odd).astype(bf16), jnp.where(first_, odd, even).astype(bf16))


def mlp2_kernel(micro, hc, cot, gain, wfc, wout, out, gh, keep_fc, send_fc, keep_out, send_out, gg, hs, nd, ndt, gm, acc, dn):
    step = pl.program_id(0)

    @pl.when(step == 0)
    def _():
        blank = jnp.zeros((PR - PT, D2), f32)
        for b in range(2):
            at = slice(PR * b, PR * (b + 1))
            v = hc[b]
            hs[at, :] = v
            unit, _ = norm_stats(v)
            nd[at, :] = (unit * gain[...]).astype(bf16)
            g = cot[0, b, 0].astype(f32)
            gm[at, :] = jnp.concatenate([g, blank], axis=0).astype(bf16)
        ndt[...] = nd[...].T

    act, slope = gelu_both(mm(nd[...], wfc[...]))
    act = act.astype(bf16)
    gi = (slope * mm_nt(gm[...], wout[...])).astype(bf16)
    m = micro[0]
    gw = mm_tn(act, gm[...])
    rows = keep_fc.shape[1]
    for i in range(keep_out.shape[0]):
        keep, send = pick_share(m, gw[8 * rows * i : 8 * rows * i + 4 * rows], gw[8 * rows * i + 4 * rows : 8 * rows * (i + 1)])
        for a in range(4):
            keep_out[i, :, D2 * a : D2 * (a + 1)] = keep[rows * a : rows * (a + 1)]
            send_out[i, :, D2 * a : D2 * (a + 1)] = send[rows * a : rows * (a + 1)]
    gw = mm(ndt[...], gi)
    for i in range(keep_fc.shape[0]):
        keep, send = pick_share(m, gw[2 * rows * i : 2 * rows * i + rows], gw[2 * rows * i + rows : 2 * rows * (i + 1)])
        keep_fc[i] = keep
        send_fc[i] = send
    o = mm(act, wout[...])
    d = mm_nt(gi, wfc[...])

    @pl.when(step == 0)
    def _():
        acc[...] = o
        dn[...] = d

    @pl.when(step > 0)
    def _():
        acc[...] += o
        dn[...] += d

    @pl.when(step == F2 // PART - 1)
    def _():
        v = hs[...]
        y = v + acc[...]
        unit, inv = norm_stats(v)
        dx, dg = norm_back(dn[...], unit, inv, gain[...])
        gg[...] = dg
        g = (gm[...].astype(f32) + dx).astype(bf16)
        for b in range(2):
            out[0, b, 0] = y[PR * b : PR * b + PT].astype(bf16)
            gh[b] = g[PR * b : PR * (b + 1)]


def scalar(value):
    return (value.astype(jnp.int32).reshape(1), pl.BlockSpec(memory_space=pltpu.SMEM))


def mlp2(micro, clips, hc, cot, gain, wfc, wout):
    rows = D2 // (2 * clips)
    steps = F2 // PART
    ins = [scalar(micro), whole(hc), whole(cot), whole(gain), cols_tiled(wfc, PART), rows_tiled(wout, PART)]
    share = shape_of((clips, rows, F2), bf16)
    fc_spec = (share, pl.BlockSpec((clips, rows, PART), lambda i: (0, 0, i)))
    out_spec = (share, pl.BlockSpec((clips // steps, rows, F2), lambda i: (i, 0, 0)))
    outs = [
        whole(shape_of(cot.shape, bf16)),
        whole(shape_of((2, PR, D2), bf16)),
        fc_spec,
        fc_spec,
        out_spec,
        out_spec,
        whole(shape_of((1, D2), f32)),
    ]
    n = 2 * PR
    scratch = [
        VMEM((n, D2), f32),
        VMEM((n, D2), bf16),
        VMEM((D2, n), bf16),
        VMEM((n, D2), bf16),
        VMEM((n, D2), f32),
        VMEM((n, D2), f32),
    ]
    return call(mlp2_kernel, (steps,), ins, outs, scratch, flops=12 * n * D2 * F2, name="block2_mlp")


def head_backward(q, g, k, v, tiles):
    kt = k.T
    dk = jnp.zeros((KR, LANE), f32)
    dv = jnp.zeros((KR, LANE), f32)
    dqs = []
    for at in tiles:
        p = jnp.exp2(mm_nt(k, q[at]) * RATE)
        ds = (p * mm_nt(v, g[at])).astype(bf16)
        dv = dv + mm(p.astype(bf16), g[at])
        dk = dk + mm(ds, q[at])
        dqs.append((mm(kt, ds) * SCALE).T)
    return (dqs, dk * SCALE, dv)


def grad_ext(gz, o):
    delta = jnp.sum(jnp.where(lanes(gz.shape) < HD, gz.astype(f32) * o.astype(f32), 0.0), axis=-1, keepdims=True)
    return put3(gz.astype(f32), -delta).astype(bf16)


def add_columns(ref, step, value, again):
    at = pl.ds(pl.multiple_of(step * PAIR, PAIR), PAIR)

    @pl.when(again)
    def _():
        ref[:, at] += value

    @pl.when(jnp.logical_not(again))
    def _():
        ref[:, at] = value


def att2_back_kernel(
    micro, gh, wp, qe, o, k, v, zc, pc, kall, wskip, wq, wk, wv,
    dnear, dfar, dpc, keep_a, send_a, keep_b, send_b,
    gq_w, gk_w, gv_w, gp_w, gs_w, dkv, qkv, dnear0, dfar0,
):
    step = pl.program_id(0)
    turn = step % (H2 // 2)
    again = step >= H2 // 2

    @pl.when(turn == 0)
    def _():
        dpc[...] = mm_nt(gh[...], wskip[...])
        skip = mm_tn(pc[...], gh[...])
        gs_w[...] = jnp.where(again, gs_w[...], 0.0) + skip
        dkv[...] = jnp.zeros_like(dkv)

    gz = mm_nt(gh[...], wp[...]).astype(bf16)
    gp = mm_tn(zc[...], gh[...])
    at_rows = pl.ds(pl.multiple_of(turn * PAIR, PAIR), PAIR)

    @pl.when(again)
    def _():
        gp_w[at_rows, :] += gp

    @pl.when(jnp.logical_not(again))
    def _():
        gp_w[at_rows, :] = gp

    heads = [slice(LANE * h, LANE * (h + 1)) for h in range(2)]
    gq, dk, dv = [], [], []
    for at in heads:
        g = grad_ext(gz[:, at], o[:, at])
        dqs, dkh, dvh = head_backward(qe[:, at], g, k[:, at], v[:, at], [slice(0, PR)])
        gq.append((gz[:, at].astype(f32) + dqs[0]).astype(bf16))
        dk.append(dkh.astype(bf16))
        dv.append(dvh.astype(bf16))
    gq = jnp.concatenate(gq, axis=1)
    dk = jnp.concatenate(dk, axis=1)
    dv = jnp.concatenate(dv, axis=1)
    dpc[...] += mm_nt(gq, wq[...])
    dkv[...] += mm_nt(dk, wk[...]) + mm_nt(dv, wv[...])
    add_columns(gq_w, turn, mm_tn(pc[...], gq), again)
    add_columns(gk_w, turn, mm_tn(kall[...], dk), again)
    add_columns(gv_w, turn, mm_tn(kall[...], dv), again)

    @pl.when(turn == H2 // 2 - 1)
    def _():
        dpc[...] += dkv[0:PR, :]

    @pl.when(step == H2 // 2 - 1)
    def _():
        dnear0[...] = dkv[PR : PR + MR, :].astype(bf16)
        dfar0[...] = dkv[PR + MR : KR, :].astype(bf16)

    @pl.when(step == H2 - 1)
    def _():
        dnear[...] = dkv[PR : PR + MR, :].astype(bf16)
        dfar[...] = dkv[PR + MR : KR, :].astype(bf16)
        pack2(micro, gq_w, gk_w, gv_w, gp_w, gs_w, keep_a, send_a, keep_b, send_b, qkv)


def att2_back(gh, wp, qe, o, k, v, zc, pc, kall, wskip, w, micro, clips, jobs):
    n = H2 // 2
    ins = [scalar(micro), per_video(gh, n), turn_rows(wp, n, PAIR)]
    ins += [video_cols(a, n, PAIR) for a in (qe, o, k, v, zc)]
    ins += [per_video(pc, n), per_video(kall, n), whole(wskip)]
    ins += [turn_cols(w, n, PAIR, j * n) for j in range(3)]
    outs = [whole(shape_of((MR, D1), bf16))] * 2 + [per_video(shape_of((2, PR, D1), f32), n)]
    outs += [whole(shape_of((clips,) + folded(D1 // (2 * clips), 3 * D2), bf16))] * 4
    scratch = [VMEM((D1, W2), f32)] * 3 + [VMEM((W2, D2), f32), VMEM((D1, D2), f32)]
    scratch += [VMEM((KR, D1), f32), VMEM((D1, 3 * D2), f32)] + [VMEM((MR, D1), bf16)] * 2
    flops = 4 * (10 * PR * KR * W2 + 4 * PR * D1 * W2 + 4 * KR * D1 * W2 + 4 * PR * W2 * D2)
    jobs = [Shift(28, -1, (n - 1, 1), (2 * n - 1, 1)), Shift(29, -2, (n - 1, 1), (2 * n - 1, 1))] + jobs
    return call(att2_back_kernel, (2 * n,), ins, outs, scratch, flops=flops, name="block2_attention_back", jobs=jobs, tag=4)


def mlp1_back_kernel(
    micro, dpc, rn0, rf0, gains, hm, ubgp, oz, wout, wfc, wp,
    gha, gze, gg_c, gg_m, gw_p, keep_a, send_a, keep_b, send_b,
    gw_out, gw_fc, ds, flip, rn1, rf1,
):
    step = pl.program_id(0)
    turn = step % PIECES

    @pl.when(step == 0)
    def _():
        for ref in (gg_c, gg_m, gw_out, gw_fc, gw_p):
            ref[...] = jnp.zeros_like(ref)

    def spread(rn, rf):
        got = add_up(rn[...], rf[...]).astype(bf16)
        d = 0.25 * (dpc[...] + mm_tn(tmean_matrix(), got))
        for s in range(4):
            ds[PT * s : PT * (s + 1), :] = d[0:PT]

    pl.when(step == 0)(lambda: spread(rn0, rf0))
    pl.when(step == PIECES)(lambda: spread(rn1, rf1))

    unit, inv = norm_stats(hm[:, D1:])
    dnc = ds[pl.ds(pl.multiple_of(turn * PIECE, PIECE), PIECE), :]
    gmid, dg = norm_back(dnc, unit, inv, gains[2:3, :])
    gg_c[...] += dg
    gm = gmid.astype(bf16)
    gmt = gm.T
    unit_b, inv_b = norm_stats(hm[:, :D1])
    nbt = (unit_b * gains[1:2, :]).astype(bf16).T
    part = F1 // 3
    dn = jnp.zeros((PIECE, D1), f32)
    ahead = mm_nt(gm, wout[:part, :])
    for j in range(3):
        at = slice(part * j, part * (j + 1))
        inner = ahead
        if j < 2:
            ahead = mm_nt(gm, wout[part * (j + 1) : part * (j + 2), :])
        slope = ubgp[:, F1 + part * j : F1 + part * (j + 1)].astype(f32)
        gi = (slope * inner).astype(bf16)
        gw_out[:, at] += mm(gmt, ubgp[:, at])
        gw_fc[:, at] += mm(nbt, gi)
        dn = dn + mm_nt(gi, wfc[:, at])
    dx, dg = norm_back(dn, unit_b, inv_b, gains[1:2, :])
    gg_m[...] += dg
    g = gmid + dx
    gha[...] = g
    gh = g.astype(bf16)
    gw_p[...] += mm_tn(oz[:, W1:], gh)
    gz = mm_nt(gh, wp[...]).astype(bf16)
    for h in range(H1):
        at = slice(LANE * h, LANE * (h + 1))
        gze[:, at] = grad_ext(gz[:, at], oz[:, at])

    @pl.when(step == 2 * PIECES - 1)
    def _():
        pack_mlp1(micro, gw_fc, gw_out, keep_a, send_a, keep_b, send_b, flip)


def mlp1_back(dpc, got0, near1, far1, gains, hm, ubgp, ozq, wout, wfc, wp, micro, clips, jobs):
    n = PIECES
    ins = [scalar(micro), per_video(dpc, n), whole(got0[0]), whole(got0[1]), whole(gains)]
    ins += [video_rows(hm, n, PIECE), video_rows(ubgp, n, PIECE), video_rows(ozq, n, PIECE, 2 * W1)]
    ins += [whole(wout), whole(wfc), whole(wp)]
    outs = [video_rows(shape_of((2, QT, D1), f32), n, PIECE), video_rows(shape_of((2, QT, W1), bf16), n, PIECE)]
    outs += [whole(shape_of((1, D1), f32))] * 2 + [whole(shape_of((W1, D1), f32))]
    outs += [whole(shape_of((clips,) + folded(D1 // (2 * clips), F1), bf16))] * 4
    scratch = [VMEM((D1, F1), f32)] * 2 + [VMEM((QT, D1), f32), VMEM((F1, D1), f32)]
    flops = 4 * QT * (4 * D1 * F1 + 2 * D1 * W1)
    jobs = [Shift(near1, -1, (0, 0), (n, 0), True), Shift(far1, -2, (0, 0), (n, 0), True)] + jobs
    return call(mlp1_back_kernel, (2 * n,), ins, outs, scratch, flops=flops, name="block1_mlp_back", jobs=jobs, tag=5)


QUERY_TILES = [slice(0, 512), slice(512, 1024), slice(1024, QT)]


def att1_back_kernel(
    micro, qe, gze, k, v, xn, kall, wq, wk, wv, gp,
    dnear, dfar, down, dna, keep_a, send_a, keep_b, send_b,
    gq_w, gk_w, gv_w, dkv, nat, qkv, dnear0, dfar0,
):
    step = pl.program_id(0)
    turn = step % (H1 // 2)
    again = step >= H1 // 2

    @pl.when(turn == 0)
    def _():
        dkv[...] = jnp.zeros_like(dkv)
        dna[...] = jnp.zeros_like(dna)
        nat[...] = xn[...].T

    gq, dk, dv = [[] for _ in QUERY_TILES], [], []
    for h in range(2):
        at = slice(LANE * h, LANE * (h + 1))
        g = gze[:, at]
        dqs, dkh, dvh = head_backward(qe[:, at], g, k[:, at], v[:, at], QUERY_TILES)
        for i, rows in enumerate(QUERY_TILES):
            gq[i].append((g[rows].astype(f32) + dqs[i]).astype(bf16))
        dk.append(dkh.astype(bf16))
        dv.append(dvh.astype(bf16))
    gq = jnp.concatenate([jnp.concatenate(t, axis=1) for t in gq], axis=0)
    lane = lanes((1, PAIR)) % LANE
    gq = jnp.where(lane < HD, gq, jnp.zeros_like(gq))
    dk = jnp.concatenate(dk, axis=1)
    dv = jnp.concatenate(dv, axis=1)
    dna[...] += mm_nt(gq, wq[...])
    dkv[...] += mm_nt(dk, wk[...]) + mm_nt(dv, wv[...])
    add_columns(gq_w, turn, mm(nat[...], gq), again)
    add_columns(gk_w, turn, mm_tn(kall[...], dk), again)
    add_columns(gv_w, turn, mm_tn(kall[...], dv), again)

    @pl.when(turn == H1 // 2 - 1)
    def _():
        down[...] = dkv[0:PR, :]

    @pl.when(step == H1 // 2 - 1)
    def _():
        dnear0[...] = dkv[PR : PR + MR, :].astype(bf16)
        dfar0[...] = dkv[PR + MR : KR, :].astype(bf16)

    @pl.when(step == H1 - 1)
    def _():
        dnear[...] = dkv[PR : PR + MR, :].astype(bf16)
        dfar[...] = dkv[PR + MR : KR, :].astype(bf16)
        pack_att1(micro, gq_w, gk_w, gv_w, gp, keep_a, send_a, keep_b, send_b, qkv)


def att1_back(ozq, gze, k, v, xn, kall, w, gp, micro, clips, jobs):
    n = H1 // 2
    ins = [scalar(micro), video_cols(ozq, n, PAIR, 2 * n)] + [video_cols(a, n, PAIR) for a in (gze, k, v)]
    ins += [(xn, pl.BlockSpec((None, QT, D1), lambda i: (i // n, 0, 1))), per_video(kall, n)]
    ins += [turn_cols(w, n, PAIR, j * n) for j in range(3)] + [whole(gp)]
    outs = [whole(shape_of((MR, D1), bf16))] * 2
    outs += [per_video(shape_of((2, PR, D1), f32), n), per_video(shape_of((2, QT, D1), f32), n)]
    outs += [whole(shape_of((clips,) + folded(D1 // (2 * clips), 2 * D1), bf16))] * 4
    scratch = [VMEM((D1, W1), f32)] * 3
    scratch += [VMEM((KR, D1), f32), VMEM((D1, QT), bf16), VMEM((D1, 4 * D1), f32)] + [VMEM((MR, D1), bf16)] * 2
    flops = 4 * (10 * QT * KR * W1 + 2 * QT * D1 * W1 + 4 * KR * D1 * W1)
    jobs = [Shift(25, -1, (n - 1, 1), (2 * n - 1, 1)), Shift(26, -2, (n - 1, 1), (2 * n - 1, 1))] + jobs
    return call(att1_back_kernel, (2 * n,), ins, outs, scratch, flops=flops, name="block1_attention_back", jobs=jobs, tag=6)


def strip(grad):
    return jnp.concatenate([grad[:, LANE * h : LANE * h + HD] for h in range(grad.shape[1] // LANE)], axis=1)


def fold(v):
    rows, cols = v.shape
    if rows != 24:
        return v
    rest = jnp.concatenate([v[16:, : cols // 2], v[16:, cols // 2 :]], axis=0)
    return jnp.concatenate([v[:16], rest], axis=1)


def unfold(v, rows):
    if rows != 24:
        return v
    cols = v.shape[1] * 2 // 3
    rest = jnp.concatenate([v[:8, cols:], v[8:, cols:]], axis=1)
    return jnp.concatenate([v[:, :cols], rest], axis=0)


def folded(rows, cols):
    return (16, cols * 3 // 2) if rows == 24 else (rows, cols)


def store_shares(micro, clips, pieces):
    for i in range(clips):
        for keep, send, piece in pieces:
            k, t = pick_share(micro, fold(piece(2 * i)), fold(piece(2 * i + 1)))
            keep[i] = k
            send[i] = t


def pack2(micro, gq, gk, gv, gp, gs, keep_a, send_a, keep_b, send_b, qkv):
    for j, g in enumerate((gq, gk, gv)):
        qkv[:, D2 * j : D2 * (j + 1)] = strip(g[...])
    clips, rows = keep_a.shape[0], D1 // (2 * keep_a.shape[0])

    def proj(share, a):
        lo = rows * (2 * share + a)
        h = lo // HD
        start = lo + (LANE - HD) * h
        if (lo + rows - 1) // HD == h:
            return gp[start : start + rows, :]
        cut = HD * (h + 1) - lo
        return jnp.concatenate([gp[start : start + cut, :], gp[LANE * (h + 1) : LANE * (h + 1) + rows - cut, :]], axis=0)

    def piece_a(n):
        return qkv[rows * n : rows * (n + 1), :]

    def piece_b(n):
        return jnp.concatenate([proj(n, 0), proj(n, 1), gs[rows * n : rows * (n + 1), :]], axis=1)

    store_shares(micro[0], clips, ((keep_a, send_a, piece_a), (keep_b, send_b, piece_b)))


def pack_mlp1(micro, gfc, gout, keep_a, send_a, keep_b, send_b, flip):
    flip[...] = gout[...].T
    clips, rows = keep_a.shape[0], D1 // (2 * keep_a.shape[0])

    def piece_a(n):
        return gfc[rows * n : rows * (n + 1), :]

    def piece_b(n):
        return jnp.concatenate([flip[rows * (4 * n + a) : rows * (4 * n + a + 1), :] for a in range(4)], axis=1)

    store_shares(micro[0], clips, ((keep_a, send_a, piece_a), (keep_b, send_b, piece_b)))


def pack_att1(micro, gq, gk, gv, gp, keep_a, send_a, keep_b, send_b, qkv):
    for j, g in enumerate((gq, gk, gv)):
        qkv[:, D1 * j : D1 * (j + 1)] = strip(g[...])
    for h in range(H1):
        qkv[HD * h : HD * (h + 1), 3 * D1 :] = gp[LANE * h : LANE * h + HD, :]
    clips, rows = keep_a.shape[0], D1 // (2 * keep_a.shape[0])
    half = 2 * D1

    def piece_a(n):
        return qkv[rows * n : rows * (n + 1), :half]

    def piece_b(n):
        return qkv[rows * n : rows * (n + 1), half:]

    store_shares(micro[0], clips, ((keep_a, send_a, piece_a), (keep_b, send_b, piece_b)))


def stack_blocks(v, count):
    return jnp.concatenate(jnp.split(v, count, axis=1), axis=0)


def bit_order(bits, stream):
    order = list(range(bits))
    if stream % 2 == 1 and bits > 1:
        order[0], order[1] = 1, 0
    return order


def finish_kernel(clips, starts, *refs):
    count = len(starts)
    keeps, gots = refs[:count], refs[count : 2 * count]
    pos = 2 * count
    gg_m, gg_c, gg_d, gain, dnear, dfar, dna, down, xn, gha, rn0, rf0 = refs[pos : pos + 12]
    pos += 12
    gx, gains = refs[pos : pos + 2]
    done = refs[pos + 2 : pos + 2 + count]
    pos += 2 + count
    ds, gs, rn1, rf1, g_all, g_four = refs[pos : pos + 6]
    pos += 6
    bits = clips.bit_length() - 1
    land, stage, ends = {}, {}, {}
    for i in range(count):
        if starts[i] < 0:
            land[i] = refs[pos]
            pos += 1
        for k in range(max(starts[i], 0), bits):
            stage[i, k] = refs[pos : pos + 3]
            pos += 3
        ends[i] = refs[pos : pos + 2]
        pos += 2
    sem_s, sem_r, gsem_s, gsem_r, fsem_s, fsem_r, msem_s, msem_r = refs[pos:]

    g, c, m = (lax.axis_index(a) for a in ("group", "clip", "micro"))
    barrier = pltpu.get_barrier_semaphore()
    others = [{"clip": lax.rem(c + d, clips)} for d in range(1, clips)]
    others += [{"micro": 1 - m}, {"group": 1 - g}, {"group": 1 - g, "micro": 1 - m}]
    for other in others:
        pl.semaphore_signal(barrier, inc=1, device_id=other, device_id_type=MESH)
    pl.semaphore_wait(barrier, len(others))

    shifts = [(dnear, rn1, -1), (dfar, rf1, -2)]

    def memory_copy(i):
        src, dst, steps = shifts[i]
        return pltpu.make_async_remote_copy(
            src_ref=src, dst_ref=dst, send_sem=msem_s.at[i], recv_sem=msem_r.at[i],
            device_id={"clip": c + steps}, device_id_type=MESH,
        )

    for i in range(2):
        pl.when(exists(shifts[i][2]))(lambda i=i: memory_copy(i).start())

    copies = {}

    def send(i, number, src, dst, other):
        n = i * (bits + 2) + number + 1
        copies[i, number] = pltpu.make_async_remote_copy(
            src_ref=src, dst_ref=dst, send_sem=sem_s.at[n], recv_sem=sem_r.at[n],
            device_id=other, device_id_type=MESH,
        )
        copies[i, number].start()

    def advance(i, number):
        if number < 0:
            send(i, number, gots[i], land[i], {"micro": 1 - m})
            return
        if (i, number - 1) in copies:
            copies[i, number - 1].wait()
        if number == starts[i]:
            keep, got = keeps[i], gots[i]
        elif number == 0:
            keep, got = keeps[i], land[i]
        else:
            keep, got = stage[i, number - 1][0], stage[i, number - 1][2]
        if number == bits:
            ends[i][0][...] = add_up(keep[0], got[0]).astype(bf16)
            send(i, number, ends[i][0], ends[i][1], {"group": 1 - g})
        else:
            order = bit_order(bits, i)
            bit = order[number]
            low = sum(1 for b in order[number + 1 :] if b < bit)
            kept, away, there = stage[i, number]
            split_shares(keep, got, kept, away, bit, low, 2 ** (bits - number - 1))
            send(i, number, away, there, {"clip": flipped(bit)})

    at_stage = list(starts)

    def advance_all():
        for i in range(count):
            if at_stage[i] <= bits:
                advance(i, at_stage[i])
                at_stage[i] += 1

    def norm_part(b, rn, rf):
        got = add_up(rn, rf).astype(bf16)
        d = 0.25 * (down[b] + mm_tn(tmean_matrix(), got))
        for s in range(4):
            ds[PT * s : PT * (s + 1), :] = d[0:PT]
        total = jnp.zeros((1, D1), f32)
        for i in range(PIECES):
            at = slice(PIECE * i, PIECE * (i + 1))
            unit, inv = norm_stats(xn[b, at, :].astype(f32))
            dx, dg = norm_back(dna[b, at, :] + ds[at, :], unit, inv, gain[0:1, :])
            total = total + dg
            gs[at, :] = gha[b, at, :] + dx
        return total

    def order_part(b):
        for i in range(PIECES):
            lo = min(CELL * i // 8 * 8, PT - 112)
            window = jnp.concatenate([gs[PT * s + lo : PT * s + lo + 112, :] for s in range(4)], axis=0).astype(bf16)
            shape = (PIECE, 4 * 112)
            t = rows_of(shape) + PIECE * i
            f = t // (HT * WD)
            rest = t - f * (HT * WD)
            r = rest // WD
            col = rest - r * WD
            r2 = r // 2
            c2 = col // 2
            s = 2 * (r - 2 * r2) + (col - 2 * c2)
            p = f * CELL + r2 * 7 + c2
            pick = jnp.where(s * 112 + p - lo == lanes(shape), 1.0, 0.0).astype(bf16)
            gx[b, PIECE * i : PIECE * (i + 1), :] = mm(pick, window).astype(bf16)

    advance_all()
    gg = norm_part(0, rn0[...], rf0[...])
    advance_all()
    order_part(0)
    advance_all()
    for i in range(2):
        _, dst, steps = shifts[i]
        pl.when(exists(steps))(lambda i=i: memory_copy(i).wait_send())

        @pl.when(exists(-steps))
        def _():
            memory_copy(i).wait_recv()

        @pl.when(jnp.logical_not(exists(-steps)))
        def _():
            dst[...] = jnp.zeros_like(dst)

    gg = gg + norm_part(1, rn1[...], rf1[...])
    advance_all()
    g_all[c] = jnp.concatenate(
        [gg, gg_m[...], gg_c[...], gg_d[:, :D1], gg_d[:, D1:], jnp.zeros((3, D1), f32)], axis=0
    )
    gcopies = []
    for d in range(1, clips):
        gcopies.append(
            pltpu.make_async_remote_copy(
                src_ref=g_all.at[c], dst_ref=g_all.at[c], send_sem=gsem_s.at[d - 1], recv_sem=gsem_r.at[d - 1],
                device_id={"clip": lax.rem(c + d, clips)}, device_id_type=MESH,
            )
        )
        gcopies[-1].start()
    order_part(1)
    advance_all()
    for copy in gcopies:
        copy.wait()
    total = g_all[0]
    for i in range(1, clips):
        total = total + g_all[i]
    place = 2 * g + m
    g_four[place] = total
    fcopies = []
    for i, other in enumerate(others[-3:]):
        fcopies.append(
            pltpu.make_async_remote_copy(
                src_ref=g_four.at[place], dst_ref=g_four.at[place], send_sem=fsem_s.at[i], recv_sem=fsem_r.at[i],
                device_id=other, device_id_type=MESH,
            )
        )
        fcopies[-1].start()
    for _ in range(bits + 2):
        advance_all()
    for copy in fcopies:
        copy.wait()
    gains[...] = (g_four[0] + g_four[1]) + (g_four[2] + g_four[3])
    for i in range(count):
        copies[i, bits].wait()
        done[i][...] = add_up(*(ref[...] for ref in ends[i]))


def finish(clips, streams, starts, gg_m, gg_c, gg_d, gain, dnear, dfar, dna, down, xn, gha, got0, tag):
    bits = clips.bit_length() - 1
    count = len(streams)
    ins = [whole(k) for k, _ in streams] + [(t, HBM) if n < 0 else whole(t) for (_, t), n in zip(streams, starts)]
    ins += [whole(a) for a in (gg_m, gg_c, gg_d, gain)] + [(dnear, HBM), (dfar, HBM)]
    ins += [whole(dna), whole(down), (xn, pl.BlockSpec((2, QT, D1), lambda i: (0, 0, 0))), whole(gha)]
    ins += [whole(a) for a in got0]
    parts = [k.shape[1:] for k, _ in streams]
    outs = [whole(shape_of((2, QT, D1), bf16)), whole(shape_of((8, D1), f32))]
    outs += [whole(shape_of(p, f32)) for p in parts]
    scratch = [VMEM((QT, D1), f32)] * 2 + [VMEM((MR, D1), bf16)] * 2
    scratch += [VMEM((clips, 8, D1), f32), VMEM((4, 8, D1), f32)]
    for p, n in zip(parts, starts):
        if n < 0:
            scratch.append(VMEM((clips,) + p, bf16))
        for k in range(max(n, 0), bits):
            scratch += [VMEM((2 ** (bits - 1 - k),) + p, bf16)] * 3
        scratch += [VMEM(p, bf16)] * 2
    dma = pltpu.SemaphoreType.DMA
    for n in (count * (bits + 2), clips - 1, 3, 2):
        scratch += [dma((n,))] * 2
    return pl.pallas_call(
        partial(finish_kernel, clips, starts),
        grid=(1,),
        in_specs=[t for _, t in ins],
        out_specs=[t for _, t in outs],
        out_shape=[t for t, _ in outs],
        scratch_shapes=scratch,
        compiler_params=pltpu.CompilerParams(
            vmem_limit_bytes=VMEM_LIMIT, collective_id=tag, has_side_effects=True
        ),
        name="finish",
    )(*[a for a, _ in ins])


def body(inputs, offsets, cotangent, gain_attn1, w_qkv1, w_proj1, gain_mlp1, w_fc1, w_out1,
         gain_attn2, w_qkv2, w_proj2, w_skip, gain_mlp2, w_fc2, w_out2):
    clip = lax.axis_index("clip")
    gains_in = jnp.stack([gain_attn1, gain_mlp1, gain_attn2])
    g_m2 = gain_mlp2.reshape(1, -1)
    row = jnp.arange(KR, dtype=jnp.int32)[:, None]
    place = jnp.where(row < PR + MR, row - PR, row - PR - MR)
    later = (place // CELL >= offsets[0]) & (place < MT)
    hops = jnp.where(row < PR + MR, 1, 2)
    valid = jnp.where(row < PR, row < PT, later & (clip >= hops))
    lane = jnp.arange(LANE, dtype=jnp.int32)[None, :]
    kext = jnp.where(lane == HD + 3, jnp.where(valid, 0.0, -1e30), jnp.where((lane >= HD) & (lane < HD + 3), 1.0, 0.0))
    kext = kext.astype(f32)

    micro, clips = lax.axis_index("micro"), lax.axis_size("clip")
    bits = clips.bit_length() - 1

    def flat(results):
        return [r[0] for r in results]

    (xn, kva, mem, w1p, p1p, w2p, p2p), got = front(inputs, gains_in, w_qkv1, w_proj1, w_qkv2, w_proj2)
    (ka, Ka, Va, ozq, hm, ubgp, pc, mem), got = block1(kva, flat(got), mem[1], kext, xn, w1p, p1p, gains_in, w_fc1, w_out1)
    (kc, Kc, Vc, qec, oc, zc, hc), _ = block2(pc, flat(got[2:]), mem[1], kext, w2p, w_skip, p2p)
    output, gh, keep_fc, send_fc, keep_out, send_out, gg_mlp2 = mlp2(micro, clips, hc, cotangent, g_m2, w_fc2, w_out2)

    orders = [bit_order(bits, i) for i in range(2)]

    def chains(parts, plan, last):
        return [Chain(p, o, plan, last) for p, o in zip(parts, orders)]

    n = H2 // 2
    jobs = chains([(keep_fc, send_fc), (keep_out, send_out)], [(-1, 0), (0, 3)], 2 * n - 1)
    (near1, far1, dpc, *packed), got = att2_back(gh, p2p, qec, oc, Kc, Vc, zc, pc, kc, w_skip, w2p, micro, clips, jobs)
    got0, big = flat(got[:2]), got[2:]
    att2 = [(packed[0], packed[1]), (packed[2], packed[3])]
    n = PIECES
    jobs = chains(big, [(1, 1), (2, 7)], 2 * n - 1) + chains(att2, [(-1, 0), (0, 4)], 2 * n - 1)
    (gha, gze, gg_c, gg_m, gp, *packed), got = mlp1_back(
        dpc, got0, near1, far1, gains_in, hm, ubgp, ozq, w_out1, w_fc1, p1p, micro, clips, jobs
    )
    big, att2 = got[2:4], got[4:]
    mlp1 = [(packed[0], packed[1]), (packed[2], packed[3])]
    n = H1 // 2
    jobs = chains(att2, [(1, 0), (2, 2)], 2 * n - 1) + chains(mlp1, [(-1, 0), (0, 1), (1, 2)], 2 * n - 1)
    (near1, far1, down, dna, *packed), got = att1_back(ozq, gze, Ka, Va, xn, ka, w1p, gp, micro, clips, jobs)
    got0, att2, mlp1 = flat(got[:2]), got[2:4], got[4:]
    att1 = [(packed[0], packed[1]), (packed[2], packed[3])]
    streams = [tuple(p) for p in att1 + mlp1 + att2 + big]
    starts = [-1, -1, 2, 2, 3, 3, 3, 3]
    gx, gains, *sums = finish(
        clips, streams, starts, gg_m, gg_c, gg_mlp2, gains_in, near1, far1, dna, down, xn, gha, got0, 7
    )
    rows = D1 // (2 * clips)
    left, right, gw_fc1, gw_out1, gw_qkv2, rest2 = (unfold(v, rows) for v in sums[:6])
    gw_fc2, gw_out2 = sums[6:]
    shares = (
        jnp.concatenate([left, right[:, :D1]], axis=1),
        right[:, D1:],
        gw_fc1,
        stack_blocks(gw_out1, 4),
        gw_qkv2,
        stack_blocks(rest2[:, : 2 * D2], 2),
        rest2[:, 2 * D2 :],
        gw_fc2,
        stack_blocks(gw_out2, 4),
    )
    gains = (gains[0], gains[1], gains[2], gains[3:5].reshape(-1))
    return (output, gx.reshape(inputs.shape)) + gains + tuple(v.reshape(-1) for v in shares)


def solution(mesh):
    tokens = P("group", "micro", "clip", None, None)
    share = P(("clip", "micro"))
    return jax.shard_map(
        body,
        mesh=mesh,
        in_specs=(tokens, P("group"), tokens) + (P(),) * 13,
        out_specs=(tokens, tokens) + (P(),) * 4 + (share,) * 9,
        check_vma=False,
    )
```

```python
from functools import partial

import jax
import jax.numpy as jnp
from jax import lax
from jax.experimental import pallas as pl
from jax.experimental.pallas import tpu as pltpu
from jax.sharding import PartitionSpec as P

D1 = 384
D2 = 768
F1 = 1536
F2 = 3072
QT = 1568
PT = 392
MT = 196
HD = 96
FR = 8
HT = 14
WD = 14
H1 = 4
H2 = 8
CELL = (HT // 2) * (WD // 2)
LANE = 128
PR = 400
MR = 208
KR = PR + 2 * MR
TILE = 784
STEPS = QT // TILE
PIECE = 224
PIECES = QT // PIECE
W1 = H1 * LANE
W2 = H2 * LANE
epsilon = 1e-06
f32 = jnp.float32
bf16 = jnp.bfloat16
SCALE = HD ** (-0.5)
RATE = SCALE * 1.4426950408889634
VMEM_LIMIT = 60 * 1024 * 1024
VMEM = pltpu.VMEM


def mm(a, b):
    return lax.dot_general(a, b, (((1,), (0,)), ((), ())), preferred_element_type=f32)


def mm_nt(a, b):
    return lax.dot_general(a, b, (((1,), (1,)), ((), ())), preferred_element_type=f32)


def mm_tn(a, b):
    return lax.dot_general(a, b, (((0,), (0,)), ((), ())), preferred_element_type=f32)


def lanes(shape):
    return lax.broadcasted_iota(jnp.int32, shape, len(shape) - 1)


def rows_of(shape):
    return lax.broadcasted_iota(jnp.int32, shape, len(shape) - 2)


def norm_stats(values):
    center = values - jnp.mean(values, axis=-1, keepdims=True)
    inv = lax.rsqrt(jnp.mean(center * center, axis=-1, keepdims=True) + epsilon)
    return (center * inv, inv)


def norm_back(grad, unit, inv, gain):
    du = grad * gain
    dg = jnp.sum(grad * unit, axis=0, keepdims=True)
    dx = inv * (
        du - jnp.mean(du, axis=-1, keepdims=True) - unit * jnp.mean(du * unit, axis=-1, keepdims=True)
    )
    return (dx, dg)


def gelu_both(x):
    z = jnp.abs(x)
    t = 1.0 / (1.0 + 0.23164188 * z)
    e = jnp.exp2(x * x * -0.7213475204444817)
    poly = t * (0.127414796 + t * (-0.142248368 + t * (0.7107068705 + t * (-0.7265760135 + t * 0.5307027145))))
    tail = poly * e
    phi = jnp.where(x >= 0.0, 1.0 - tail, tail)
    return (x * phi, phi + (x * 0.3989422804014327) * e)


def split3(v):
    hi = v.astype(bf16).astype(f32)
    mid = (v - hi).astype(bf16).astype(f32)
    return (hi, mid, v - hi - mid)


def put3(base, v):
    hi, mid, low = split3(v)
    lane = lanes(base.shape)
    return jnp.where(
        lane < HD, base, jnp.where(lane == HD, hi, jnp.where(lane == HD + 1, mid, jnp.where(lane == HD + 2, low, base)))
    )


def tmean_matrix():
    rows = rows_of((MR, PR))
    cols = lanes((MR, PR))
    hit = rows < 0
    for pair in range(FR // 2):
        inside = (rows >= pair * CELL) & (rows < (pair + 1) * CELL)
        shift_by = cols - rows - pair * CELL
        hit = hit | (inside & ((shift_by == 0) | (shift_by == CELL)))
    return jnp.where(hit, 0.5, 0.0).astype(bf16)


def pool_rows(ref):
    total = ref[0:PT, :] + ref[PT : 2 * PT, :] + ref[2 * PT : 3 * PT, :] + ref[3 * PT : 4 * PT, :]
    return jnp.concatenate([0.25 * total, jnp.zeros((PR - PT, total.shape[1]), f32)], axis=0).astype(bf16)


MESH = pl.DeviceIdType.MESH
HBM = pl.BlockSpec(memory_space=pl.ANY)


def add_up(a, b):
    return a.astype(f32) + b.astype(f32)


class Shift:
    def __init__(self, source, steps, begin, end, inner=False, video=None):
        self.source, self.video = source, video
        self.ins = [] if isinstance(source, int) else [(source, HBM)]
        shape = (MR, D1)
        self.outs = [] if inner else [whole(shape_of(shape, bf16))]
        self.scratch = [VMEM(shape, bf16)]
        self.peers = [("shift", steps), ("shift", -steps)]
        self.steps, self.inner = steps, inner
        self.sems = 1
        self.events = {begin: [self.start], end: [self.finish]}

    def copy(self, refs, sems, args):
        src = args[self.source] if isinstance(self.source, int) else refs[0]
        if self.video is not None:
            src = src.at[self.video]
        return pltpu.make_async_remote_copy(
            src_ref=src, dst_ref=refs[-1], send_sem=sems[0].at[0], recv_sem=sems[1].at[0],
            device_id={"clip": lax.axis_index("clip") + self.steps}, device_id_type=MESH,
        )

    def start(self, refs, sems, args):
        pl.when(exists(self.steps))(lambda: self.copy(refs, sems, args).start())

    def finish(self, refs, sems, args):
        land = refs[-1]
        pl.when(exists(self.steps))(lambda: self.copy(refs, sems, args).wait_send())
        pl.when(exists(-self.steps))(lambda: self.copy(refs, sems, args).wait_recv())

        @pl.when(jnp.logical_not(exists(-self.steps)))
        def _():
            land[...] = jnp.zeros_like(land)

        if not self.inner:
            refs[-2][...] = land[...]


GROUP = 99


class Chain:
    def __init__(self, parts, order, plan, last):
        keep, other = parts
        self.order, self.plan = order, plan
        tail = keep.shape[1:]
        self.ins = [(keep, HBM), (other, HBM)]
        self.scratch = [VMEM(keep.shape, bf16), VMEM(other.shape, bf16)]
        count = keep.shape[0]
        for number, _ in plan:
            if number < 0:
                continue
            if number == GROUP:
                self.scratch += [VMEM((1,) + tail, bf16)] * 2
                continue
            count //= 2
            self.scratch += [VMEM((count,) + tail, bf16)] * 2
            if number != plan[-1][0]:
                self.scratch.append(VMEM((count,) + tail, bf16))
        self.only_swap = plan[-1][0] < 0
        self.ends = plan[-1][0] == GROUP
        final = (shape_of((count,) + tail, bf16), HBM)
        self.outs = [final] if self.only_swap else [whole(final[0]), final]
        if self.ends:
            self.outs = [whole(shape_of(tail, f32))]
        self.peers = [self.peer(n) for n, _ in plan]
        self.sems = len(plan) + 2
        self.events = {(0, 0): [self.load]}
        for i, (_, step) in enumerate(plan):
            self.events.setdefault((step, 0), []).append(partial(self.advance, i))
        self.events.setdefault((last, 1), []).append(self.finish)
        self.first = plan[0][0]

    def peer(self, number):
        if number < 0:
            return ("micro", 0)
        return ("group", 0) if number == GROUP else ("bit", self.order[number])

    def slots(self, refs):
        other = refs[1]
        outs = refs[2 : 2 + len(self.outs)]
        held = refs[2 + len(self.outs) :]
        pos, slots = 2, []
        for i, (number, _) in enumerate(self.plan):
            final = i == len(self.plan) - 1
            if number < 0:
                slots.append((held[0], other, outs[-1] if final else held[1]))
            elif number == GROUP:
                slots.append((held[pos], held[pos], held[pos + 1]))
                pos += 2
            elif final:
                slots.append((held[pos], held[pos + 1], outs[-1]))
            else:
                slots.append(tuple(held[pos : pos + 3]))
                pos += 3
        return slots

    def load(self, refs, sems, args):
        n = len(self.plan)
        held = refs[2 + len(self.outs) :]
        if not self.only_swap:
            pltpu.make_async_copy(refs[0], held[0], sems[0].at[n]).start()
        if self.first >= 0:
            pltpu.make_async_copy(refs[1], held[1], sems[0].at[n + 1]).start()

    def loaded(self, refs, sems, other):
        n = len(self.plan)
        held = refs[2 + len(self.outs) :]
        pltpu.make_async_copy(refs[0], held[0], sems[0].at[n]).wait()
        if other:
            pltpu.make_async_copy(refs[1], held[1], sems[0].at[n + 1]).wait()

    def copy(self, i, refs, sems):
        number = self.plan[i][0]
        _, away, land = self.slots(refs)[i]
        if number < 0:
            to = {"micro": 1 - lax.axis_index("micro")}
        elif number == GROUP:
            to = {"group": 1 - lax.axis_index("group")}
        else:
            to = {"clip": flipped(self.order[number])}
        return pltpu.make_async_remote_copy(
            src_ref=away, dst_ref=land, send_sem=sems[0].at[i], recv_sem=sems[1].at[i],
            device_id=to, device_id_type=MESH,
        )

    def advance(self, i, refs, sems, args):
        number = self.plan[i][0]
        slots = self.slots(refs)
        if i > 0:
            self.copy(i - 1, refs, sems).wait()
        if number >= 0:
            if i == 0:
                self.loaded(refs, sems, True)
                keep, got = refs[2 + len(self.outs) :][:2]
            else:
                if self.plan[i - 1][0] < 0:
                    self.loaded(refs, sems, False)
                keep, got = slots[i - 1][0], slots[i - 1][2]
            kept, away, _ = slots[i]
            if number == GROUP:
                kept[...] = keep[...] + got[...]
            else:
                bit = self.order[number]
                low = sum(1 for b in self.order[number + 1 :] if b < bit)
                split_shares(keep, got, kept, away, bit, low, kept.shape[0])
        self.copy(i, refs, sems).start()

    def finish(self, refs, sems, args):
        self.copy(len(self.plan) - 1, refs, sems).wait()
        kept, _, land = self.slots(refs)[-1]
        if self.ends:
            refs[2][...] = add_up(kept[0], land[0])
        elif not self.only_swap:
            refs[2][...] = kept[...]


def side(bit):
    return lax.rem(lax.div(lax.axis_index("clip"), 2**bit), 2)


def flipped(bit):
    return lax.axis_index("clip") + (1 - 2 * side(bit)) * 2**bit


def exists(steps):
    other = lax.axis_index("clip") + steps
    return jnp.logical_and(other >= 0, other < lax.axis_size("clip"))


def split_shares(keep, got, kept, send, bit, low, half):
    mine = side(bit)
    for t in range(half):
        base = ((t >> low) << (low + 1)) + (t & (2**low - 1))
        away = base + (1 - mine) * 2**low
        home = base + mine * 2**low
        send[t] = keep[away] + got[away]
        kept[t] = keep[home] + got[home]


def greet(peers):
    barrier = pltpu.get_barrier_semaphore()
    count = jnp.int32(0)
    for kind, arg in sorted(set(peers)):
        if kind == "shift":
            there = exists(arg)
            to = {"clip": lax.axis_index("clip") + arg}

            @pl.when(there)
            def _():
                pl.semaphore_signal(barrier, inc=1, device_id=to, device_id_type=MESH)

            count = count + there.astype(jnp.int32)
        else:
            to = {"clip": flipped(arg)} if kind == "bit" else {kind: 1 - lax.axis_index(kind)}
            pl.semaphore_signal(barrier, inc=1, device_id=to, device_id_type=MESH)
            count = count + 1
    pl.semaphore_wait(barrier, count)


def call(kernel, grid, ins, outs, scratch=(), flops=0, name=None, jobs=(), tag=None):
    ins, outs, scratch = list(ins), list(outs), list(scratch)
    n_in, n_out, n_scratch = len(ins), len(outs), len(scratch)
    places = []
    for job in jobs:
        places.append((len(ins), len(outs), len(scratch)))
        ins += job.ins
        outs += job.outs
        scratch += job.scratch + [pltpu.SemaphoreType.DMA((job.sems,))] * 2

    def body_(*refs):
        i, o = len(ins), len(ins) + len(outs)
        args = refs[:n_in] + refs[i : i + n_out] + refs[o : o + n_scratch]
        if not jobs:
            kernel(*args)
            return
        step = pl.program_id(0)
        sets, lands = [], []
        for job, (pi, po, ps) in zip(jobs, places):
            mine = refs[pi : pi + len(job.ins)] + refs[i + po : i + po + len(job.outs)]
            mine += refs[o + ps : o + ps + len(job.scratch)]
            sems = refs[o + ps + len(job.scratch) : o + ps + len(job.scratch) + 2]
            sets.append((job, mine, sems))
            if getattr(job, "inner", False):
                lands.append(mine[-1])
        moments = sorted({when for job in jobs for when in job.events})

        def run(moment):
            for job, mine, sems in sets:
                for event in job.events.get(moment, ()):
                    event(mine, sems, args)

        @pl.when(step == 0)
        def _():
            greet([p for job in jobs for p in job.peers])

        for moment in moments:
            if moment[1] == 0:
                pl.when(step == moment[0])(partial(run, moment))
        kernel(*args, *lands)
        for moment in moments:
            if moment[1] == 1:
                pl.when(step == moment[0])(partial(run, moment))

    arrays = [a for a, _ in ins]
    moved = sum(a.size * a.dtype.itemsize for a in arrays) + sum(t.size * t.dtype.itemsize for t, _ in outs)
    got = pl.pallas_call(
        body_,
        grid=grid,
        in_specs=[t for _, t in ins],
        out_specs=[t for _, t in outs],
        out_shape=[t for t, _ in outs],
        scratch_shapes=scratch,
        compiler_params=pltpu.CompilerParams(
            vmem_limit_bytes=VMEM_LIMIT,
            dimension_semantics=("arbitrary",) * len(grid),
            **(dict(collective_id=tag, has_side_effects=True) if jobs else {}),
        ),
        cost_estimate=pl.CostEstimate(flops=int(flops), bytes_accessed=int(moved), transcendentals=0),
        name=name,
    )(*arrays)
    results = [got[po : po + len(job.outs)] for job, (_, po, _) in zip(jobs, places)]
    return (got[:n_out], results) if jobs else got


def whole(array):
    return (array, pl.BlockSpec(array.shape, lambda i: (0,) * array.ndim))


def per_video(array, n):
    return (array, pl.BlockSpec((None,) + array.shape[1:], lambda i: (i // n, 0, 0)))


def video_rows(array, n, tile, cols=None, at=0):
    return (array, pl.BlockSpec((None, tile, cols or array.shape[2]), lambda i: (i // n, i % n, at)))


def video_cols(array, n, tile, at=0):
    return (array, pl.BlockSpec((None, array.shape[1], tile), lambda i: (i // n, 0, i % n + at)))


def turn_cols(array, n, tile, at=0):
    return (array, pl.BlockSpec((array.shape[0], tile), lambda i: (0, i % n + at)))


def turn_rows(array, n, tile):
    return (array, pl.BlockSpec((tile, array.shape[1]), lambda i: (i % n, 0)))


def rows_tiled(array, tile=TILE):
    return (array, pl.BlockSpec((tile, array.shape[1]), lambda i: (i, 0)))


def cols_tiled(array, tile, first=0):
    return (array, pl.BlockSpec((array.shape[0], tile), lambda i: (0, i + first)))


def shape_of(shape, dtype):
    return jax.ShapeDtypeStruct(shape, dtype)


def pad_kernel(wa, pa, wc, pc, wa_out, pa_out, wc_out, pc_out):
    for src, dst in ((wa, wa_out), (wc, wc_out)):
        blank = jnp.zeros((src.shape[0], LANE - HD), bf16)
        for j in range(src.shape[1] // HD):
            dst[:, LANE * j : LANE * (j + 1)] = jnp.concatenate([src[:, HD * j : HD * (j + 1)], blank], axis=1)
    for src, dst in ((pa, pa_out), (pc, pc_out)):
        blank = jnp.zeros((LANE - HD, src.shape[1]), bf16)
        for j in range(src.shape[0] // HD):
            dst[LANE * j : LANE * j + HD, :] = src[HD * j : HD * (j + 1), :]
            dst[LANE * j + HD : LANE * (j + 1), :] = blank


def source_of(rows_shape, start):
    r = rows_of(rows_shape)
    s = r // 56
    p = r - s * 56 + start
    f = p // CELL
    rest = p - f * CELL
    r2 = rest // 7
    c2 = rest - r2 * 7
    a = s // 2
    return f * (HT * WD) + r2 * (2 * WD) + a * WD + c2 * 2 + (s - 2 * a)


def first_kernel(x, gain, xn, kv, mem, xs):
    for i in range(7):
        lo = 196 * i // 16 * 16
        hi = min(QT, (196 * i + 392 + 15) // 16 * 16)
        shape = (PIECE, hi - lo)
        pick = jnp.where(source_of(shape, 56 * i) == lanes(shape) + lo, 1.0, 0.0).astype(bf16)
        out = mm(pick, x[0, 0, 0, lo:hi, :])
        for s in range(4):
            xs[PT * s + 56 * i : PT * s + 56 * (i + 1), :] = out[56 * s : 56 * (s + 1)]
    for i in range(PIECES):
        at = slice(PIECE * i, PIECE * (i + 1))
        v = xs[at, :]
        unit, _ = norm_stats(v)
        n = (unit * gain[...]).astype(bf16)
        xn[at, :D1] = v.astype(bf16)
        xn[at, D1:] = n
        xs[at, :] = n.astype(f32)
    pooled = pool_rows(xs)
    kv[...] = pooled
    mem[...] = mm(tmean_matrix(), pooled).astype(bf16)


def front_kernel(x, ga, gb, gc, gd, wa, pa, wc, pc, xn, kv, mem, gains, wa_out, pa_out, wc_out, pc_out, xs, mem0):
    step = pl.program_id(0)

    @pl.when(step == 0)
    def _():
        gains[...] = jnp.concatenate(
            [g[...].reshape(1, D1) for g in (ga, gb, gc)]
            + [gd[0:D1].reshape(1, D1), gd[D1:].reshape(1, D1), jnp.zeros((3, D1), f32)],
            axis=0,
        )

    first_kernel(x, gains.at[0:1, :], xn, kv, mem, xs)

    @pl.when(step == 0)
    def _():
        mem0[...] = mem[...]

    @pl.when(step == 1)
    def _():
        pad_kernel(wa, pa, wc, pc, wa_out, pa_out, wc_out, pc_out)


def front(inputs, gains, w_qkv1, w_proj1, w_qkv2, w_proj2):
    ins = [(inputs, pl.BlockSpec((1, 1, 1, QT, D1), lambda i: (0, i, 0, 0, 0)))] + [whole(g) for g in gains]
    ins += [whole(w) for w in (w_qkv1, w_proj1, w_qkv2, w_proj2)]
    outs = [per_video(shape_of((2,) + t, bf16), 1) for t in ((QT, 2 * D1), (PR, D1), (MR, D1))]
    outs += [whole(shape_of((8, D1), f32))]
    outs += [whole(shape_of(t, bf16)) for t in ((D1, 3 * W1), (W1, D1), (D1, 3 * W2), (W2, D2))]
    jobs = [Shift(18, 1, (0, 1), (1, 1)), Shift(18, 2, (0, 1), (1, 1))]
    return call(
        front_kernel, (2,), ins, outs, [VMEM((QT, D1), f32), VMEM((MR, D1), bf16)],
        flops=4 * QT * 416 * D1, name="first_norm", jobs=jobs, tag=1,
    )


def keys_ext(kall, wk, wv, kext, heads, k_out, v_out):
    k = mm(kall, wk)
    v = mm(kall, wv)
    lane = lanes((KR, LANE))
    ones = jnp.where((lane >= HD) & (lane < HD + 3), 1.0, 0.0)
    for h in range(heads):
        at = slice(LANE * h, LANE * (h + 1))
        k_out[:, at] = (k[:, at] * RATE + kext).astype(bf16)
        v_out[:, at] = (v[:, at] + ones).astype(bf16)


def head_forward(q, s, v):
    top = jnp.max(s, axis=-1, keepdims=True)
    e = jnp.exp2(s - top).astype(bf16)
    mixed = mm(e, v)
    total = mixed[:, HD : HD + 1]
    lse = top + jnp.log(total) * 1.4426950408889634
    return (mixed * (1.0 / total), put3(q.astype(f32), -lse).astype(bf16))


def one_lane(shape):
    return jnp.where(lanes(shape) % LANE == HD + 3, 1.0, 0.0)


def remember(kall, step, near0, far0, near1, far1):
    @pl.when(step == 0)
    def _():
        kall[PR : PR + MR, :] = near0[...]
        kall[PR + MR : KR, :] = far0[...]

    @pl.when(step > 0)
    def _():
        kall[PR : PR + MR, :] = near1[...]
        kall[PR + MR : KR, :] = far1[...]


def block1_kernel(
    kv, near0, far0, kext, xn, wq, wk, wv, wp, gains, wfc, wout,
    kall, k_out, v_out, ozq, hm, ubgp, pc, mem, xs, mem0, near1, far1,
):
    step = pl.program_id(0)
    video, turn = step // STEPS, step % STEPS

    @pl.when(turn == 0)
    def _():
        kall[0:PR, :] = kv[...]
        remember(kall, step, near0, far0, near1, far1)
        keys_ext(kall[...], wk[...], wv[...], kext[...], H1, k_out, v_out)

    q = (mm(xn[:, D1:], wq[...]) + one_lane((TILE, W1))).astype(bf16)
    heads = [slice(LANE * h, LANE * (h + 1)) for h in range(H1)]
    scores = [mm_nt(q[:, at], k_out[:, at]) for at in heads]
    for h, at in enumerate(heads):
        o, qx = head_forward(q[:, at], scores[h], v_out[:, at])
        ozq[:, 2 * W1 + LANE * h : 2 * W1 + LANE * (h + 1)] = qx
        ozq[:, at] = o.astype(bf16)
        ozq[:, W1 + LANE * h : W1 + LANE * (h + 1)] = (o + q[:, at].astype(f32)).astype(bf16)
    ha = xn[:, :D1].astype(f32) + mm(ozq[:, W1 : 2 * W1], wp[...])
    hm[:, :D1] = ha
    unit, _ = norm_stats(ha)
    nb = (unit * gains[1:2, :]).astype(bf16)
    part = F1 // 3
    mid = ha
    ahead = mm(nb, wfc[:, :part])
    for j in range(3):
        at = slice(part * j, part * (j + 1))
        inner = ahead
        if j < 2:
            ahead = mm(nb, wfc[:, part * (j + 1) : part * (j + 2)])
        act, slope = gelu_both(inner)
        act = act.astype(bf16)
        ubgp[:, at] = act
        ubgp[:, F1 + part * j : F1 + part * (j + 1)] = slope.astype(bf16)
        mid = mid + mm(act, wout[at, :])
    hm[:, D1:] = mid
    unit, _ = norm_stats(mid)
    xs[pl.ds(pl.multiple_of(turn * TILE, TILE), TILE), :] = (unit * gains[2:3, :]).astype(bf16).astype(f32)

    @pl.when(turn == STEPS - 1)
    def _():
        pooled = pool_rows(xs)
        pc[...] = pooled
        m = mm(tmean_matrix(), pooled).astype(bf16)
        mem[...] = m

        @pl.when(video == 0)
        def _():
            mem0[...] = m


def block1(kv, got0, mem, kext, xn, w, wp, gains, wfc, wout):
    n = STEPS
    ins = [per_video(kv, n), whole(got0[0]), whole(got0[1]), whole(kext), video_rows(xn, n, TILE)]
    ins += [cols_fixed(w, W1, j) for j in range(3)]
    ins += [whole(wp), whole(gains), whole(wfc), whole(wout)]
    outs = [per_video(shape_of((2, KR, c), bf16), n) for c in (D1, W1, W1)]
    outs += [video_rows(shape_of((2, QT, c), t), n, TILE) for c, t in ((3 * W1, bf16), (2 * D1, f32), (2 * F1, bf16))]
    outs += [per_video(shape_of((2, r, D1), bf16), n) for r in (PR, MR)]
    flops = 4 * QT * (D1 * W1 * 2 + 2 * D1 * F1 + 4 * KR * W1)
    jobs = [Shift(mem, k, (0, 0), (n, 0), True, 1) for k in (1, 2)]
    jobs += [Shift(21, k, (n - 1, 1), (2 * n - 1, 1)) for k in (1, 2)]
    scratch = [VMEM((QT, D1), f32), VMEM((MR, D1), bf16)]
    return call(block1_kernel, (2 * n,), ins, outs, scratch, flops=flops, name="block1_forward", jobs=jobs, tag=2)


def cols_fixed(array, tile, at):
    return (array, pl.BlockSpec((array.shape[0], tile), lambda i: (0, at)))


PAIR = 2 * LANE


def block2_kernel(pc, near0, far0, kext, wq, wk, wv, wskip, wp, kall, k_out, v_out, qe, o_out, zc, hc, near1, far1):
    step = pl.program_id(0)

    @pl.when(step % (H2 // 2) == 0)
    def _():
        kall[0:PR, :] = pc[...]
        remember(kall, step, near0, far0, near1, far1)
        hc[...] = mm(pc[...], wskip[...])

    keys_ext(kall[...], wk[...], wv[...], kext[...], 2, k_out, v_out)
    q = (mm(pc[...], wq[...]) + one_lane((PR, PAIR))).astype(bf16)
    heads = [slice(LANE * h, LANE * (h + 1)) for h in range(2)]
    scores = [mm_nt(q[:, at], k_out[:, at]) for at in heads]
    for h, at in enumerate(heads):
        o, qx = head_forward(q[:, at], scores[h], v_out[:, at])
        qe[:, at] = qx
        o_out[:, at] = o.astype(bf16)
        zc[:, at] = (o + q[:, at].astype(f32)).astype(bf16)
    hc[...] += mm(zc[...], wp[...])


def block2(pc, got0, mem, kext, w, wskip, wp):
    n = H2 // 2
    ins = [per_video(pc, n), whole(got0[0]), whole(got0[1]), whole(kext)]
    ins += [turn_cols(w, n, PAIR, j * n) for j in range(3)]
    ins += [whole(wskip), turn_rows(wp, n, PAIR)]
    outs = [per_video(shape_of((2, KR, D1), bf16), n)]
    outs += [video_cols(shape_of((2, r, W2), bf16), n, PAIR) for r in (KR, KR, PR, PR, PR)]
    outs += [per_video(shape_of((2, PR, D2), f32), n)]
    flops = 4 * (PR * D1 * (W2 + D2) + 2 * KR * D1 * W2 + PR * W2 * D2 + 4 * PR * KR * W2)
    jobs = [Shift(mem, k, (0, 0), (n, 0), True, 1) for k in (1, 2)]
    return call(block2_kernel, (2 * n,), ins, outs, flops=flops, name="block2_attention", jobs=jobs, tag=3)


PART = 768


def pick_share(micro, even, odd):
    first_ = micro == 0
    return (jnp.where(first_, even, odd).astype(bf16), jnp.where(first_, odd, even).astype(bf16))


def wide(gains):
    return jnp.concatenate([gains[3:4, :], gains[4:5, :]], axis=1)


def mlp2_kernel(micro, hc, cot, gain, wfc, wout, out, gh, keep_fc, send_fc, keep_out, send_out, gg, hs, nd, ndt, gm, acc, dn):
    step = pl.program_id(0)

    @pl.when(step == 0)
    def _():
        blank = jnp.zeros((PR - PT, D2), f32)
        for b in range(2):
            at = slice(PR * b, PR * (b + 1))
            v = hc[b]
            hs[at, :] = v
            unit, _ = norm_stats(v)
            nd[at, :] = (unit * wide(gain)).astype(bf16)
            g = cot[0, b, 0].astype(f32)
            gm[at, :] = jnp.concatenate([g, blank], axis=0).astype(bf16)
        ndt[...] = nd[...].T

    act, slope = gelu_both(mm(nd[...], wfc[...]))
    act = act.astype(bf16)
    gi = (slope * mm_nt(gm[...], wout[...])).astype(bf16)
    m = micro[0]
    gw = mm_tn(act, gm[...])
    rows = keep_fc.shape[1]
    for i in range(keep_out.shape[0]):
        keep, send = pick_share(m, gw[8 * rows * i : 8 * rows * i + 4 * rows], gw[8 * rows * i + 4 * rows : 8 * rows * (i + 1)])
        for a in range(4):
            keep_out[i, :, D2 * a : D2 * (a + 1)] = keep[rows * a : rows * (a + 1)]
            send_out[i, :, D2 * a : D2 * (a + 1)] = send[rows * a : rows * (a + 1)]
    gw = mm(ndt[...], gi)
    for i in range(keep_fc.shape[0]):
        keep, send = pick_share(m, gw[2 * rows * i : 2 * rows * i + rows], gw[2 * rows * i + rows : 2 * rows * (i + 1)])
        keep_fc[i] = keep
        send_fc[i] = send
    o = mm(act, wout[...])
    d = mm_nt(gi, wfc[...])

    @pl.when(step == 0)
    def _():
        acc[...] = o
        dn[...] = d

    @pl.when(step > 0)
    def _():
        acc[...] += o
        dn[...] += d

    @pl.when(step == F2 // PART - 1)
    def _():
        v = hs[...]
        y = v + acc[...]
        unit, inv = norm_stats(v)
        dx, dg = norm_back(dn[...], unit, inv, wide(gain))
        gg[...] = dg
        g = (gm[...].astype(f32) + dx).astype(bf16)
        for b in range(2):
            out[0, b, 0] = y[PR * b : PR * b + PT].astype(bf16)
            gh[b] = g[PR * b : PR * (b + 1)]


def scalar(value):
    return (value.astype(jnp.int32).reshape(1), pl.BlockSpec(memory_space=pltpu.SMEM))


def mlp2(micro, clips, hc, cot, gain, wfc, wout):
    rows = D2 // (2 * clips)
    steps = F2 // PART
    ins = [scalar(micro), whole(hc), whole(cot), whole(gain), cols_tiled(wfc, PART), rows_tiled(wout, PART)]
    share = shape_of((clips, rows, F2), bf16)
    fc_spec = (share, pl.BlockSpec((clips, rows, PART), lambda i: (0, 0, i)))
    out_spec = (share, pl.BlockSpec((clips // steps, rows, F2), lambda i: (i, 0, 0)))
    outs = [
        whole(shape_of(cot.shape, bf16)),
        whole(shape_of((2, PR, D2), bf16)),
        fc_spec,
        fc_spec,
        out_spec,
        out_spec,
        whole(shape_of((1, D2), f32)),
    ]
    n = 2 * PR
    scratch = [
        VMEM((n, D2), f32),
        VMEM((n, D2), bf16),
        VMEM((D2, n), bf16),
        VMEM((n, D2), bf16),
        VMEM((n, D2), f32),
        VMEM((n, D2), f32),
    ]
    return call(mlp2_kernel, (steps,), ins, outs, scratch, flops=12 * n * D2 * F2, name="block2_mlp")


def heads_backward(heads, tiles):
    items = [(h, at) for h in range(len(heads)) for at in tiles]

    def products(item):
        q, g, k, v = heads[item[0]]
        return (mm_nt(k, q[item[1]]), mm_nt(v, g[item[1]]))

    out = [([], [], []) for _ in heads]
    kts = [k.T for _, _, k, _ in heads]
    ahead = products(items[0])
    for i, (h, at) in enumerate(items):
        score, dp = ahead
        if i + 1 < len(items):
            ahead = products(items[i + 1])
        q, g, _, _ = heads[h]
        p = jnp.exp2(score)
        ds = (p * dp).astype(bf16)
        dqs, dks, dvs = out[h]
        dvs.append(mm(p.astype(bf16), g[at]))
        dks.append(mm(ds, q[at]))
        dqs.append((mm(kts[h], ds) * (SCALE / RATE)).T)
    return [(dqs, sum(dks[1:], dks[0]) * SCALE, sum(dvs[1:], dvs[0])) for dqs, dks, dvs in out]


def grad_ext(gz, o):
    delta = jnp.sum(jnp.where(lanes(gz.shape) < HD, gz.astype(f32) * o.astype(f32), 0.0), axis=-1, keepdims=True)
    return put3(gz.astype(f32), -delta).astype(bf16)


def put_columns(ref, turn, value):
    ref[:, pl.ds(pl.multiple_of(turn * PAIR, PAIR), PAIR)] = value


def add_to(ref, value, again):
    @pl.when(again)
    def _():
        ref[...] += value

    @pl.when(jnp.logical_not(again))
    def _():
        ref[...] = value


def att2_back_kernel(
    micro, gh, wp, qe, o, k, v, zc, pc, kall, wskip, w,
    dnear, dfar, dpc, keep_a, send_a, keep_b, send_b,
    gq_w, gk_w, gv_w, gp_w, gs_w, dnear0, dfar0, gqs, dks, dvs,
):
    step = pl.program_id(0)
    turn = step % (H2 // 2)
    again = step >= H2 // 2
    gz = mm_nt(gh[...], wp[...]).astype(bf16)
    heads = [slice(LANE * h, LANE * (h + 1)) for h in range(2)]
    gq, dk, dv = [], [], []
    sets = [(qe[:, at], grad_ext(gz[:, at], o[:, at]), k[:, at], v[:, at]) for at in heads]
    for at, (dqs, dkh, dvh) in zip(heads, heads_backward(sets, [slice(0, PR)])):
        gq.append((gz[:, at].astype(f32) + dqs[0]).astype(bf16))
        dk.append(dkh.astype(bf16))
        dv.append(dvh.astype(bf16))
    put_columns(gqs, turn, jnp.concatenate(gq, axis=1))
    put_columns(dks, turn, jnp.concatenate(dk, axis=1))
    put_columns(dvs, turn, jnp.concatenate(dv, axis=1))

    @pl.when(turn == H2 // 2 - 1)
    def _():
        g = gh[...]
        kallt = kall[...].T
        pct = pc[...].T
        add_to(gq_w, mm(pct, gqs[...]), again)
        add_to(gk_w, mm(kallt, dks[...]), again)
        add_to(gv_w, mm(kallt, dvs[...]), again)
        add_to(gp_w, mm_tn(zc[...], g), again)
        add_to(gs_w, mm(pct, g), again)
        dkv = mm_nt(dks[...], w[:, W2 : 2 * W2]) + mm_nt(dvs[...], w[:, 2 * W2 :])
        dpc[...] = mm_nt(g, wskip[...]) + mm_nt(gqs[...], w[:, :W2]) + dkv[0:PR]
        near = dkv[PR : PR + MR].astype(bf16)
        far = dkv[PR + MR : KR].astype(bf16)

        @pl.when(jnp.logical_not(again))
        def _():
            dnear0[...] = near
            dfar0[...] = far

        @pl.when(again)
        def _():
            dnear[...] = near
            dfar[...] = far
            pack2(micro, gq_w, gk_w, gv_w, gp_w, gs_w, keep_a, send_a, keep_b, send_b)


def att2_back(gh, wp, qe, o, k, v, zc, pc, kall, wskip, w, micro, clips, jobs):
    n = H2 // 2
    ins = [scalar(micro), per_video(gh, n), turn_rows(wp, n, PAIR)]
    ins += [video_cols(a, n, PAIR) for a in (qe, o, k, v)]
    ins += [per_video(a, n) for a in (zc, pc, kall)] + [whole(wskip), whole(w)]
    outs = [whole(shape_of((MR, D1), bf16))] * 2 + [per_video(shape_of((2, PR, D1), f32), n)]
    outs += [whole(shape_of((clips,) + folded(D1 // (2 * clips), 3 * D2), bf16))] * 4
    scratch = [VMEM((D1, W2), f32)] * 3 + [VMEM((W2, D2), f32), VMEM((D1, D2), f32)]
    scratch += [VMEM((MR, D1), bf16)] * 2
    scratch += [VMEM((PR, W2), bf16), VMEM((KR, W2), bf16), VMEM((KR, W2), bf16)]
    flops = 4 * (10 * PR * KR * W2 + 4 * PR * D1 * W2 + 4 * KR * D1 * W2 + 4 * PR * W2 * D2)
    jobs = [Shift(24, -1, (n - 1, 1), (2 * n - 1, 1)), Shift(25, -2, (n - 1, 1), (2 * n - 1, 1))] + jobs
    return call(att2_back_kernel, (2 * n,), ins, outs, scratch, flops=flops, name="block2_attention_back", jobs=jobs, tag=4)


def mlp1_back_kernel(
    micro, dpc, rn0, rf0, gains, hm, ubgp, oz, wout, wfc, wp,
    gha, gze, gg_c, gg_m, gw_p, keep_a, send_a, keep_b, send_b,
    gw_out, gw_fc, ds, flip, rn1, rf1,
):
    step = pl.program_id(0)
    turn = step % PIECES

    @pl.when(step == 0)
    def _():
        for ref in (gg_c, gg_m, gw_out, gw_fc, gw_p):
            ref[...] = jnp.zeros_like(ref)

    def spread(rn, rf):
        got = add_up(rn[...], rf[...]).astype(bf16)
        d = 0.25 * (dpc[...] + mm_tn(tmean_matrix(), got))
        for s in range(4):
            ds[PT * s : PT * (s + 1), :] = d[0:PT]

    pl.when(step == 0)(lambda: spread(rn0, rf0))
    pl.when(step == PIECES)(lambda: spread(rn1, rf1))

    unit, inv = norm_stats(hm[:, D1:])
    dnc = ds[pl.ds(pl.multiple_of(turn * PIECE, PIECE), PIECE), :]
    gmid, dg = norm_back(dnc, unit, inv, gains[2:3, :])
    gg_c[...] += dg
    gm = gmid.astype(bf16)
    gmt = gm.T
    unit_b, inv_b = norm_stats(hm[:, :D1])
    nbt = (unit_b * gains[1:2, :]).astype(bf16).T
    part = F1 // 3
    dn = jnp.zeros((PIECE, D1), f32)
    ahead = mm_nt(gm, wout[:part, :])
    for j in range(3):
        at = slice(part * j, part * (j + 1))
        inner = ahead
        if j < 2:
            ahead = mm_nt(gm, wout[part * (j + 1) : part * (j + 2), :])
        slope = ubgp[:, F1 + part * j : F1 + part * (j + 1)].astype(f32)
        gi = (slope * inner).astype(bf16)
        gw_out[:, at] += mm(gmt, ubgp[:, at])
        gw_fc[:, at] += mm(nbt, gi)
        dn = dn + mm_nt(gi, wfc[:, at])
    dx, dg = norm_back(dn, unit_b, inv_b, gains[1:2, :])
    gg_m[...] += dg
    g = gmid + dx
    gha[...] = g
    gh = g.astype(bf16)
    gw_p[...] += mm_tn(oz[:, W1:], gh)
    gz = mm_nt(gh, wp[...]).astype(bf16)
    for h in range(H1):
        at = slice(LANE * h, LANE * (h + 1))
        gze[:, at] = grad_ext(gz[:, at], oz[:, at])

    @pl.when(step == 2 * PIECES - 1)
    def _():
        pack_mlp1(micro, gw_fc, gw_out, keep_a, send_a, keep_b, send_b, flip)


def mlp1_back(dpc, got0, near1, far1, gains, hm, ubgp, ozq, wout, wfc, wp, micro, clips, jobs):
    n = PIECES
    ins = [scalar(micro), per_video(dpc, n), whole(got0[0]), whole(got0[1]), whole(gains)]
    ins += [video_rows(hm, n, PIECE), video_rows(ubgp, n, PIECE), video_rows(ozq, n, PIECE, 2 * W1)]
    ins += [whole(wout), whole(wfc), whole(wp)]
    outs = [video_rows(shape_of((2, QT, D1), f32), n, PIECE), video_rows(shape_of((2, QT, W1), bf16), n, PIECE)]
    outs += [whole(shape_of((1, D1), f32))] * 2 + [whole(shape_of((W1, D1), f32))]
    outs += [whole(shape_of((clips,) + folded(D1 // (2 * clips), F1), bf16))] * 4
    scratch = [VMEM((D1, F1), f32)] * 2 + [VMEM((QT, D1), f32), VMEM((F1, D1), f32)]
    flops = 4 * QT * (4 * D1 * F1 + 2 * D1 * W1)
    jobs = [Shift(near1, -1, (0, 0), (n, 0), True), Shift(far1, -2, (0, 0), (n, 0), True)] + jobs
    return call(mlp1_back_kernel, (2 * n,), ins, outs, scratch, flops=flops, name="block1_mlp_back", jobs=jobs, tag=5)


QUERY_TILES = [slice(0, 512), slice(512, 1024), slice(1024, QT)]


def att1_back_kernel(
    micro, qe, gze, k, v, xn, kall, w, gp,
    dnear, dfar, down, dna, keep_a, send_a, keep_b, send_b,
    gq_w, gk_w, gv_w, qkv, dnear0, dfar0, gqs, dks, dvs,
):
    step = pl.program_id(0)
    turn = step % (H1 // 2)
    again = step >= H1 // 2
    gq, dk, dv = [[] for _ in QUERY_TILES], [], []
    sets = [tuple(r[:, LANE * h : LANE * (h + 1)] for r in (qe, gze, k, v)) for h in range(2)]
    for (_, g, _, _), (dqs, dkh, dvh) in zip(sets, heads_backward(sets, QUERY_TILES)):
        for i, rows in enumerate(QUERY_TILES):
            gq[i].append((g[rows].astype(f32) + dqs[i]).astype(bf16))
        dk.append(dkh.astype(bf16))
        dv.append(dvh.astype(bf16))
    gq = jnp.concatenate([jnp.concatenate(t, axis=1) for t in gq], axis=0)
    lane = lanes((1, PAIR)) % LANE
    put_columns(gqs, turn, jnp.where(lane < HD, gq, jnp.zeros_like(gq)))
    put_columns(dks, turn, jnp.concatenate(dk, axis=1))
    put_columns(dvs, turn, jnp.concatenate(dv, axis=1))

    @pl.when(turn == H1 // 2 - 1)
    def _():
        kallt = kall[...].T
        add_to(gq_w, mm(xn[...].T, gqs[...]), again)
        add_to(gk_w, mm(kallt, dks[...]), again)
        add_to(gv_w, mm(kallt, dvs[...]), again)
        dkv = mm_nt(dks[...], w[:, W1 : 2 * W1]) + mm_nt(dvs[...], w[:, 2 * W1 :])
        dna[...] = mm_nt(gqs[...], w[:, :W1])
        down[...] = dkv[0:PR]
        near = dkv[PR : PR + MR].astype(bf16)
        far = dkv[PR + MR : KR].astype(bf16)

        @pl.when(jnp.logical_not(again))
        def _():
            dnear0[...] = near
            dfar0[...] = far

        @pl.when(again)
        def _():
            dnear[...] = near
            dfar[...] = far
            pack_att1(micro, gq_w, gk_w, gv_w, gp, keep_a, send_a, keep_b, send_b, qkv)


def att1_back(ozq, gze, k, v, xn, kall, w, gp, micro, clips, jobs):
    n = H1 // 2
    ins = [scalar(micro), video_cols(ozq, n, PAIR, 2 * n)] + [video_cols(a, n, PAIR) for a in (gze, k, v)]
    ins += [(xn, pl.BlockSpec((None, QT, D1), lambda i: (i // n, 0, 1))), per_video(kall, n)]
    ins += [whole(w), whole(gp)]
    outs = [whole(shape_of((MR, D1), bf16))] * 2
    outs += [per_video(shape_of((2, PR, D1), f32), n), per_video(shape_of((2, QT, D1), f32), n)]
    outs += [whole(shape_of((clips,) + folded(D1 // (2 * clips), 2 * D1), bf16))] * 4
    scratch = [VMEM((D1, W1), f32)] * 3
    scratch += [VMEM((D1, 4 * D1), f32)] + [VMEM((MR, D1), bf16)] * 2
    scratch += [VMEM((QT, W1), bf16), VMEM((KR, W1), bf16), VMEM((KR, W1), bf16)]
    flops = 4 * (10 * QT * KR * W1 + 2 * QT * D1 * W1 + 4 * KR * D1 * W1)
    jobs = [Shift(21, -1, (n - 1, 1), (2 * n - 1, 1)), Shift(22, -2, (n - 1, 1), (2 * n - 1, 1))] + jobs
    return call(att1_back_kernel, (2 * n,), ins, outs, scratch, flops=flops, name="block1_attention_back", jobs=jobs, tag=6)


def strip(grad):
    return jnp.concatenate([grad[:, LANE * h : LANE * h + HD] for h in range(grad.shape[1] // LANE)], axis=1)


def fold(v):
    rows, cols = v.shape
    if rows != 24:
        return v
    rest = jnp.concatenate([v[16:, : cols // 2], v[16:, cols // 2 :]], axis=0)
    return jnp.concatenate([v[:16], rest], axis=1)


def unfold(v, rows):
    if rows != 24:
        return v
    cols = v.shape[1] * 2 // 3
    rest = jnp.concatenate([v[:8, cols:], v[8:, cols:]], axis=1)
    return jnp.concatenate([v[:, :cols], rest], axis=0)


def folded(rows, cols):
    return (16, cols * 3 // 2) if rows == 24 else (rows, cols)


def store_shares(micro, clips, pieces):
    for i in range(clips):
        for keep, send, piece in pieces:
            k, t = pick_share(micro, fold(piece(2 * i)), fold(piece(2 * i + 1)))
            keep[i] = k
            send[i] = t


def pack2(micro, gq, gk, gv, gp, gs, keep_a, send_a, keep_b, send_b):
    clips, rows = keep_a.shape[0], D1 // (2 * keep_a.shape[0])

    def proj(share, a):
        lo = rows * (2 * share + a)
        h = lo // HD
        start = lo + (LANE - HD) * h
        if (lo + rows - 1) // HD == h:
            return gp[start : start + rows, :]
        cut = HD * (h + 1) - lo
        return jnp.concatenate([gp[start : start + cut, :], gp[LANE * (h + 1) : LANE * (h + 1) + rows - cut, :]], axis=0)

    def piece_a(n):
        return jnp.concatenate([strip(t[rows * n : rows * (n + 1), :]) for t in (gq, gk, gv)], axis=1)

    def piece_b(n):
        return jnp.concatenate([proj(n, 0), proj(n, 1), gs[rows * n : rows * (n + 1), :]], axis=1)

    store_shares(micro[0], clips, ((keep_a, send_a, piece_a), (keep_b, send_b, piece_b)))


def pack_mlp1(micro, gfc, gout, keep_a, send_a, keep_b, send_b, flip):
    flip[...] = gout[...].T
    clips, rows = keep_a.shape[0], D1 // (2 * keep_a.shape[0])

    def piece_a(n):
        return gfc[rows * n : rows * (n + 1), :]

    def piece_b(n):
        return jnp.concatenate([flip[rows * (4 * n + a) : rows * (4 * n + a + 1), :] for a in range(4)], axis=1)

    store_shares(micro[0], clips, ((keep_a, send_a, piece_a), (keep_b, send_b, piece_b)))


def pack_att1(micro, gq, gk, gv, gp, keep_a, send_a, keep_b, send_b, qkv):
    for j, g in enumerate((gq, gk, gv)):
        qkv[:, D1 * j : D1 * (j + 1)] = strip(g[...])
    for h in range(H1):
        qkv[HD * h : HD * (h + 1), 3 * D1 :] = gp[LANE * h : LANE * h + HD, :]
    clips, rows = keep_a.shape[0], D1 // (2 * keep_a.shape[0])
    half = 2 * D1

    def piece_a(n):
        return qkv[rows * n : rows * (n + 1), :half]

    def piece_b(n):
        return qkv[rows * n : rows * (n + 1), half:]

    store_shares(micro[0], clips, ((keep_a, send_a, piece_a), (keep_b, send_b, piece_b)))


def flatten_into(out, v, row=0, column=0, columns=None):
    rows, cols = v.shape
    wide_ = (columns or cols) // LANE
    for j in range(cols // LANE):
        out[pl.ds(row * wide_ + column // LANE + j, rows, stride=wide_), :] = v[:, LANE * j : LANE * (j + 1)]


def lay_out_kernel(rows, left, right, fc1, out1, qkv2, rest2, fc2, out2, *outs):
    left, right, fc1, out1, qkv2, rest2 = (unfold(v[...], rows) for v in (left, right, fc1, out1, qkv2, rest2))
    flatten_into(outs[0], left, 0, 0, 3 * D1)
    flatten_into(outs[0], right[:, :D1], 0, 2 * D1, 3 * D1)
    flatten_into(outs[1], right[:, D1:])
    flatten_into(outs[2], fc1)
    flatten_into(outs[4], qkv2)
    for a in range(2):
        flatten_into(outs[5], rest2[:, D2 * a : D2 * (a + 1)], rows * a)
    flatten_into(outs[6], rest2[:, 2 * D2 :])
    flatten_into(outs[7], fc2[...])
    for a in range(4):
        flatten_into(outs[3], out1[:, D1 * a : D1 * (a + 1)], rows * a)
        flatten_into(outs[8], out2[:, D2 * a : D2 * (a + 1)], 2 * rows * a)


def lay_out(clips, sums):
    sizes = (3 * D1 * D1, D1 * D1, D1 * F1, D1 * F1, 3 * D1 * D2, D2 * D2, D1 * D2, D2 * F2, D2 * F2)
    outs = [whole(shape_of((n // (2 * clips * LANE), LANE), f32)) for n in sizes]
    return call(partial(lay_out_kernel, D1 // (2 * clips)), (1,), [whole(v) for v in sums], outs, name="lay_out")


def bit_order(bits, stream):
    order = list(range(bits))
    if stream % 2 == 1 and bits > 1:
        order[0], order[1] = 1, 0
    return order


def finish_kernel(clips, starts, *refs):
    count = len(starts)
    keeps, gots = refs[:count], refs[count : 2 * count]
    pos = 2 * count
    gg_m, gg_c, gg_d, gain, dnear, dfar, dna, down, xn, gha, rn0, rf0 = refs[pos : pos + 12]
    pos += 12
    gx, gains = refs[pos : pos + 2]
    done = refs[pos + 2 : pos + 2 + count]
    pos += 2 + count
    ds, gs, rn1, rf1, g_all, g_four = refs[pos : pos + 6]
    pos += 6
    bits = clips.bit_length() - 1
    land, stage, ends = {}, {}, {}
    for i in range(count):
        if starts[i] < 0:
            land[i] = refs[pos]
            pos += 1
        for k in range(max(starts[i], 0), bits):
            stage[i, k] = refs[pos : pos + 3]
            pos += 3
        ends[i] = refs[pos : pos + 2]
        pos += 2
    sem_s, sem_r, gsem_s, gsem_r, fsem_s, fsem_r, msem_s, msem_r = refs[pos:]

    g, c, m = (lax.axis_index(a) for a in ("group", "clip", "micro"))
    barrier = pltpu.get_barrier_semaphore()
    others = [{"clip": lax.rem(c + d, clips)} for d in range(1, clips)]
    others += [{"micro": 1 - m}, {"group": 1 - g}, {"group": 1 - g, "micro": 1 - m}]
    for other in others:
        pl.semaphore_signal(barrier, inc=1, device_id=other, device_id_type=MESH)
    pl.semaphore_wait(barrier, len(others))

    shifts = [(dnear, rn1, -1), (dfar, rf1, -2)]

    def memory_copy(i):
        src, dst, steps = shifts[i]
        return pltpu.make_async_remote_copy(
            src_ref=src, dst_ref=dst, send_sem=msem_s.at[i], recv_sem=msem_r.at[i],
            device_id={"clip": c + steps}, device_id_type=MESH,
        )

    for i in range(2):
        pl.when(exists(shifts[i][2]))(lambda i=i: memory_copy(i).start())

    copies = {}

    def send(i, number, src, dst, other):
        n = i * (bits + 2) + number + 1
        copies[i, number] = pltpu.make_async_remote_copy(
            src_ref=src, dst_ref=dst, send_sem=sem_s.at[n], recv_sem=sem_r.at[n],
            device_id=other, device_id_type=MESH,
        )
        copies[i, number].start()

    def advance(i, number):
        if number < 0:
            send(i, number, gots[i], land[i], {"micro": 1 - m})
            return
        if (i, number - 1) in copies:
            copies[i, number - 1].wait()
        if number == starts[i]:
            keep, got = keeps[i], gots[i]
        elif number == 0:
            keep, got = keeps[i], land[i]
        else:
            keep, got = stage[i, number - 1][0], stage[i, number - 1][2]
        if number == bits:
            ends[i][0][...] = add_up(keep[0], got[0]).astype(bf16)
            send(i, number, ends[i][0], ends[i][1], {"group": 1 - g})
        else:
            order = bit_order(bits, i)
            bit = order[number]
            low = sum(1 for b in order[number + 1 :] if b < bit)
            kept, away, there = stage[i, number]
            split_shares(keep, got, kept, away, bit, low, 2 ** (bits - number - 1))
            send(i, number, away, there, {"clip": flipped(bit)})

    at_stage = list(starts)

    def advance_all():
        for i in range(count):
            if at_stage[i] <= bits:
                advance(i, at_stage[i])
                at_stage[i] += 1

    def norm_part(b, rn, rf):
        got = add_up(rn, rf).astype(bf16)
        d = 0.25 * (down[b] + mm_tn(tmean_matrix(), got))
        for s in range(4):
            ds[PT * s : PT * (s + 1), :] = d[0:PT]
        total = jnp.zeros((1, D1), f32)
        for i in range(PIECES):
            at = slice(PIECE * i, PIECE * (i + 1))
            unit, inv = norm_stats(xn[b, at, :].astype(f32))
            dx, dg = norm_back(dna[b, at, :] + ds[at, :], unit, inv, gain[0:1, :])
            total = total + dg
            gs[at, :] = gha[b, at, :] + dx
        return total

    def order_part(b):
        for i in range(PIECES):
            lo = min(CELL * i // 8 * 8, PT - 112)
            window = jnp.concatenate([gs[PT * s + lo : PT * s + lo + 112, :] for s in range(4)], axis=0).astype(bf16)
            shape = (PIECE, 4 * 112)
            t = rows_of(shape) + PIECE * i
            f = t // (HT * WD)
            rest = t - f * (HT * WD)
            r = rest // WD
            col = rest - r * WD
            r2 = r // 2
            c2 = col // 2
            s = 2 * (r - 2 * r2) + (col - 2 * c2)
            p = f * CELL + r2 * 7 + c2
            pick = jnp.where(s * 112 + p - lo == lanes(shape), 1.0, 0.0).astype(bf16)
            gx[b, PIECE * i : PIECE * (i + 1), :] = mm(pick, window).astype(bf16)

    advance_all()
    gg = norm_part(0, rn0[...], rf0[...])
    advance_all()
    order_part(0)
    advance_all()
    for i in range(2):
        _, dst, steps = shifts[i]
        pl.when(exists(steps))(lambda i=i: memory_copy(i).wait_send())

        @pl.when(exists(-steps))
        def _():
            memory_copy(i).wait_recv()

        @pl.when(jnp.logical_not(exists(-steps)))
        def _():
            dst[...] = jnp.zeros_like(dst)

    gg = gg + norm_part(1, rn1[...], rf1[...])
    advance_all()
    g_all[c] = jnp.concatenate(
        [gg, gg_m[...], gg_c[...], gg_d[:, :D1], gg_d[:, D1:], jnp.zeros((3, D1), f32)], axis=0
    )
    gcopies = []
    for d in range(1, clips):
        gcopies.append(
            pltpu.make_async_remote_copy(
                src_ref=g_all.at[c], dst_ref=g_all.at[c], send_sem=gsem_s.at[d - 1], recv_sem=gsem_r.at[d - 1],
                device_id={"clip": lax.rem(c + d, clips)}, device_id_type=MESH,
            )
        )
        gcopies[-1].start()
    order_part(1)
    advance_all()
    for copy in gcopies:
        copy.wait()
    total = g_all[0]
    for i in range(1, clips):
        total = total + g_all[i]
    place = 2 * g + m
    g_four[place] = total
    fcopies = []
    for i, other in enumerate(others[-3:]):
        fcopies.append(
            pltpu.make_async_remote_copy(
                src_ref=g_four.at[place], dst_ref=g_four.at[place], send_sem=fsem_s.at[i], recv_sem=fsem_r.at[i],
                device_id=other, device_id_type=MESH,
            )
        )
        fcopies[-1].start()
    for _ in range(bits + 2):
        advance_all()
    for copy in fcopies:
        copy.wait()
    gains[...] = (g_four[0] + g_four[1]) + (g_four[2] + g_four[3])
    for i in range(count):
        copies[i, bits].wait()
        done[i][...] = add_up(*(ref[...] for ref in ends[i]))


def finish(clips, streams, starts, gg_m, gg_c, gg_d, gain, dnear, dfar, dna, down, xn, gha, got0, tag):
    bits = clips.bit_length() - 1
    count = len(streams)
    ins = [whole(k) for k, _ in streams] + [(t, HBM) if n < 0 else whole(t) for (_, t), n in zip(streams, starts)]
    ins += [whole(a) for a in (gg_m, gg_c, gg_d, gain)] + [(dnear, HBM), (dfar, HBM)]
    ins += [whole(dna), whole(down), (xn, pl.BlockSpec((2, QT, D1), lambda i: (0, 0, 0))), whole(gha)]
    ins += [whole(a) for a in got0]
    parts = [k.shape[1:] for k, _ in streams]
    outs = [whole(shape_of((2, QT, D1), bf16)), whole(shape_of((8, D1), f32))]
    outs += [whole(shape_of(p, f32)) for p in parts]
    scratch = [VMEM((QT, D1), f32)] * 2 + [VMEM((MR, D1), bf16)] * 2
    scratch += [VMEM((clips, 8, D1), f32), VMEM((4, 8, D1), f32)]
    for p, n in zip(parts, starts):
        if n < 0:
            scratch.append(VMEM((clips,) + p, bf16))
        for k in range(max(n, 0), bits):
            scratch += [VMEM((2 ** (bits - 1 - k),) + p, bf16)] * 3
        scratch += [VMEM(p, bf16)] * 2
    dma = pltpu.SemaphoreType.DMA
    for n in (count * (bits + 2), clips - 1, 3, 2):
        scratch += [dma((n,))] * 2
    return pl.pallas_call(
        partial(finish_kernel, clips, starts),
        grid=(1,),
        in_specs=[t for _, t in ins],
        out_specs=[t for _, t in outs],
        out_shape=[t for t, _ in outs],
        scratch_shapes=scratch,
        compiler_params=pltpu.CompilerParams(
            vmem_limit_bytes=VMEM_LIMIT, collective_id=tag, has_side_effects=True
        ),
        name="finish",
    )(*[a for a, _ in ins])


def body(inputs, offsets, cotangent, gain_attn1, w_qkv1, w_proj1, gain_mlp1, w_fc1, w_out1,
         gain_attn2, w_qkv2, w_proj2, w_skip, gain_mlp2, w_fc2, w_out2):
    clip = lax.axis_index("clip")
    row = jnp.arange(KR, dtype=jnp.int32)[:, None]
    place = jnp.where(row < PR + MR, row - PR, row - PR - MR)
    later = (place // CELL >= offsets[0]) & (place < MT)
    hops = jnp.where(row < PR + MR, 1, 2)
    valid = jnp.where(row < PR, row < PT, later & (clip >= hops))
    lane = jnp.arange(LANE, dtype=jnp.int32)[None, :]
    kext = jnp.where(lane == HD + 3, jnp.where(valid, 0.0, -1e30), jnp.where((lane >= HD) & (lane < HD + 3), 1.0, 0.0))
    kext = kext.astype(f32)

    micro, clips = lax.axis_index("micro"), lax.axis_size("clip")
    bits = clips.bit_length() - 1

    def flat(results):
        return [r[0] for r in results]

    gains_in = (gain_attn1, gain_mlp1, gain_attn2, gain_mlp2)
    (xn, kva, mem, gains_in, w1p, p1p, w2p, p2p), got = front(inputs, gains_in, w_qkv1, w_proj1, w_qkv2, w_proj2)
    (ka, Ka, Va, ozq, hm, ubgp, pc, mem), got = block1(kva, flat(got), mem, kext, xn, w1p, p1p, gains_in, w_fc1, w_out1)
    (kc, Kc, Vc, qec, oc, zc, hc), _ = block2(pc, flat(got[2:]), mem, kext, w2p, w_skip, p2p)
    output, gh, keep_fc, send_fc, keep_out, send_out, gg_mlp2 = mlp2(micro, clips, hc, cotangent, gains_in, w_fc2, w_out2)

    orders = [bit_order(bits, i) for i in range(2)]

    def chains(parts, plan, last):
        return [Chain(p, o, plan, last) for p, o in zip(parts, orders)]

    n = H2 // 2
    jobs = chains([(keep_fc, send_fc), (keep_out, send_out)], [(-1, 0), (0, 3)], 2 * n - 1)
    (near1, far1, dpc, *packed), got = att2_back(gh, p2p, qec, oc, Kc, Vc, zc, pc, kc, w_skip, w2p, micro, clips, jobs)
    got0, big = flat(got[:2]), got[2:]
    att2 = [(packed[0], packed[1]), (packed[2], packed[3])]
    n = PIECES
    jobs = chains(big, [(1, 1), (2, 7)], 2 * n - 1) + chains(att2, [(-1, 0), (0, 4)], 2 * n - 1)
    (gha, gze, gg_c, gg_m, gp, *packed), got = mlp1_back(
        dpc, got0, near1, far1, gains_in, hm, ubgp, ozq, w_out1, w_fc1, p1p, micro, clips, jobs
    )
    big, att2 = got[2:4], got[4:]
    mlp1 = [(packed[0], packed[1]), (packed[2], packed[3])]
    n = H1 // 2
    rest = [(k, 0) for k in range(3, bits)]
    jobs = chains(big, rest + [(GROUP, 0)], 2 * n - 1)
    rest = [(k, 2) for k in range(2, bits)]
    jobs += chains(att2, [(1, 0)] + rest + [(GROUP, 3)], 2 * n - 1)
    rest = [(k, 3) for k in range(2, bits)]
    jobs += chains(mlp1, [(-1, 0), (0, 1), (1, 2)] + rest, 2 * n - 1)
    (near1, far1, down, dna, *packed), got = att1_back(ozq, gze, Ka, Va, xn, ka, w1p, gp, micro, clips, jobs)
    got0, big, att2, mlp1 = flat(got[:2]), flat(got[2:4]), flat(got[4:6]), got[6:]
    att1 = [(packed[0], packed[1]), (packed[2], packed[3])]
    streams = [tuple(p) for p in att1 + mlp1]
    starts = [-1, -1, bits, bits]
    gx, gains, *sums = finish(
        clips, streams, starts, gg_m, gg_c, gg_mlp2, gains_in, near1, far1, dna, down, xn, gha, got0, 7
    )
    shares = lay_out(clips, sums + att2 + big)
    gains = (gains[0], gains[1], gains[2], gains[3:5].reshape(-1))
    return (output, gx.reshape(inputs.shape)) + gains + tuple(v.reshape(-1) for v in shares)


def solution(mesh):
    tokens = P("group", "micro", "clip", None, None)
    share = P(("clip", "micro"))
    return jax.shard_map(
        body,
        mesh=mesh,
        in_specs=(tokens, P("group"), tokens) + (P(),) * 13,
        out_specs=(tokens, tokens) + (P(),) * 4 + (share,) * 9,
        check_vma=False,
    )
```

```python
from functools import partial

import jax
import jax.numpy as jnp
from jax import lax
from jax.experimental import pallas as pl
from jax.experimental.pallas import tpu as pltpu
from jax.sharding import PartitionSpec as P

D1 = 384
D2 = 768
F1 = 1536
F2 = 3072
QT = 1568
PT = 392
MT = 196
HD = 96
FR = 8
HT = 14
WD = 14
H1 = 4
H2 = 8
CELL = (HT // 2) * (WD // 2)
LANE = 128
PR = 400
MR = 208
KR = PR + 2 * MR
TILE = 784
STEPS = QT // TILE
PIECE = 224
PIECES = QT // PIECE
W1 = H1 * LANE
W2 = H2 * LANE
epsilon = 1e-06
f32 = jnp.float32
bf16 = jnp.bfloat16
SCALE = HD ** (-0.5)
RATE = SCALE * 1.4426950408889634
VMEM_LIMIT = 60 * 1024 * 1024
VMEM = pltpu.VMEM


def mm(a, b):
    return lax.dot_general(a, b, (((1,), (0,)), ((), ())), preferred_element_type=f32)


def mm_nt(a, b):
    return lax.dot_general(a, b, (((1,), (1,)), ((), ())), preferred_element_type=f32)


def mm_tn(a, b):
    return lax.dot_general(a, b, (((0,), (0,)), ((), ())), preferred_element_type=f32)


def lanes(shape):
    return lax.broadcasted_iota(jnp.int32, shape, len(shape) - 1)


def rows_of(shape):
    return lax.broadcasted_iota(jnp.int32, shape, len(shape) - 2)


def norm_stats(values):
    center = values - jnp.mean(values, axis=-1, keepdims=True)
    inv = lax.rsqrt(jnp.mean(center * center, axis=-1, keepdims=True) + epsilon)
    return (center * inv, inv)


def norm_back(grad, unit, inv, gain):
    du = grad * gain
    dg = jnp.sum(grad * unit, axis=0, keepdims=True)
    dx = inv * (
        du - jnp.mean(du, axis=-1, keepdims=True) - unit * jnp.mean(du * unit, axis=-1, keepdims=True)
    )
    return (dx, dg)


def gelu_both(x):
    z = jnp.abs(x)
    t = 1.0 / (1.0 + 0.23164188 * z)
    e = jnp.exp2(x * x * -0.7213475204444817)
    poly = t * (0.127414796 + t * (-0.142248368 + t * (0.7107068705 + t * (-0.7265760135 + t * 0.5307027145))))
    tail = poly * e
    phi = jnp.where(x >= 0.0, 1.0 - tail, tail)
    return (x * phi, phi + (x * 0.3989422804014327) * e)


def split3(v):
    hi = v.astype(bf16).astype(f32)
    mid = (v - hi).astype(bf16).astype(f32)
    return (hi, mid, v - hi - mid)


def put3(base, v):
    hi, mid, low = split3(v)
    lane = lanes(base.shape)
    return jnp.where(
        lane < HD, base, jnp.where(lane == HD, hi, jnp.where(lane == HD + 1, mid, jnp.where(lane == HD + 2, low, base)))
    )


def tmean_matrix():
    rows = rows_of((MR, PR))
    cols = lanes((MR, PR))
    hit = rows < 0
    for pair in range(FR // 2):
        inside = (rows >= pair * CELL) & (rows < (pair + 1) * CELL)
        shift_by = cols - rows - pair * CELL
        hit = hit | (inside & ((shift_by == 0) | (shift_by == CELL)))
    return jnp.where(hit, 0.5, 0.0).astype(bf16)


def pool_rows(ref):
    total = ref[0:PT, :] + ref[PT : 2 * PT, :] + ref[2 * PT : 3 * PT, :] + ref[3 * PT : 4 * PT, :]
    return jnp.concatenate([0.25 * total, jnp.zeros((PR - PT, total.shape[1]), f32)], axis=0).astype(bf16)


MESH = pl.DeviceIdType.MESH
HBM = pl.BlockSpec(memory_space=pl.ANY)


def add_up(a, b):
    return a.astype(f32) + b.astype(f32)


class Shift:
    def __init__(self, source, steps, begin, end, inner=False, video=None):
        self.source, self.video = source, video
        self.ins = [] if isinstance(source, int) else [(source, HBM)]
        shape = (MR, D1)
        self.outs = [] if inner else [whole(shape_of(shape, bf16))]
        self.scratch = [VMEM(shape, bf16)]
        self.peers = [("shift", steps), ("shift", -steps)]
        self.steps, self.inner = steps, inner
        self.sems = 1
        self.events = {begin: [self.start], end: [self.finish]}

    def copy(self, refs, sems, args):
        src = args[self.source] if isinstance(self.source, int) else refs[0]
        if self.video is not None:
            src = src.at[self.video]
        return pltpu.make_async_remote_copy(
            src_ref=src, dst_ref=refs[-1], send_sem=sems[0].at[0], recv_sem=sems[1].at[0],
            device_id={"clip": lax.axis_index("clip") + self.steps}, device_id_type=MESH,
        )

    def start(self, refs, sems, args):
        pl.when(exists(self.steps))(lambda: self.copy(refs, sems, args).start())

    def finish(self, refs, sems, args):
        land = refs[-1]
        pl.when(exists(self.steps))(lambda: self.copy(refs, sems, args).wait_send())
        pl.when(exists(-self.steps))(lambda: self.copy(refs, sems, args).wait_recv())

        @pl.when(jnp.logical_not(exists(-self.steps)))
        def _():
            land[...] = jnp.zeros_like(land)

        if not self.inner:
            refs[-2][...] = land[...]


GROUP = 99


class Chain:
    def __init__(self, parts, order, plan, last):
        keep, other = parts
        self.order, self.plan = order, plan
        tail = keep.shape[1:]
        self.ins = [(keep, HBM), (other, HBM)]
        self.scratch = [VMEM(keep.shape, bf16), VMEM(other.shape, bf16)]
        count = keep.shape[0]
        for number, _ in plan:
            if number < 0:
                continue
            if number == GROUP:
                self.scratch += [VMEM((1,) + tail, bf16)] * 2
                continue
            count //= 2
            self.scratch += [VMEM((count,) + tail, bf16)] * 2
            if number != plan[-1][0]:
                self.scratch.append(VMEM((count,) + tail, bf16))
        self.only_swap = plan[-1][0] < 0
        self.ends = plan[-1][0] == GROUP
        final = (shape_of((count,) + tail, bf16), HBM)
        self.outs = [final] if self.only_swap else [whole(final[0]), final]
        if self.ends:
            self.outs = [whole(shape_of(tail, f32))]
        self.peers = [self.peer(n) for n, _ in plan]
        self.sems = len(plan) + 2
        self.events = {(0, 0): [self.load]}
        for i, (_, step) in enumerate(plan):
            self.events.setdefault((step, 0), []).append(partial(self.advance, i))
        self.events.setdefault((last, 1), []).append(self.finish)
        self.first = plan[0][0]

    def peer(self, number):
        if number < 0:
            return ("micro", 0)
        return ("group", 0) if number == GROUP else ("bit", self.order[number])

    def slots(self, refs):
        other = refs[1]
        outs = refs[2 : 2 + len(self.outs)]
        held = refs[2 + len(self.outs) :]
        pos, slots = 2, []
        for i, (number, _) in enumerate(self.plan):
            final = i == len(self.plan) - 1
            if number < 0:
                slots.append((held[0], other, outs[-1] if final else held[1]))
            elif number == GROUP:
                slots.append((held[pos], held[pos], held[pos + 1]))
                pos += 2
            elif final:
                slots.append((held[pos], held[pos + 1], outs[-1]))
            else:
                slots.append(tuple(held[pos : pos + 3]))
                pos += 3
        return slots

    def load(self, refs, sems, args):
        n = len(self.plan)
        held = refs[2 + len(self.outs) :]
        if not self.only_swap:
            pltpu.make_async_copy(refs[0], held[0], sems[0].at[n]).start()
        if self.first >= 0:
            pltpu.make_async_copy(refs[1], held[1], sems[0].at[n + 1]).start()

    def loaded(self, refs, sems, other):
        n = len(self.plan)
        held = refs[2 + len(self.outs) :]
        pltpu.make_async_copy(refs[0], held[0], sems[0].at[n]).wait()
        if other:
            pltpu.make_async_copy(refs[1], held[1], sems[0].at[n + 1]).wait()

    def copy(self, i, refs, sems):
        number = self.plan[i][0]
        _, away, land = self.slots(refs)[i]
        if number < 0:
            to = {"micro": 1 - lax.axis_index("micro")}
        elif number == GROUP:
            to = {"group": 1 - lax.axis_index("group")}
        else:
            to = {"clip": flipped(self.order[number])}
        return pltpu.make_async_remote_copy(
            src_ref=away, dst_ref=land, send_sem=sems[0].at[i], recv_sem=sems[1].at[i],
            device_id=to, device_id_type=MESH,
        )

    def advance(self, i, refs, sems, args):
        number = self.plan[i][0]
        slots = self.slots(refs)
        if i > 0:
            self.copy(i - 1, refs, sems).wait()
        if number >= 0:
            if i == 0:
                self.loaded(refs, sems, True)
                keep, got = refs[2 + len(self.outs) :][:2]
            else:
                if self.plan[i - 1][0] < 0:
                    self.loaded(refs, sems, False)
                keep, got = slots[i - 1][0], slots[i - 1][2]
            kept, away, _ = slots[i]
            if number == GROUP:
                kept[...] = keep[...] + got[...]
            else:
                bit = self.order[number]
                low = sum(1 for b in self.order[number + 1 :] if b < bit)
                split_shares(keep, got, kept, away, bit, low, kept.shape[0])
        self.copy(i, refs, sems).start()

    def finish(self, refs, sems, args):
        self.copy(len(self.plan) - 1, refs, sems).wait()
        kept, _, land = self.slots(refs)[-1]
        if self.ends:
            refs[2][...] = add_up(kept[0], land[0])
        elif not self.only_swap:
            refs[2][...] = kept[...]


def side(bit):
    return lax.rem(lax.div(lax.axis_index("clip"), 2**bit), 2)


def flipped(bit):
    return lax.axis_index("clip") + (1 - 2 * side(bit)) * 2**bit


def exists(steps):
    other = lax.axis_index("clip") + steps
    return jnp.logical_and(other >= 0, other < lax.axis_size("clip"))


def split_shares(keep, got, kept, send, bit, low, half):
    mine = side(bit)
    for t in range(half):
        base = ((t >> low) << (low + 1)) + (t & (2**low - 1))
        away = base + (1 - mine) * 2**low
        home = base + mine * 2**low
        send[t] = keep[away] + got[away]
        kept[t] = keep[home] + got[home]


def greet(peers):
    barrier = pltpu.get_barrier_semaphore()
    count = jnp.int32(0)
    for kind, arg in sorted(set(peers)):
        if kind == "shift":
            there = exists(arg)
            to = {"clip": lax.axis_index("clip") + arg}

            @pl.when(there)
            def _():
                pl.semaphore_signal(barrier, inc=1, device_id=to, device_id_type=MESH)

            count = count + there.astype(jnp.int32)
        else:
            to = {"clip": flipped(arg)} if kind == "bit" else {kind: 1 - lax.axis_index(kind)}
            pl.semaphore_signal(barrier, inc=1, device_id=to, device_id_type=MESH)
            count = count + 1
    pl.semaphore_wait(barrier, count)


def call(kernel, grid, ins, outs, scratch=(), flops=0, name=None, jobs=(), tag=None):
    ins, outs, scratch = list(ins), list(outs), list(scratch)
    n_in, n_out, n_scratch = len(ins), len(outs), len(scratch)
    places = []
    for job in jobs:
        places.append((len(ins), len(outs), len(scratch)))
        ins += job.ins
        outs += job.outs
        scratch += job.scratch + [pltpu.SemaphoreType.DMA((job.sems,))] * 2

    def body_(*refs):
        i, o = len(ins), len(ins) + len(outs)
        args = refs[:n_in] + refs[i : i + n_out] + refs[o : o + n_scratch]
        if not jobs:
            kernel(*args)
            return
        step = pl.program_id(0)
        sets, lands = [], []
        for job, (pi, po, ps) in zip(jobs, places):
            mine = refs[pi : pi + len(job.ins)] + refs[i + po : i + po + len(job.outs)]
            mine += refs[o + ps : o + ps + len(job.scratch)]
            sems = refs[o + ps + len(job.scratch) : o + ps + len(job.scratch) + 2]
            sets.append((job, mine, sems))
            if getattr(job, "inner", False):
                lands.append(mine[-1])
        moments = sorted({when for job in jobs for when in job.events})

        def run(moment):
            for job, mine, sems in sets:
                for event in job.events.get(moment, ()):
                    event(mine, sems, args)

        @pl.when(step == 0)
        def _():
            greet([p for job in jobs for p in job.peers])

        for moment in moments:
            if moment[1] == 0:
                pl.when(step == moment[0])(partial(run, moment))
        kernel(*args, *lands)
        for moment in moments:
            if moment[1] == 1:
                pl.when(step == moment[0])(partial(run, moment))

    arrays = [a for a, _ in ins]
    moved = sum(a.size * a.dtype.itemsize for a in arrays) + sum(t.size * t.dtype.itemsize for t, _ in outs)
    got = pl.pallas_call(
        body_,
        grid=grid,
        in_specs=[t for _, t in ins],
        out_specs=[t for _, t in outs],
        out_shape=[t for t, _ in outs],
        scratch_shapes=scratch,
        compiler_params=pltpu.CompilerParams(
            vmem_limit_bytes=VMEM_LIMIT,
            dimension_semantics=("arbitrary",) * len(grid),
            **(dict(collective_id=tag, has_side_effects=True) if jobs else {}),
        ),
        cost_estimate=pl.CostEstimate(flops=int(flops), bytes_accessed=int(moved), transcendentals=0),
        name=name,
    )(*arrays)
    results = [got[po : po + len(job.outs)] for job, (_, po, _) in zip(jobs, places)]
    return (got[:n_out], results) if jobs else got


def whole(array):
    return (array, pl.BlockSpec(array.shape, lambda i: (0,) * array.ndim))


def per_video(array, n):
    return (array, pl.BlockSpec((None,) + array.shape[1:], lambda i: (i // n, 0, 0)))


def video_rows(array, n, tile, cols=None, at=0):
    return (array, pl.BlockSpec((None, tile, cols or array.shape[2]), lambda i: (i // n, i % n, at)))


def video_cols(array, n, tile, at=0):
    return (array, pl.BlockSpec((None, array.shape[1], tile), lambda i: (i // n, 0, i % n + at)))


def turn_cols(array, n, tile, at=0):
    return (array, pl.BlockSpec((array.shape[0], tile), lambda i: (0, i % n + at)))


def turn_rows(array, n, tile):
    return (array, pl.BlockSpec((tile, array.shape[1]), lambda i: (i % n, 0)))


def rows_tiled(array, tile=TILE):
    return (array, pl.BlockSpec((tile, array.shape[1]), lambda i: (i, 0)))


def cols_tiled(array, tile, first=0):
    return (array, pl.BlockSpec((array.shape[0], tile), lambda i: (0, i + first)))


def shape_of(shape, dtype):
    return jax.ShapeDtypeStruct(shape, dtype)


def pad_kernel(wa, pa, wc, pc, wa_out, pa_out, wc_out, pc_out):
    for src, dst in ((wa, wa_out), (wc, wc_out)):
        blank = jnp.zeros((src.shape[0], LANE - HD), bf16)
        for j in range(src.shape[1] // HD):
            dst[:, LANE * j : LANE * (j + 1)] = jnp.concatenate([src[:, HD * j : HD * (j + 1)], blank], axis=1)
    for src, dst in ((pa, pa_out), (pc, pc_out)):
        blank = jnp.zeros((LANE - HD, src.shape[1]), bf16)
        for j in range(src.shape[0] // HD):
            dst[LANE * j : LANE * j + HD, :] = src[HD * j : HD * (j + 1), :]
            dst[LANE * j + HD : LANE * (j + 1), :] = blank


def source_of(rows_shape, start):
    r = rows_of(rows_shape)
    s = r // 56
    p = r - s * 56 + start
    f = p // CELL
    rest = p - f * CELL
    r2 = rest // 7
    c2 = rest - r2 * 7
    a = s // 2
    return f * (HT * WD) + r2 * (2 * WD) + a * WD + c2 * 2 + (s - 2 * a)


def first_kernel(x, gain, xn, kv, mem, xs):
    for i in range(7):
        lo = 196 * i // 16 * 16
        hi = min(QT, (196 * i + 392 + 15) // 16 * 16)
        shape = (PIECE, hi - lo)
        pick = jnp.where(source_of(shape, 56 * i) == lanes(shape) + lo, 1.0, 0.0).astype(bf16)
        out = mm(pick, x[0, 0, 0, lo:hi, :])
        for s in range(4):
            xs[PT * s + 56 * i : PT * s + 56 * (i + 1), :] = out[56 * s : 56 * (s + 1)]
    for i in range(PIECES):
        at = slice(PIECE * i, PIECE * (i + 1))
        v = xs[at, :]
        unit, _ = norm_stats(v)
        n = (unit * gain[...]).astype(bf16)
        xn[at, :D1] = v.astype(bf16)
        xn[at, D1:] = n
        xs[at, :] = n.astype(f32)
    pooled = pool_rows(xs)
    kv[...] = pooled
    mem[...] = mm(tmean_matrix(), pooled).astype(bf16)


def front_kernel(x, ga, gb, gc, gd, wa, pa, wc, pc, xn, kv, mem, gains, wa_out, pa_out, wc_out, pc_out, xs, mem0):
    step = pl.program_id(0)

    @pl.when(step == 0)
    def _():
        gains[...] = jnp.concatenate(
            [g[...].reshape(1, D1) for g in (ga, gb, gc)]
            + [gd[0:D1].reshape(1, D1), gd[D1:].reshape(1, D1), jnp.zeros((3, D1), f32)],
            axis=0,
        )

    first_kernel(x, gains.at[0:1, :], xn, kv, mem, xs)

    @pl.when(step == 0)
    def _():
        mem0[...] = mem[...]

    @pl.when(step == 1)
    def _():
        pad_kernel(wa, pa, wc, pc, wa_out, pa_out, wc_out, pc_out)


def front(inputs, gains, w_qkv1, w_proj1, w_qkv2, w_proj2):
    ins = [(inputs, pl.BlockSpec((1, 1, 1, QT, D1), lambda i: (0, i, 0, 0, 0)))] + [whole(g) for g in gains]
    ins += [whole(w) for w in (w_qkv1, w_proj1, w_qkv2, w_proj2)]
    outs = [per_video(shape_of((2,) + t, bf16), 1) for t in ((QT, 2 * D1), (PR, D1), (MR, D1))]
    outs += [whole(shape_of((8, D1), f32))]
    outs += [whole(shape_of(t, bf16)) for t in ((D1, 3 * W1), (W1, D1), (D1, 3 * W2), (W2, D2))]
    jobs = [Shift(18, 1, (0, 1), (1, 1)), Shift(18, 2, (0, 1), (1, 1))]
    return call(
        front_kernel, (2,), ins, outs, [VMEM((QT, D1), f32), VMEM((MR, D1), bf16)],
        flops=4 * QT * 416 * D1, name="first_norm", jobs=jobs, tag=1,
    )


def keys_ext(kall, wk, wv, kext, heads, k_out, v_out):
    k = mm(kall, wk)
    v = mm(kall, wv)
    lane = lanes((KR, LANE))
    ones = jnp.where((lane >= HD) & (lane < HD + 3), 1.0, 0.0)
    for h in range(heads):
        at = slice(LANE * h, LANE * (h + 1))
        k_out[:, at] = (k[:, at] * RATE + kext).astype(bf16)
        v_out[:, at] = (v[:, at] + ones).astype(bf16)


def head_forward(q, s, v):
    top = jnp.max(s, axis=-1, keepdims=True)
    e = jnp.exp2(s - top).astype(bf16)
    mixed = mm(e, v)
    total = mixed[:, HD : HD + 1]
    lse = top + jnp.log(total) * 1.4426950408889634
    return (mixed * (1.0 / total), put3(q.astype(f32), -lse).astype(bf16))


def one_lane(shape):
    return jnp.where(lanes(shape) % LANE == HD + 3, 1.0, 0.0)


def remember(kall, step, near0, far0, near1, far1):
    @pl.when(step == 0)
    def _():
        kall[PR : PR + MR, :] = near0[...]
        kall[PR + MR : KR, :] = far0[...]

    @pl.when(step > 0)
    def _():
        kall[PR : PR + MR, :] = near1[...]
        kall[PR + MR : KR, :] = far1[...]


def block1_kernel(
    kv, near0, far0, kext, xn, wq, wk, wv, wp, gains, wfc, wout,
    kall, k_out, v_out, ozq, hm, ubgp, pc, mem, xs, mem0, near1, far1,
):
    step = pl.program_id(0)
    video, turn = step // STEPS, step % STEPS

    @pl.when(turn == 0)
    def _():
        kall[0:PR, :] = kv[...]
        remember(kall, step, near0, far0, near1, far1)
        keys_ext(kall[...], wk[...], wv[...], kext[...], H1, k_out, v_out)

    q = (mm(xn[:, D1:], wq[...]) + one_lane((TILE, W1))).astype(bf16)
    heads = [slice(LANE * h, LANE * (h + 1)) for h in range(H1)]
    scores = [mm_nt(q[:, at], k_out[:, at]) for at in heads]
    for h, at in enumerate(heads):
        o, qx = head_forward(q[:, at], scores[h], v_out[:, at])
        ozq[:, 2 * W1 + LANE * h : 2 * W1 + LANE * (h + 1)] = qx
        ozq[:, at] = o.astype(bf16)
        ozq[:, W1 + LANE * h : W1 + LANE * (h + 1)] = (o + q[:, at].astype(f32)).astype(bf16)
    ha = xn[:, :D1].astype(f32) + mm(ozq[:, W1 : 2 * W1], wp[...])
    hm[:, :D1] = ha
    unit, _ = norm_stats(ha)
    nb = (unit * gains[1:2, :]).astype(bf16)
    part = F1 // 3
    mid = ha
    ahead = mm(nb, wfc[:, :part])
    for j in range(3):
        at = slice(part * j, part * (j + 1))
        inner = ahead
        if j < 2:
            ahead = mm(nb, wfc[:, part * (j + 1) : part * (j + 2)])
        act, slope = gelu_both(inner)
        act = act.astype(bf16)
        ubgp[:, at] = act
        ubgp[:, F1 + part * j : F1 + part * (j + 1)] = slope.astype(bf16)
        mid = mid + mm(act, wout[at, :])
    hm[:, D1:] = mid
    unit, _ = norm_stats(mid)
    xs[pl.ds(pl.multiple_of(turn * TILE, TILE), TILE), :] = (unit * gains[2:3, :]).astype(bf16).astype(f32)

    @pl.when(turn == STEPS - 1)
    def _():
        pooled = pool_rows(xs)
        pc[...] = pooled
        m = mm(tmean_matrix(), pooled).astype(bf16)
        mem[...] = m

        @pl.when(video == 0)
        def _():
            mem0[...] = m


def block1(kv, got0, mem, kext, xn, w, wp, gains, wfc, wout):
    n = STEPS
    ins = [per_video(kv, n), whole(got0[0]), whole(got0[1]), whole(kext), video_rows(xn, n, TILE)]
    ins += [cols_fixed(w, W1, j) for j in range(3)]
    ins += [whole(wp), whole(gains), whole(wfc), whole(wout)]
    outs = [per_video(shape_of((2, KR, c), bf16), n) for c in (D1, W1, W1)]
    outs += [video_rows(shape_of((2, QT, c), t), n, TILE) for c, t in ((3 * W1, bf16), (2 * D1, f32), (2 * F1, bf16))]
    outs += [per_video(shape_of((2, r, D1), bf16), n) for r in (PR, MR)]
    flops = 4 * QT * (D1 * W1 * 2 + 2 * D1 * F1 + 4 * KR * W1)
    jobs = [Shift(mem, k, (0, 0), (n, 0), True, 1) for k in (1, 2)]
    jobs += [Shift(21, k, (n - 1, 1), (2 * n - 1, 1)) for k in (1, 2)]
    scratch = [VMEM((QT, D1), f32), VMEM((MR, D1), bf16)]
    return call(block1_kernel, (2 * n,), ins, outs, scratch, flops=flops, name="block1_forward", jobs=jobs, tag=2)


def cols_fixed(array, tile, at):
    return (array, pl.BlockSpec((array.shape[0], tile), lambda i: (0, at)))


PAIR = 2 * LANE


def block2_kernel(pc, near0, far0, kext, wq, wk, wv, wskip, wp, kall, k_out, v_out, qe, o_out, zc, hc, near1, far1):
    step = pl.program_id(0)

    @pl.when(step % (H2 // 2) == 0)
    def _():
        kall[0:PR, :] = pc[...]
        remember(kall, step, near0, far0, near1, far1)
        hc[...] = mm(pc[...], wskip[...])

    keys_ext(kall[...], wk[...], wv[...], kext[...], 2, k_out, v_out)
    q = (mm(pc[...], wq[...]) + one_lane((PR, PAIR))).astype(bf16)
    heads = [slice(LANE * h, LANE * (h + 1)) for h in range(2)]
    scores = [mm_nt(q[:, at], k_out[:, at]) for at in heads]
    for h, at in enumerate(heads):
        o, qx = head_forward(q[:, at], scores[h], v_out[:, at])
        qe[:, at] = qx
        o_out[:, at] = o.astype(bf16)
        zc[:, at] = (o + q[:, at].astype(f32)).astype(bf16)
    hc[...] += mm(zc[...], wp[...])


def block2(pc, got0, mem, kext, w, wskip, wp):
    n = H2 // 2
    ins = [per_video(pc, n), whole(got0[0]), whole(got0[1]), whole(kext)]
    ins += [turn_cols(w, n, PAIR, j * n) for j in range(3)]
    ins += [whole(wskip), turn_rows(wp, n, PAIR)]
    outs = [per_video(shape_of((2, KR, D1), bf16), n)]
    outs += [video_cols(shape_of((2, r, W2), bf16), n, PAIR) for r in (KR, KR, PR, PR, PR)]
    outs += [per_video(shape_of((2, PR, D2), f32), n)]
    flops = 4 * (PR * D1 * (W2 + D2) + 2 * KR * D1 * W2 + PR * W2 * D2 + 4 * PR * KR * W2)
    jobs = [Shift(mem, k, (0, 0), (n, 0), True, 1) for k in (1, 2)]
    return call(block2_kernel, (2 * n,), ins, outs, flops=flops, name="block2_attention", jobs=jobs, tag=3)


PART = 768


def pick_share(micro, even, odd):
    first_ = micro == 0
    return (jnp.where(first_, even, odd).astype(bf16), jnp.where(first_, odd, even).astype(bf16))


def wide(gains):
    return jnp.concatenate([gains[3:4, :], gains[4:5, :]], axis=1)


def mlp2_kernel(micro, hc, cot, gain, wfc, wout, out, gh, keep_fc, send_fc, keep_out, send_out, gg, hs, nd, ndt, gm, acc, dn):
    step = pl.program_id(0)

    @pl.when(step == 0)
    def _():
        blank = jnp.zeros((PR - PT, D2), f32)
        for b in range(2):
            at = slice(PR * b, PR * (b + 1))
            v = hc[b]
            hs[at, :] = v
            unit, _ = norm_stats(v)
            nd[at, :] = (unit * wide(gain)).astype(bf16)
            g = cot[0, b, 0].astype(f32)
            gm[at, :] = jnp.concatenate([g, blank], axis=0).astype(bf16)
        ndt[...] = nd[...].T

    act, slope = gelu_both(mm(nd[...], wfc[...]))
    act = act.astype(bf16)
    gi = (slope * mm_nt(gm[...], wout[...])).astype(bf16)
    m = micro[0]
    gw = mm_tn(act, gm[...])
    rows = keep_fc.shape[1]
    for i in range(keep_out.shape[0]):
        keep, send = pick_share(m, gw[8 * rows * i : 8 * rows * i + 4 * rows], gw[8 * rows * i + 4 * rows : 8 * rows * (i + 1)])
        for a in range(4):
            keep_out[i, :, D2 * a : D2 * (a + 1)] = keep[rows * a : rows * (a + 1)]
            send_out[i, :, D2 * a : D2 * (a + 1)] = send[rows * a : rows * (a + 1)]
    gw = mm(ndt[...], gi)
    for i in range(keep_fc.shape[0]):
        keep, send = pick_share(m, gw[2 * rows * i : 2 * rows * i + rows], gw[2 * rows * i + rows : 2 * rows * (i + 1)])
        keep_fc[i] = keep
        send_fc[i] = send
    o = mm(act, wout[...])
    d = mm_nt(gi, wfc[...])

    @pl.when(step == 0)
    def _():
        acc[...] = o
        dn[...] = d

    @pl.when(step > 0)
    def _():
        acc[...] += o
        dn[...] += d

    @pl.when(step == F2 // PART - 1)
    def _():
        v = hs[...]
        y = v + acc[...]
        unit, inv = norm_stats(v)
        dx, dg = norm_back(dn[...], unit, inv, wide(gain))
        gg[...] = dg
        g = (gm[...].astype(f32) + dx).astype(bf16)
        for b in range(2):
            out[0, b, 0] = y[PR * b : PR * b + PT].astype(bf16)
            gh[b] = g[PR * b : PR * (b + 1)]


def scalar(value):
    return (value.astype(jnp.int32).reshape(1), pl.BlockSpec(memory_space=pltpu.SMEM))


def mlp2(micro, clips, hc, cot, gain, wfc, wout):
    rows = D2 // (2 * clips)
    steps = F2 // PART
    ins = [scalar(micro), whole(hc), whole(cot), whole(gain), cols_tiled(wfc, PART), rows_tiled(wout, PART)]
    share = shape_of((clips, rows, F2), bf16)
    fc_spec = (share, pl.BlockSpec((clips, rows, PART), lambda i: (0, 0, i)))
    out_spec = (share, pl.BlockSpec((clips // steps, rows, F2), lambda i: (i, 0, 0)))
    outs = [
        whole(shape_of(cot.shape, bf16)),
        whole(shape_of((2, PR, D2), bf16)),
        fc_spec,
        fc_spec,
        out_spec,
        out_spec,
        whole(shape_of((1, D2), f32)),
    ]
    n = 2 * PR
    scratch = [
        VMEM((n, D2), f32),
        VMEM((n, D2), bf16),
        VMEM((D2, n), bf16),
        VMEM((n, D2), bf16),
        VMEM((n, D2), f32),
        VMEM((n, D2), f32),
    ]
    return call(mlp2_kernel, (steps,), ins, outs, scratch, flops=12 * n * D2 * F2, name="block2_mlp")


def heads_backward(heads, tiles):
    items = [(h, at) for h in range(len(heads)) for at in tiles]

    def products(item):
        q, g, k, v = heads[item[0]]
        return (mm_nt(k, q[item[1]]), mm_nt(v, g[item[1]]))

    out = [([], [], []) for _ in heads]
    kts = [k.T for _, _, k, _ in heads]
    ahead = products(items[0])
    for i, (h, at) in enumerate(items):
        score, dp = ahead
        if i + 1 < len(items):
            ahead = products(items[i + 1])
        q, g, _, _ = heads[h]
        p = jnp.exp2(score)
        ds = (p * dp).astype(bf16)
        dqs, dks, dvs = out[h]
        dvs.append(mm(p.astype(bf16), g[at]))
        dks.append(mm(ds, q[at]))
        dqs.append((mm(kts[h], ds) * (SCALE / RATE)).T)
    return [(dqs, sum(dks[1:], dks[0]) * SCALE, sum(dvs[1:], dvs[0])) for dqs, dks, dvs in out]


def grad_ext(gz, o):
    delta = jnp.sum(jnp.where(lanes(gz.shape) < HD, gz.astype(f32) * o.astype(f32), 0.0), axis=-1, keepdims=True)
    return put3(gz.astype(f32), -delta).astype(bf16)


def put_columns(ref, turn, value):
    ref[:, pl.ds(pl.multiple_of(turn * PAIR, PAIR), PAIR)] = value


def add_to(ref, value, again):
    @pl.when(again)
    def _():
        ref[...] += value

    @pl.when(jnp.logical_not(again))
    def _():
        ref[...] = value


def att2_back_kernel(
    micro, gh, wp, qe, o, k, v, zc, pc, kall, wskip, w,
    dnear, dfar, dpc, keep_a, send_a, keep_b, send_b,
    gq_w, gk_w, gv_w, gp_w, gs_w, dnear0, dfar0, gqs, dks, dvs,
):
    step = pl.program_id(0)
    turn = step % (H2 // 2)
    again = step >= H2 // 2
    gz = mm_nt(gh[...], wp[...]).astype(bf16)
    heads = [slice(LANE * h, LANE * (h + 1)) for h in range(2)]
    gq, dk, dv = [], [], []
    sets = [(qe[:, at], grad_ext(gz[:, at], o[:, at]), k[:, at], v[:, at]) for at in heads]
    for at, (dqs, dkh, dvh) in zip(heads, heads_backward(sets, [slice(0, PR)])):
        gq.append((gz[:, at].astype(f32) + dqs[0]).astype(bf16))
        dk.append(dkh.astype(bf16))
        dv.append(dvh.astype(bf16))
    put_columns(gqs, turn, jnp.concatenate(gq, axis=1))
    put_columns(dks, turn, jnp.concatenate(dk, axis=1))
    put_columns(dvs, turn, jnp.concatenate(dv, axis=1))

    @pl.when(turn == H2 // 2 - 1)
    def _():
        g = gh[...]
        kallt = kall[...].T
        pct = pc[...].T
        add_to(gq_w, mm(pct, gqs[...]), again)
        add_to(gk_w, mm(kallt, dks[...]), again)
        add_to(gv_w, mm(kallt, dvs[...]), again)
        add_to(gp_w, mm_tn(zc[...], g), again)
        add_to(gs_w, mm(pct, g), again)
        dkv = mm_nt(dks[...], w[:, W2 : 2 * W2]) + mm_nt(dvs[...], w[:, 2 * W2 :])
        dpc[...] = mm_nt(g, wskip[...]) + mm_nt(gqs[...], w[:, :W2]) + dkv[0:PR]
        near = dkv[PR : PR + MR].astype(bf16)
        far = dkv[PR + MR : KR].astype(bf16)

        @pl.when(jnp.logical_not(again))
        def _():
            dnear0[...] = near
            dfar0[...] = far

        @pl.when(again)
        def _():
            dnear[...] = near
            dfar[...] = far
            pack2(micro, gq_w, gk_w, gv_w, gp_w, gs_w, keep_a, send_a, keep_b, send_b)


def att2_back(gh, wp, qe, o, k, v, zc, pc, kall, wskip, w, micro, clips, jobs):
    n = H2 // 2
    ins = [scalar(micro), per_video(gh, n), turn_rows(wp, n, PAIR)]
    ins += [video_cols(a, n, PAIR) for a in (qe, o, k, v)]
    ins += [per_video(a, n) for a in (zc, pc, kall)] + [whole(wskip), whole(w)]
    outs = [whole(shape_of((MR, D1), bf16))] * 2 + [per_video(shape_of((2, PR, D1), f32), n)]
    outs += [whole(shape_of((clips,) + folded(D1 // (2 * clips), 3 * D2), bf16))] * 4
    scratch = [VMEM((D1, W2), f32)] * 3 + [VMEM((W2, D2), f32), VMEM((D1, D2), f32)]
    scratch += [VMEM((MR, D1), bf16)] * 2
    scratch += [VMEM((PR, W2), bf16), VMEM((KR, W2), bf16), VMEM((KR, W2), bf16)]
    flops = 4 * (10 * PR * KR * W2 + 4 * PR * D1 * W2 + 4 * KR * D1 * W2 + 4 * PR * W2 * D2)
    jobs = [Shift(24, -1, (n - 1, 1), (2 * n - 1, 1)), Shift(25, -2, (n - 1, 1), (2 * n - 1, 1))] + jobs
    return call(att2_back_kernel, (2 * n,), ins, outs, scratch, flops=flops, name="block2_attention_back", jobs=jobs, tag=4)


def mlp1_back_kernel(
    micro, dpc, rn0, rf0, gains, hm, ubgp, oz, wout, wfc, wp,
    gha, gze, gg_c, gg_m, gw_p, keep_a, send_a, keep_b, send_b,
    gw_out, gw_fc, ds, flip, rn1, rf1,
):
    step = pl.program_id(0)
    turn = step % PIECES

    @pl.when(step == 0)
    def _():
        for ref in (gg_c, gg_m, gw_out, gw_fc, gw_p):
            ref[...] = jnp.zeros_like(ref)

    def spread(rn, rf):
        got = add_up(rn[...], rf[...]).astype(bf16)
        d = 0.25 * (dpc[...] + mm_tn(tmean_matrix(), got))
        for s in range(4):
            ds[PT * s : PT * (s + 1), :] = d[0:PT]

    pl.when(step == 0)(lambda: spread(rn0, rf0))
    pl.when(step == PIECES)(lambda: spread(rn1, rf1))

    unit, inv = norm_stats(hm[:, D1:])
    dnc = ds[pl.ds(pl.multiple_of(turn * PIECE, PIECE), PIECE), :]
    gmid, dg = norm_back(dnc, unit, inv, gains[2:3, :])
    gg_c[...] += dg
    gm = gmid.astype(bf16)
    gmt = gm.T
    unit_b, inv_b = norm_stats(hm[:, :D1])
    nbt = (unit_b * gains[1:2, :]).astype(bf16).T
    part = F1 // 3
    dn = jnp.zeros((PIECE, D1), f32)
    ahead = mm_nt(gm, wout[:part, :])
    for j in range(3):
        at = slice(part * j, part * (j + 1))
        inner = ahead
        if j < 2:
            ahead = mm_nt(gm, wout[part * (j + 1) : part * (j + 2), :])
        slope = ubgp[:, F1 + part * j : F1 + part * (j + 1)].astype(f32)
        gi = (slope * inner).astype(bf16)
        gw_out[:, at] += mm(gmt, ubgp[:, at])
        gw_fc[:, at] += mm(nbt, gi)
        dn = dn + mm_nt(gi, wfc[:, at])
    dx, dg = norm_back(dn, unit_b, inv_b, gains[1:2, :])
    gg_m[...] += dg
    g = gmid + dx
    gha[...] = g
    gh = g.astype(bf16)
    gw_p[...] += mm_tn(oz[:, W1:], gh)
    gz = mm_nt(gh, wp[...]).astype(bf16)
    for h in range(H1):
        at = slice(LANE * h, LANE * (h + 1))
        gze[:, at] = grad_ext(gz[:, at], oz[:, at])

    @pl.when(step == 2 * PIECES - 1)
    def _():
        pack_mlp1(micro, gw_fc, gw_out, keep_a, send_a, keep_b, send_b, flip)


def mlp1_back(dpc, got0, near1, far1, gains, hm, ubgp, ozq, wout, wfc, wp, micro, clips, jobs):
    n = PIECES
    ins = [scalar(micro), per_video(dpc, n), whole(got0[0]), whole(got0[1]), whole(gains)]
    ins += [video_rows(hm, n, PIECE), video_rows(ubgp, n, PIECE), video_rows(ozq, n, PIECE, 2 * W1)]
    ins += [whole(wout), whole(wfc), whole(wp)]
    outs = [video_rows(shape_of((2, QT, D1), f32), n, PIECE), video_rows(shape_of((2, QT, W1), bf16), n, PIECE)]
    outs += [whole(shape_of((1, D1), f32))] * 2 + [whole(shape_of((W1, D1), f32))]
    outs += [whole(shape_of((clips,) + folded(D1 // (2 * clips), F1), bf16))] * 4
    scratch = [VMEM((D1, F1), f32)] * 2 + [VMEM((QT, D1), f32), VMEM((F1, D1), f32)]
    flops = 4 * QT * (4 * D1 * F1 + 2 * D1 * W1)
    jobs = [Shift(near1, -1, (0, 0), (n, 0), True), Shift(far1, -2, (0, 0), (n, 0), True)] + jobs
    return call(mlp1_back_kernel, (2 * n,), ins, outs, scratch, flops=flops, name="block1_mlp_back", jobs=jobs, tag=5)


QUERY_TILES = [slice(0, 512), slice(512, 1024), slice(1024, QT)]


def att1_back_kernel(
    micro, qe, gze, k, v, xn, kall, w, gp,
    dnear, dfar, down, dna, keep_a, send_a, keep_b, send_b,
    gq_w, gk_w, gv_w, qkv, dnear0, dfar0, gqs, dks, dvs,
):
    step = pl.program_id(0)
    turn = step % (H1 // 2)
    again = step >= H1 // 2
    gq, dk, dv = [[] for _ in QUERY_TILES], [], []
    sets = [tuple(r[:, LANE * h : LANE * (h + 1)] for r in (qe, gze, k, v)) for h in range(2)]
    for (_, g, _, _), (dqs, dkh, dvh) in zip(sets, heads_backward(sets, QUERY_TILES)):
        for i, rows in enumerate(QUERY_TILES):
            gq[i].append((g[rows].astype(f32) + dqs[i]).astype(bf16))
        dk.append(dkh.astype(bf16))
        dv.append(dvh.astype(bf16))
    gq = jnp.concatenate([jnp.concatenate(t, axis=1) for t in gq], axis=0)
    lane = lanes((1, PAIR)) % LANE
    put_columns(gqs, turn, jnp.where(lane < HD, gq, jnp.zeros_like(gq)))
    put_columns(dks, turn, jnp.concatenate(dk, axis=1))
    put_columns(dvs, turn, jnp.concatenate(dv, axis=1))

    @pl.when(turn == H1 // 2 - 1)
    def _():
        kallt = kall[...].T
        add_to(gq_w, mm(xn[...].T, gqs[...]), again)
        add_to(gk_w, mm(kallt, dks[...]), again)
        add_to(gv_w, mm(kallt, dvs[...]), again)
        dkv = mm_nt(dks[...], w[:, W1 : 2 * W1]) + mm_nt(dvs[...], w[:, 2 * W1 :])
        dna[...] = mm_nt(gqs[...], w[:, :W1])
        down[...] = dkv[0:PR]
        near = dkv[PR : PR + MR].astype(bf16)
        far = dkv[PR + MR : KR].astype(bf16)

        @pl.when(jnp.logical_not(again))
        def _():
            dnear0[...] = near
            dfar0[...] = far

        @pl.when(again)
        def _():
            dnear[...] = near
            dfar[...] = far
            pack_att1(micro, gq_w, gk_w, gv_w, gp, keep_a, send_a, keep_b, send_b, qkv)


def att1_back(ozq, gze, k, v, xn, kall, w, gp, micro, clips, jobs):
    n = H1 // 2
    ins = [scalar(micro), video_cols(ozq, n, PAIR, 2 * n)] + [video_cols(a, n, PAIR) for a in (gze, k, v)]
    ins += [(xn, pl.BlockSpec((None, QT, D1), lambda i: (i // n, 0, 1))), per_video(kall, n)]
    ins += [whole(w), whole(gp)]
    outs = [whole(shape_of((MR, D1), bf16))] * 2
    outs += [per_video(shape_of((2, PR, D1), f32), n), per_video(shape_of((2, QT, D1), f32), n)]
    outs += [whole(shape_of((clips,) + folded(D1 // (2 * clips), 2 * D1), bf16))] * 4
    scratch = [VMEM((D1, W1), f32)] * 3
    scratch += [VMEM((D1, 4 * D1), f32)] + [VMEM((MR, D1), bf16)] * 2
    scratch += [VMEM((QT, W1), bf16), VMEM((KR, W1), bf16), VMEM((KR, W1), bf16)]
    flops = 4 * (10 * QT * KR * W1 + 2 * QT * D1 * W1 + 4 * KR * D1 * W1)
    jobs = [Shift(21, -1, (n - 1, 1), (2 * n - 1, 1)), Shift(22, -2, (n - 1, 1), (2 * n - 1, 1))] + jobs
    return call(att1_back_kernel, (2 * n,), ins, outs, scratch, flops=flops, name="block1_attention_back", jobs=jobs, tag=6)


def strip(grad):
    return jnp.concatenate([grad[:, LANE * h : LANE * h + HD] for h in range(grad.shape[1] // LANE)], axis=1)


def fold(v):
    rows, cols = v.shape
    if rows != 24:
        return v
    rest = jnp.concatenate([v[16:, : cols // 2], v[16:, cols // 2 :]], axis=0)
    return jnp.concatenate([v[:16], rest], axis=1)


def unfold(v, rows):
    if rows != 24:
        return v
    cols = v.shape[1] * 2 // 3
    rest = jnp.concatenate([v[:8, cols:], v[8:, cols:]], axis=1)
    return jnp.concatenate([v[:, :cols], rest], axis=0)


def folded(rows, cols):
    return (16, cols * 3 // 2) if rows == 24 else (rows, cols)


def store_shares(micro, clips, pieces):
    for i in range(clips):
        for keep, send, piece in pieces:
            k, t = pick_share(micro, fold(piece(2 * i)), fold(piece(2 * i + 1)))
            keep[i] = k
            send[i] = t


def pack2(micro, gq, gk, gv, gp, gs, keep_a, send_a, keep_b, send_b):
    clips, rows = keep_a.shape[0], D1 // (2 * keep_a.shape[0])

    def proj(share, a):
        lo = rows * (2 * share + a)
        h = lo // HD
        start = lo + (LANE - HD) * h
        if (lo + rows - 1) // HD == h:
            return gp[start : start + rows, :]
        cut = HD * (h + 1) - lo
        return jnp.concatenate([gp[start : start + cut, :], gp[LANE * (h + 1) : LANE * (h + 1) + rows - cut, :]], axis=0)

    def piece_a(n):
        return jnp.concatenate([strip(t[rows * n : rows * (n + 1), :]) for t in (gq, gk, gv)], axis=1)

    def piece_b(n):
        return jnp.concatenate([proj(n, 0), proj(n, 1), gs[rows * n : rows * (n + 1), :]], axis=1)

    store_shares(micro[0], clips, ((keep_a, send_a, piece_a), (keep_b, send_b, piece_b)))


def pack_mlp1(micro, gfc, gout, keep_a, send_a, keep_b, send_b, flip):
    flip[...] = gout[...].T
    clips, rows = keep_a.shape[0], D1 // (2 * keep_a.shape[0])

    def piece_a(n):
        return gfc[rows * n : rows * (n + 1), :]

    def piece_b(n):
        return jnp.concatenate([flip[rows * (4 * n + a) : rows * (4 * n + a + 1), :] for a in range(4)], axis=1)

    store_shares(micro[0], clips, ((keep_a, send_a, piece_a), (keep_b, send_b, piece_b)))


def pack_att1(micro, gq, gk, gv, gp, keep_a, send_a, keep_b, send_b, qkv):
    for j, g in enumerate((gq, gk, gv)):
        qkv[:, D1 * j : D1 * (j + 1)] = strip(g[...])
    for h in range(H1):
        qkv[HD * h : HD * (h + 1), 3 * D1 :] = gp[LANE * h : LANE * h + HD, :]
    clips, rows = keep_a.shape[0], D1 // (2 * keep_a.shape[0])
    half = 2 * D1

    def piece_a(n):
        return qkv[rows * n : rows * (n + 1), :half]

    def piece_b(n):
        return qkv[rows * n : rows * (n + 1), half:]

    store_shares(micro[0], clips, ((keep_a, send_a, piece_a), (keep_b, send_b, piece_b)))


def flatten_into(out, v, row=0, column=0, columns=None):
    rows, cols = v.shape
    wide_ = (columns or cols) // LANE
    for j in range(cols // LANE):
        out[pl.ds(row * wide_ + column // LANE + j, rows, stride=wide_), :] = v[:, LANE * j : LANE * (j + 1)]


def lay_out_kernel(rows, left, right, fc1, out1, qkv2, rest2, fc2, out2, gains, gx, *outs):
    for i in range(3):
        outs[9 + i][...] = gains[i : i + 1, :].reshape(D1)
    outs[12][0:D1] = gains[3:4, :].reshape(D1)
    outs[12][D1:] = gains[4:5, :].reshape(D1)
    outs[13][...] = gx[...]
    left, right, fc1, out1, qkv2, rest2 = (unfold(v[...], rows) for v in (left, right, fc1, out1, qkv2, rest2))
    flatten_into(outs[0], left, 0, 0, 3 * D1)
    flatten_into(outs[0], right[:, :D1], 0, 2 * D1, 3 * D1)
    flatten_into(outs[1], right[:, D1:])
    flatten_into(outs[2], fc1)
    flatten_into(outs[4], qkv2)
    for a in range(2):
        flatten_into(outs[5], rest2[:, D2 * a : D2 * (a + 1)], rows * a)
    flatten_into(outs[6], rest2[:, 2 * D2 :])
    flatten_into(outs[7], fc2[...])
    for a in range(4):
        flatten_into(outs[3], out1[:, D1 * a : D1 * (a + 1)], rows * a)
        flatten_into(outs[8], out2[:, D2 * a : D2 * (a + 1)], 2 * rows * a)


def lay_out(clips, sums, gains, gx):
    sizes = (3 * D1 * D1, D1 * D1, D1 * F1, D1 * F1, 3 * D1 * D2, D2 * D2, D1 * D2, D2 * F2, D2 * F2)
    outs = [whole(shape_of((n // (2 * clips * LANE), LANE), f32)) for n in sizes]
    outs += [whole(shape_of((n,), f32)) for n in (D1, D1, D1, D2)] + [whole(shape_of(gx.shape, bf16))]
    return call(partial(lay_out_kernel, D1 // (2 * clips)), (1,), [whole(v) for v in sums + [gains, gx]], outs, name="lay_out")


def bit_order(bits, stream):
    order = list(range(bits))
    if stream % 2 == 1 and bits > 1:
        order[0], order[1] = 1, 0
    return order


def finish_kernel(clips, starts, *refs):
    count = len(starts)
    keeps, gots = refs[:count], refs[count : 2 * count]
    pos = 2 * count
    gg_m, gg_c, gg_d, gain, dnear, dfar, dna_h, down, xn_h, gha_h, rn0, rf0 = refs[pos : pos + 12]
    pos += 12
    gx, gains = refs[pos : pos + 2]
    done = refs[pos + 2 : pos + 2 + count]
    pos += 2 + count
    dna, xn, gha, ds, gs, rn1, rf1, g_all, g_four = refs[pos : pos + 9]
    pos += 9
    bits = clips.bit_length() - 1
    land, stage, ends = {}, {}, {}
    for i in range(count):
        if starts[i] < 0:
            land[i] = refs[pos]
            pos += 1
        for k in range(max(starts[i], 0), bits):
            stage[i, k] = refs[pos : pos + 3]
            pos += 3
        ends[i] = refs[pos : pos + 2]
        pos += 2
    sem_s, sem_r, gsem_s, gsem_r, fsem_s, fsem_r, msem_s, msem_r, lsem = refs[pos:]

    def loads(b):
        pairs = ((dna_h.at[b], dna.at[b]), (xn_h.at[b, :, 0:D1], xn.at[b]), (gha_h.at[b], gha.at[b]))
        return [pltpu.make_async_copy(src, dst, lsem.at[3 * b + i]) for i, (src, dst) in enumerate(pairs)]

    for b in range(2):
        for load in loads(b):
            load.start()

    g, c, m = (lax.axis_index(a) for a in ("group", "clip", "micro"))
    barrier = pltpu.get_barrier_semaphore()
    others = [{"clip": lax.rem(c + d, clips)} for d in range(1, clips)]
    others += [{"micro": 1 - m}, {"group": 1 - g}, {"group": 1 - g, "micro": 1 - m}]
    for other in others:
        pl.semaphore_signal(barrier, inc=1, device_id=other, device_id_type=MESH)
    pl.semaphore_wait(barrier, len(others))

    shifts = [(dnear, rn1, -1), (dfar, rf1, -2)]

    def memory_copy(i):
        src, dst, steps = shifts[i]
        return pltpu.make_async_remote_copy(
            src_ref=src, dst_ref=dst, send_sem=msem_s.at[i], recv_sem=msem_r.at[i],
            device_id={"clip": c + steps}, device_id_type=MESH,
        )

    for i in range(2):
        pl.when(exists(shifts[i][2]))(lambda i=i: memory_copy(i).start())

    copies = {}

    def send(i, number, src, dst, other):
        n = i * (bits + 2) + number + 1
        copies[i, number] = pltpu.make_async_remote_copy(
            src_ref=src, dst_ref=dst, send_sem=sem_s.at[n], recv_sem=sem_r.at[n],
            device_id=other, device_id_type=MESH,
        )
        copies[i, number].start()

    def advance(i, number):
        if number < 0:
            send(i, number, gots[i], land[i], {"micro": 1 - m})
            return
        if (i, number - 1) in copies:
            copies[i, number - 1].wait()
        if number == starts[i]:
            keep, got = keeps[i], gots[i]
        elif number == 0:
            keep, got = keeps[i], land[i]
        else:
            keep, got = stage[i, number - 1][0], stage[i, number - 1][2]
        if number == bits:
            ends[i][0][...] = add_up(keep[0], got[0]).astype(bf16)
            send(i, number, ends[i][0], ends[i][1], {"group": 1 - g})
        else:
            order = bit_order(bits, i)
            bit = order[number]
            low = sum(1 for b in order[number + 1 :] if b < bit)
            kept, away, there = stage[i, number]
            split_shares(keep, got, kept, away, bit, low, 2 ** (bits - number - 1))
            send(i, number, away, there, {"clip": flipped(bit)})

    at_stage = list(starts)

    def advance_all():
        for i in range(count):
            if at_stage[i] <= bits:
                advance(i, at_stage[i])
                at_stage[i] += 1

    def norm_part(b, rn, rf):
        for load in loads(b):
            load.wait()
        got = add_up(rn, rf).astype(bf16)
        d = 0.25 * (down[b] + mm_tn(tmean_matrix(), got))
        for s in range(4):
            ds[PT * s : PT * (s + 1), :] = d[0:PT]
        total = jnp.zeros((1, D1), f32)
        for i in range(PIECES):
            at = slice(PIECE * i, PIECE * (i + 1))
            unit, inv = norm_stats(xn[b, at, :].astype(f32))
            dx, dg = norm_back(dna[b, at, :] + ds[at, :], unit, inv, gain[0:1, :])
            total = total + dg
            gs[at, :] = gha[b, at, :] + dx
        return total

    def order_part(b):
        for i in range(PIECES):
            lo = min(CELL * i // 8 * 8, PT - 112)
            window = jnp.concatenate([gs[PT * s + lo : PT * s + lo + 112, :] for s in range(4)], axis=0).astype(bf16)
            shape = (PIECE, 4 * 112)
            t = rows_of(shape) + PIECE * i
            f = t // (HT * WD)
            rest = t - f * (HT * WD)
            r = rest // WD
            col = rest - r * WD
            r2 = r // 2
            c2 = col // 2
            s = 2 * (r - 2 * r2) + (col - 2 * c2)
            p = f * CELL + r2 * 7 + c2
            pick = jnp.where(s * 112 + p - lo == lanes(shape), 1.0, 0.0).astype(bf16)
            gx[b, PIECE * i : PIECE * (i + 1), :] = mm(pick, window).astype(bf16)

    advance_all()
    gg = norm_part(0, rn0[...], rf0[...])
    advance_all()
    order_part(0)
    advance_all()
    for i in range(2):
        _, dst, steps = shifts[i]
        pl.when(exists(steps))(lambda i=i: memory_copy(i).wait_send())

        @pl.when(exists(-steps))
        def _():
            memory_copy(i).wait_recv()

        @pl.when(jnp.logical_not(exists(-steps)))
        def _():
            dst[...] = jnp.zeros_like(dst)

    gg = gg + norm_part(1, rn1[...], rf1[...])
    advance_all()
    g_all[c] = jnp.concatenate(
        [gg, gg_m[...], gg_c[...], gg_d[:, :D1], gg_d[:, D1:], jnp.zeros((3, D1), f32)], axis=0
    )
    gcopies = []
    for d in range(1, clips):
        gcopies.append(
            pltpu.make_async_remote_copy(
                src_ref=g_all.at[c], dst_ref=g_all.at[c], send_sem=gsem_s.at[d - 1], recv_sem=gsem_r.at[d - 1],
                device_id={"clip": lax.rem(c + d, clips)}, device_id_type=MESH,
            )
        )
        gcopies[-1].start()
    order_part(1)
    advance_all()
    for copy in gcopies:
        copy.wait()
    total = g_all[0]
    for i in range(1, clips):
        total = total + g_all[i]
    place = 2 * g + m
    g_four[place] = total
    fcopies = []
    for i, other in enumerate(others[-3:]):
        fcopies.append(
            pltpu.make_async_remote_copy(
                src_ref=g_four.at[place], dst_ref=g_four.at[place], send_sem=fsem_s.at[i], recv_sem=fsem_r.at[i],
                device_id=other, device_id_type=MESH,
            )
        )
        fcopies[-1].start()
    for _ in range(bits + 2):
        advance_all()
    for copy in fcopies:
        copy.wait()
    gains[...] = (g_four[0] + g_four[1]) + (g_four[2] + g_four[3])
    for i in range(count):
        copies[i, bits].wait()
        done[i][...] = add_up(*(ref[...] for ref in ends[i]))


def finish(clips, streams, starts, gg_m, gg_c, gg_d, gain, dnear, dfar, dna, down, xn, gha, got0, tag):
    bits = clips.bit_length() - 1
    count = len(streams)
    ins = [whole(k) for k, _ in streams] + [(t, HBM) if n < 0 else whole(t) for (_, t), n in zip(streams, starts)]
    ins += [whole(a) for a in (gg_m, gg_c, gg_d, gain)] + [(dnear, HBM), (dfar, HBM)]
    ins += [(dna, HBM), whole(down), (xn, HBM), (gha, HBM)]
    ins += [whole(a) for a in got0]
    parts = [k.shape[1:] for k, _ in streams]
    outs = [whole(shape_of((2, QT, D1), bf16)), whole(shape_of((8, D1), f32))]
    outs += [whole(shape_of(p, f32)) for p in parts]
    scratch = [VMEM((2, QT, D1), f32), VMEM((2, QT, D1), bf16), VMEM((2, QT, D1), f32)]
    scratch += [VMEM((QT, D1), f32)] * 2 + [VMEM((MR, D1), bf16)] * 2
    scratch += [VMEM((clips, 8, D1), f32), VMEM((4, 8, D1), f32)]
    for p, n in zip(parts, starts):
        if n < 0:
            scratch.append(VMEM((clips,) + p, bf16))
        for k in range(max(n, 0), bits):
            scratch += [VMEM((2 ** (bits - 1 - k),) + p, bf16)] * 3
        scratch += [VMEM(p, bf16)] * 2
    dma = pltpu.SemaphoreType.DMA
    for n in (count * (bits + 2), clips - 1, 3, 2):
        scratch += [dma((n,))] * 2
    scratch.append(dma((6,)))
    return pl.pallas_call(
        partial(finish_kernel, clips, starts),
        grid=(1,),
        in_specs=[t for _, t in ins],
        out_specs=[t for _, t in outs],
        out_shape=[t for t, _ in outs],
        scratch_shapes=scratch,
        compiler_params=pltpu.CompilerParams(
            vmem_limit_bytes=VMEM_LIMIT, collective_id=tag, has_side_effects=True
        ),
        name="finish",
    )(*[a for a, _ in ins])


def body(inputs, offsets, cotangent, gain_attn1, w_qkv1, w_proj1, gain_mlp1, w_fc1, w_out1,
         gain_attn2, w_qkv2, w_proj2, w_skip, gain_mlp2, w_fc2, w_out2):
    clip = lax.axis_index("clip")
    row = jnp.arange(KR, dtype=jnp.int32)[:, None]
    place = jnp.where(row < PR + MR, row - PR, row - PR - MR)
    later = (place // CELL >= offsets[0]) & (place < MT)
    hops = jnp.where(row < PR + MR, 1, 2)
    valid = jnp.where(row < PR, row < PT, later & (clip >= hops))
    lane = jnp.arange(LANE, dtype=jnp.int32)[None, :]
    kext = jnp.where(lane == HD + 3, jnp.where(valid, 0.0, -1e30), jnp.where((lane >= HD) & (lane < HD + 3), 1.0, 0.0))
    kext = kext.astype(f32)

    micro, clips = lax.axis_index("micro"), lax.axis_size("clip")
    bits = clips.bit_length() - 1

    def flat(results):
        return [r[0] for r in results]

    gains_in = (gain_attn1, gain_mlp1, gain_attn2, gain_mlp2)
    (xn, kva, mem, gains_in, w1p, p1p, w2p, p2p), got = front(inputs, gains_in, w_qkv1, w_proj1, w_qkv2, w_proj2)
    (ka, Ka, Va, ozq, hm, ubgp, pc, mem), got = block1(kva, flat(got), mem, kext, xn, w1p, p1p, gains_in, w_fc1, w_out1)
    (kc, Kc, Vc, qec, oc, zc, hc), _ = block2(pc, flat(got[2:]), mem, kext, w2p, w_skip, p2p)
    output, gh, keep_fc, send_fc, keep_out, send_out, gg_mlp2 = mlp2(micro, clips, hc, cotangent, gains_in, w_fc2, w_out2)

    orders = [bit_order(bits, i) for i in range(2)]

    def chains(parts, plan, last):
        return [Chain(p, o, plan, last) for p, o in zip(parts, orders)]

    n = H2 // 2
    jobs = chains([(keep_fc, send_fc), (keep_out, send_out)], [(-1, 0), (0, 3)], 2 * n - 1)
    (near1, far1, dpc, *packed), got = att2_back(gh, p2p, qec, oc, Kc, Vc, zc, pc, kc, w_skip, w2p, micro, clips, jobs)
    got0, big = flat(got[:2]), got[2:]
    att2 = [(packed[0], packed[1]), (packed[2], packed[3])]
    n = PIECES
    jobs = chains(big, [(1, 1), (2, 7)], 2 * n - 1) + chains(att2, [(-1, 0), (0, 4)], 2 * n - 1)
    (gha, gze, gg_c, gg_m, gp, *packed), got = mlp1_back(
        dpc, got0, near1, far1, gains_in, hm, ubgp, ozq, w_out1, w_fc1, p1p, micro, clips, jobs
    )
    big, att2 = got[2:4], got[4:]
    mlp1 = [(packed[0], packed[1]), (packed[2], packed[3])]
    n = H1 // 2
    rest = [(k, 0) for k in range(3, bits)]
    jobs = chains(big, rest + [(GROUP, 0)], 2 * n - 1)
    rest = [(k, 1) for k in range(2, bits)]
    jobs += chains(att2, [(1, 0)] + rest + [(GROUP, 2)], 2 * n - 1)
    rest = [(k, 3) for k in range(2, bits)]
    jobs += chains(mlp1, [(-1, 0), (0, 1), (1, 2)] + rest, 2 * n - 1)
    (near1, far1, down, dna, *packed), got = att1_back(ozq, gze, Ka, Va, xn, ka, w1p, gp, micro, clips, jobs)
    got0, big, att2, mlp1 = flat(got[:2]), flat(got[2:4]), flat(got[4:6]), got[6:]
    att1 = [(packed[0], packed[1]), (packed[2], packed[3])]
    streams = [tuple(p) for p in att1 + mlp1]
    starts = [-1, -1, bits, bits]
    gx, gains, *sums = finish(
        clips, streams, starts, gg_m, gg_c, gg_mlp2, gains_in, near1, far1, dna, down, xn, gha, got0, 7
    )
    *shares, ga, gb, gc, gd, gx = lay_out(clips, sums + att2 + big, gains, gx)
    return (output, gx.reshape(inputs.shape), ga, gb, gc, gd) + tuple(v.reshape(-1) for v in shares)


def solution(mesh):
    tokens = P("group", "micro", "clip", None, None)
    share = P(("clip", "micro"))
    return jax.shard_map(
        body,
        mesh=mesh,
        in_specs=(tokens, P("group"), tokens) + (P(),) * 13,
        out_specs=(tokens, tokens) + (P(),) * 4 + (share,) * 9,
        check_vma=False,
    )
```
